512 devices in a mesh: seq: 128 (over z, y, core), mp: 4 (over x).
Axes of the slice: x: 4, y: 8, z: 8, core: 2. Of those that a mesh axis runs over, the one named last changes fastest.
Arguments:
- byte_hidden: bfloat16 [131072, 1024], P('seq', 'mp'), may hold values from -24 to 24
- patch_start: int32 [131072], P('seq'), may hold values from 0 to 1, as said below
- pool_query: bfloat16 [1024], P('mp'), may hold values from -4 to 4
- in_weight: bfloat16 [1024, 4096], P('seq', 'mp'), may hold values from -0.1875 to 0.1875
- latent_grad: bfloat16 [65536, 4096], P('seq', 'mp'), may hold values from -6 to 6
Outputs:
- latent: bfloat16 [65536, 4096], P('seq', 'mp')
- grad_weight: float32 [1024, 4096], P('seq', 'mp')
- grad_bytes: bfloat16 [131072, 1024], P('seq', 'mp')
The draws below stay inside these ranges and needn't reach their ends.
Inputs may be any that keep to these rules, and one draw needn't show every extreme that they name: `patch_start`: byte 0 begins a patch, and so does every byte whose position is 16 // 2 modulo 16; of the bytes 2k and 2k+1 at most one begins a patch. So no patch is longer than 16 bytes, and some patch is exactly 16 long. Each aligned block of 1024 bytes holds at most 512 patch starts, and one block holds exactly 512.
All inputs are finite; a program needn't handle non-finite values.
Results may differ from the reference program's by a relative error of at most 0.0049.
Values may be sent and summed in bfloat16 or wider, within the bound.
A program may use at most 64 MiB of HBM per device.

```python
import math
import jax
import jax.numpy as jnp
from jax import lax

DL = 1024
DM = 4096
HEAD_DIM = 64
MAXLEN = 16
BYTE_DEV = 1024
PCAP = 512
BYTES = 131072
SLOTS = 65536
N_SEQ = 128
N_MP = 4


def draw_patch_start(key, part):
    key = jax.random.fold_in(key, 11)
    blocks = BYTES // BYTE_DEV
    pairs = BYTE_DEV // 2
    half_seg = MAXLEN // 2
    keys = jax.random.split(key, 6)
    rate = jax.random.randint(keys[0], (blocks, 1), 150, 600)
    dense = jax.random.randint(keys[1], (), 0, blocks)
    sparse = (dense + 1 + jax.random.randint(keys[2], (), 0, blocks - 1)) % blocks
    picked = jax.random.randint(keys[3], (blocks, pairs), 0, 1000) < rate
    odd_bit = jax.random.randint(keys[4], (blocks, pairs), 0, 2)
    window = jax.random.randint(keys[5], (), 0, BYTE_DEV // MAXLEN - 1)
    pair_index = jnp.arange(pairs)[None, :]
    block_index = jnp.arange(blocks)[:, None]
    forced = pair_index % half_seg == MAXLEN // 4
    first = (block_index == 0) & (pair_index == 0)
    window_pair = window * half_seg + MAXLEN // 4
    empty = (block_index == sparse) & (pair_index > window_pair) & (pair_index < window_pair + half_seg)
    present = (picked | (block_index == dense)) & jnp.logical_not(empty) | forced | first
    which = jnp.where(forced | first, 0, odd_bit)
    lower = present & (which == 0)
    upper = present & (which == 1)
    return jnp.stack([lower, upper], axis=-1).reshape(BYTES).astype(jnp.int32)


def raised(result, own_key, source, target, parts, factor):
    owner, partner = [(jnp.arange(result.shape[axis_at]) // (result.shape[axis_at] // parts)).reshape([-1 if axis == axis_at else 1 for axis in range(result.ndim)]) for axis_at in (source, target)]
    chosen = jax.random.permutation(own_key, parts)[partner]
    strong = (owner == chosen) | (owner == (partner + parts // 2) % parts)
    return jnp.where(strong, factor * result, result)


def levels(own_key, dims, cuts, smallest, high):
    def one(dim, shards_of):
        steps = jax.random.uniform(jax.random.fold_in(jax.random.fold_in(own_key, 6), dim), (shards_of,), jnp.float32, smallest / len(cuts), high / len(cuts))
        return jnp.repeat(jnp.exp(steps), dims[dim] // shards_of).reshape((-1,) + (1,) * (len(dims) - dim - 1))

    factor_of = one(*cuts[0])
    for cut in cuts[1:]:
        factor_of = factor_of * one(*cut)
    return factor_of


def noise(key, extent, scale, limit, cuts=(), kind=jnp.bfloat16):
    array = jax.random.normal(key, extent, jnp.float32) * scale
    if len(cuts) > 0:
        array = levels(key, extent, cuts, -0.22, 0.18) * array
    return jnp.clip(array, min=-limit, max=limit).astype(kind)


def heavy_noise(stream_key, extent, spread, limit, cuts, heavy, kind=jnp.bfloat16):
    array = spread * jax.random.normal(stream_key, extent, jnp.float32)
    if cuts:
        array = array * levels(stream_key, extent, cuts, -0.22, 0.18)
    return jnp.clip(raised(array, jax.random.fold_in(stream_key, 3), *heavy), -limit, limit).astype(kind)


def setup_inputs(seed: int = 0) -> dict:
    key_list = jax.random.split(jax.random.key(seed), 6)
    return {
        "byte_hidden": heavy_noise(key_list[0], (BYTES, DL), 1.0, 24.0, ((0, 128), (1, 4)), (0, 1, 128, 5.5)),
        "patch_start": draw_patch_start(jax.random.fold_in(key_list[5], 71), 0),
        "pool_query": noise(key_list[2], (DL,), 1.0, 4.0, ((0, 4),)),
        "in_weight": noise(key_list[3], (DL, DM), DL ** -0.5, 0.1875, ((0, 128), (1, 4))),
        "latent_grad": noise(key_list[4], (SLOTS, DM), 1.0, 6.0, ((0, 128), (1, 4))),
    }


soft_cap = 20.0

def reference(byte_hidden, patch_start, pool_query, in_weight, latent_grad):
    head_dim = HEAD_DIM
    heads = DL // head_dim
    slots = N_SEQ * PCAP
    inv_root = 1.0 / math.sqrt(head_dim)
    hidden_f = byte_hidden.astype(jnp.float32)
    query = pool_query.astype(jnp.float32)
    raw = (hidden_f * query).reshape(BYTES, heads, head_dim).sum(-1) * inv_root
    capped = soft_cap * jnp.tanh(raw / soft_cap)
    weight_exp = jnp.exp(capped)
    position = jnp.arange(BYTES, dtype=jnp.int32)
    patch_id = (jnp.cumsum(patch_start) - 1).astype(jnp.int32)
    start_pos = lax.cummax(jnp.where(patch_start > 0, position, 0).astype(jnp.int32), axis=0)
    owner = (start_pos // BYTE_DEV).astype(jnp.int32)
    counts = patch_start.reshape(N_SEQ, BYTE_DEV).sum(1).astype(jnp.int32)
    offsets = (jnp.cumsum(counts) - counts).astype(jnp.int32)
    slot = (owner * PCAP + patch_id - offsets[owner]).astype(jnp.int32)
    weighted = jnp.repeat(weight_exp, head_dim, axis=1) * hidden_f
    numer = jax.ops.segment_sum(weighted, slot, num_segments=slots)
    denom = jax.ops.segment_sum(weight_exp, slot, num_segments=slots)
    live = (jnp.arange(PCAP, dtype=jnp.int32)[None, :] < counts[:, None]).reshape(slots)
    safe = jnp.where(live[:, None], denom, jnp.float32(1.0))
    pooled = jnp.where(live[:, None], numer / jnp.repeat(safe, head_dim, axis=1), jnp.float32(0.0))
    pooled_low = pooled.astype(jnp.bfloat16)
    latent = jnp.dot(pooled_low, in_weight, preferred_element_type=jnp.float32).astype(jnp.bfloat16)
    quarter = DM // N_MP
    grad_pooled = jnp.zeros((slots, DL), jnp.float32)
    for index in range(N_MP):
        lower = index * quarter
        piece = lax.dot_general(latent_grad[:, lower:lower + quarter], in_weight[:, lower:lower + quarter], (((1,), (1,)), ((), ())), preferred_element_type=jnp.float32)
        piece = lax.optimization_barrier(piece.astype(jnp.bfloat16))
        grad_pooled = grad_pooled + piece.astype(jnp.float32)
    grad_weight = lax.dot_general(pooled_low, latent_grad, (((0,), (0,)), ((), ())), preferred_element_type=jnp.float32) * (1.0 / math.sqrt(slots))
    share = weight_exp / safe[slot]
    grad_rows = grad_pooled[slot]
    pooled_rows = pooled[slot]
    inner = (grad_rows * (hidden_f - pooled_rows)).reshape(BYTES, heads, head_dim).sum(-1)
    coeff = share * inner * (1.0 - (capped / soft_cap) ** 2) * inv_root
    grad_bytes = jnp.repeat(share, head_dim, axis=1) * grad_rows + jnp.repeat(coeff, head_dim, axis=1) * query
    return (latent, grad_weight, grad_bytes.astype(jnp.bfloat16))
```

```python
import functools
import math

import jax
import jax.numpy as jnp
from jax import lax
from jax.experimental import pallas as pl
from jax.experimental.pallas import tpu as pltpu
from jax.sharding import PartitionSpec as P

HEAD_DIM = 64
SOFT_CAP = 20.0
RING = 8
F32 = jnp.float32
BF16 = jnp.bfloat16

W_PAIR, H_NEXT, H_PREV, S_NEXT, S_PREV, G_NEXT, G_PAIR = range(7)
A1A, A1B, A2A, A2B = 7, 14, 21, 28
WPA, WPB = 35, 43
X_UP0, X_UP1, X_UPF, X_DN1, X_DN0, X_DNF = range(51, 57)
PF_PAIR = 57
C_UPR, C_UPD, C_UPS, C_DNR, C_DND, C_DNS = range(65, 71)
D1A, D1B, D2A, D2B = 71, 78, 85, 92
F_PAIR = 99
SLOTS_SEM = 100


def dot(a, b):
    return jnp.dot(a, b, preferred_element_type=F32)


def dot_nt(a, b):
    return lax.dot_general(a, b, (((1,), (1,)), ((), ())), preferred_element_type=F32)


def dot_tn(a, b):
    return lax.dot_general(a, b, (((0,), (0,)), ((), ())), preferred_element_type=F32)


def split(value):
    high = value.astype(BF16)
    return high, (value - high.astype(F32)).astype(BF16)


def iota(shape, dim):
    return lax.broadcasted_iota(jnp.int32, shape, dim)


def kernel(
    h_hbm, st_ref, q_ref, w_ref, g_hbm,
    lat_hbm, gw_ref, gb_hbm,
    hx, st8, st_n, st_p, w32, w32r, wg, wq, gx, gl_send, gc,
    hot, hot_t, xs, ws, ts, pool, den, yv, share_s, diff_s, coef_s,
    pf, part, cr_up, cr_dn, cs_up, cs_dn, c_up, c_dn, zv, lat, gb,
    sa, sb, ra, rb, ta, tb, ua, ub, fin_s, fin_r,
    loc, ss, rs,
):
    s = lax.axis_index("seq")
    a = lax.axis_index("mp")
    n_seq, n_mp = lax.axis_size("seq"), lax.axis_size("mp")
    slots = g_hbm.shape[0]
    rows = h_hbm.shape[0]
    feats = h_hbm.shape[1]
    c = lax.rem(s, 2)
    y = lax.rem(lax.div(s, 2), RING)
    z = lax.div(s, 2 * RING)

    def wrap(value, size):
        return lax.rem(value + size, size)

    pair = (s + 1 - 2 * c, a)
    nxt = (wrap(s + 1, n_seq), a)
    prv = (wrap(s - 1, n_seq), a)
    up = (s, wrap(a + 1, n_mp))
    dn = (s, wrap(a - 1, n_mp))
    a_up, a_dn, a_far = wrap(a + 1, n_mp), wrap(a - 1, n_mp), wrap(a + 2, n_mp)

    def y_at(k):
        return wrap(y + k, RING)

    def z_at(k):
        return wrap(z + k, RING)

    def dev_y(k):
        return ((z * RING + y_at(k)) * 2 + c, a)

    def dev_z(k):
        return ((z_at(k) * RING + y) * 2 + c, a)

    def remote(src, dst, slot, device):
        return pltpu.make_async_remote_copy(
            src_ref=src, dst_ref=dst, send_sem=ss.at[slot], recv_sem=rs.at[slot],
            device_id=device, device_id_type=pl.DeviceIdType.MESH,
        )

    def send(src, dst, slot, device):
        remote(src, dst, slot, device).start()

    def arrived(dst, slot):
        remote(dst, dst, slot, pair).wait_recv()

    def sent(src, slot):
        remote(src, src, slot, pair).wait_send()

    barrier = pltpu.get_barrier_semaphore()

    def greet(device):
        pl.semaphore_signal(barrier, inc=1, device_id=device, device_id_type=pl.DeviceIdType.MESH)

    for device in (pair, nxt, prv, up, dn):
        greet(device)

    def greet_ring(k, carry):
        greet(dev_y(k))
        greet(dev_z(k))
        return carry

    lax.fori_loop(1, RING, greet_ring, 0)

    own_cols = pl.ds(pl.multiple_of(c * 512, 512), 512)
    pair_cols = pl.ds(pl.multiple_of((1 - c) * 512, 512), 512)
    copy_h = pltpu.make_async_copy(h_hbm, hx.at[pl.ds(0, rows)], loc.at[0])
    copy_h.start()
    copy_g = pltpu.make_async_copy(g_hbm, gx.at[pl.ds(0, slots)], loc.at[1])
    copy_g.start()
    copy_gc = pltpu.make_async_copy(g_hbm.at[:, own_cols], gc.at[0], loc.at[2])
    copy_gc.start()

    w32[...] = w_ref[...].astype(F32)
    st_row = st_ref[...].astype(F32)
    st8[...] = jnp.broadcast_to(st_row, st8.shape)
    hx[rows + 16:rows + 112, :] = jnp.zeros((96, feats), BF16)

    pl.semaphore_wait(barrier, 5 + 2 * (RING - 1))

    send(w32, w32r, W_PAIR, pair)
    send(h_hbm.at[pl.ds(rows - 16, 16)], hx.at[pl.ds(rows + 112, 16)], H_NEXT, nxt)
    send(h_hbm.at[pl.ds(0, 16)], hx.at[pl.ds(rows, 16)], H_PREV, prv)
    send(st8.at[:, pl.ds(rows - 128, 128)], st_p, S_NEXT, nxt)
    send(st8.at[:, pl.ds(0, 128)], st_n, S_PREV, prv)
    send(g_hbm.at[:, pair_cols], gc.at[1], G_PAIR, pair)

    r128, c128 = iota((128, 128), 0), iota((128, 128), 1)
    upper = jnp.where(r128 <= c128, 1.0, 0.0).astype(BF16)
    lower = jnp.where(c128 <= r128, 1.0, 0.0).astype(BF16)
    ones = jnp.ones((128, 128), BF16)
    hot_rows = hot.shape[0]
    slot_col = iota((hot_rows, 128), 0).astype(F32)
    lane = iota((128, 128), 1).astype(F32)
    total = jnp.zeros((8, 128), F32)
    lead8 = None
    for k in range(rows // 128):
        st_k = st8[:, 128 * k:128 * k + 128].astype(BF16)
        row_id = total + dot(st_k, upper) - 1.0
        row_id = jnp.where(row_id < 0.0, F32(slots), row_id)
        hot[:, 128 * k:128 * k + 128] = jnp.where(slot_col == row_id[0:1], 1.0, 0.0).astype(BF16)
        st_t = jnp.broadcast_to(st8[0:1, 128 * k:128 * k + 128], (128, 128)).astype(BF16)
        col_id = dot_nt(lower, st_t) + total[0:1] - 1.0
        if k == 0:
            lead8 = jnp.where(col_id[0:8] < 0.0, 1.0, 0.0).astype(F32)
        for j in range(slots // 128):
            hot_t[128 * k:128 * k + 128, 128 * j:128 * j + 128] = jnp.where(
                col_id == lane + 128.0 * j, 1.0, 0.0
            ).astype(BF16)
        total = total + dot(st_k, ones)
    lead8 = jnp.concatenate([lead8, lead8], axis=1)

    arrived(w32r, W_PAIR)
    w_own, w_other = w32[...], w32r[...]
    first = c == 0
    w16 = jnp.concatenate(
        [jnp.where(first, w_own, w_other), jnp.where(first, w_other, w_own)], axis=0
    )
    w_half = jnp.where(first, w16[:, :512], w16[:, 512:]).astype(BF16)
    wg[c, 0, z, y] = w_half[:, :256]
    wg[c, 1, y, z] = w_half[:, 256:]

    def lines(k, carry):
        send(wg.at[c, 0, z, y], wg.at[c, 0, z, y], A1A + k - 1, dev_y(k))
        send(wg.at[c, 1, y, z], wg.at[c, 1, y, z], A1B + k - 1, dev_z(k))
        return carry

    lax.fori_loop(1, RING, lines, 0)

    same = lax.div(iota((feats, feats), 0), HEAD_DIM) == lax.div(iota((feats, feats), 1), HEAD_DIM)
    query = q_ref[...].astype(F32)
    q_mat = jnp.where(same, jnp.broadcast_to(query, (feats, feats)), 0.0).astype(BF16)
    head_ones = jnp.where(same, 1.0, 0.0).astype(BF16)
    inv_root = 1.0 / math.sqrt(HEAD_DIM)

    def score(start, size):
        at = pl.ds(start, size)
        h = hx[at]
        t = jnp.tanh(dot_nt(h, q_mat) * (inv_root / SOFT_CAP))
        w = jnp.exp(SOFT_CAP * t)
        ws[at] = w
        ts[at] = t
        xs[at, 0:256], xs[at, 256:512] = split(w * h.astype(F32))
        xs[at, 512:768], xs[at, 768:1024] = split(w)

    copy_h.wait()

    def score_own(i, carry):
        score(pl.multiple_of(i * 256, 256), 256)
        return carry

    lax.fori_loop(0, rows // 256, score_own, 0)

    def planes(k, carry):
        arrived(wg.at[c, 0, z, y], A1A + k - 1)
        arrived(wg.at[c, 1, y, z], A1B + k - 1)
        return carry

    lax.fori_loop(1, RING, planes, 0)

    def planes_send(k, carry):
        send(wg.at[c, 0, z], wg.at[c, 0, z], A2A + k - 1, dev_z(k))
        send(wg.at[c, 1, y], wg.at[c, 1, y], A2B + k - 1, dev_y(k))
        return carry

    lax.fori_loop(1, RING, planes_send, 0)
    send(wg.at[c, 0, z], wg.at[c, 0, z], WPA, pair)
    send(wg.at[c, 1, y], wg.at[c, 1, y], WPB, pair)

    copy_g.wait()
    pick = iota((16, slots), 1).astype(F32) == (total[0:1, 0:1] - 1.0)
    pick = jnp.where(pick & (iota((16, slots), 0) == 0), 1.0, 0.0).astype(BF16)
    gl_send[...] = dot(pick, gx[0:slots, :]).astype(BF16)
    send(gl_send, gx.at[pl.ds(slots, 16)], G_NEXT, nxt)

    arrived(hx.at[pl.ds(rows + 112, 16)], H_NEXT)
    arrived(hx.at[pl.ds(rows, 16)], H_PREV)
    arrived(st_p, S_NEXT)
    arrived(st_n, S_PREV)
    score(rows, 128)
    after = jnp.where((r128 <= c128) & (c128 < 64), 1.0, 0.0).astype(BF16)
    before = jnp.where((r128 > c128) & (c128 >= 64), 1.0, 0.0).astype(BF16)
    starts_n = jnp.where(s == n_seq - 1, 1.0, st_n[...]).astype(BF16)
    starts_p = jnp.where(s == 0, 1.0, st_p[...]).astype(BF16)
    count = dot(starts_n, after) + dot(starts_p, before)
    halo_slot = jnp.where(iota((8, 128), 1) < 64, total - 1.0, F32(slots))
    halo_slot = jnp.where(count == 0.0, halo_slot, -9.0)
    hot[:, rows:rows + 128] = jnp.where(slot_col == halo_slot[0:1], 1.0, 0.0).astype(BF16)

    onehot = hot[...]
    denom = dot(onehot, xs[:, 512:768]) + dot(onehot, xs[:, 768:1024])
    numer = dot(onehot, xs[:, 0:256]) + dot(onehot, xs[:, 256:512])
    live = denom > 0.0
    denom = jnp.where(live, denom, 1.0)
    pooled = jnp.where(live, numer / denom, 0.0)
    half = slots // 2
    pf[0, a, 0] = pooled[:half].astype(BF16)
    pf[0, a, 1] = pooled[half:slots].astype(BF16)
    send(pf.at[0, a, 0], pf.at[0, a, 0], X_UP0, up)
    send(pf.at[0, a, 1], pf.at[0, a, 1], X_DN1, dn)
    send(pf.at[0, a, 1], pf.at[0, a, 1], X_UP1, up)
    send(pf.at[0, a, 0], pf.at[0, a, 0], X_DN0, dn)

    def to_pair(step, index, part_half):
        send(pf.at[0, index, part_half], pf.at[1, index, part_half],
             PF_PAIR + 2 * step + part_half, pair)

    to_pair(0, a, 0)
    to_pair(0, a, 1)

    yv[:, 0:256], yv[:, 256:512] = split(pooled[:slots])
    yv[:, 512:768], yv[:, 768:1024] = split(denom[:slots])
    prev_pool, prev_den = pooled[slots:slots + 1], denom[slots:slots + 1]

    def lead_rows(value8, size):
        return jnp.concatenate([value8, jnp.zeros((size - 8, feats), F32)], axis=0)

    def weigh(at, extra):
        got = dot(hot_t[at], yv[...])
        pool_rows = got[:, 0:256] + got[:, 256:512]
        den_rows = got[:, 512:768] + got[:, 768:1024]
        if extra is not None:
            pool_rows = pool_rows + extra[0]
            den_rows = den_rows + extra[1]
        t = ts[at]
        share = ws[at] / den_rows
        share_s[at] = share
        diff_s[at] = hx[at].astype(F32) - pool_rows
        coef_s[at] = share * (1.0 - t * t) * (query * inv_root)

    weigh(pl.ds(0, 256), (lead_rows(lead8 * prev_pool, 256), lead_rows(lead8 * prev_den, 256)))

    def weigh_more(i, carry):
        weigh(pl.ds(pl.multiple_of(i * 256, 256), 256), None)
        return carry

    lax.fori_loop(1, rows // 256, weigh_more, 0)

    arrived(pf.at[0, a_dn, 0], X_UP0)
    send(pf.at[0, a_dn, 0], pf.at[0, a_dn, 0], X_UPF, up)
    to_pair(1, a_dn, 0)
    arrived(pf.at[0, a_up, 1], X_DN1)
    send(pf.at[0, a_up, 1], pf.at[0, a_up, 1], X_DNF, dn)
    to_pair(2, a_up, 1)
    arrived(pf.at[0, a_dn, 1], X_UP1)
    to_pair(1, a_dn, 1)
    arrived(pf.at[0, a_up, 0], X_DN0)
    to_pair(2, a_up, 0)

    def gathered(k, carry):
        zk = z_at(-k)
        arrived(wg.at[c, 0, zk], A2A + k - 1)
        send(wg.at[c, 0, zk], wg.at[c, 0, zk], WPA + k, pair)
        yk = y_at(-k)
        arrived(wg.at[c, 1, yk], A2B + k - 1)
        send(wg.at[c, 1, yk], wg.at[c, 1, yk], WPB + k, pair)
        return carry

    lax.fori_loop(1, RING, gathered, 0)

    arrived(pf.at[0, a_far, 0], X_UPF)
    to_pair(3, a_far, 0)
    arrived(pf.at[0, a_far, 1], X_DNF)
    to_pair(3, a_far, 1)

    def from_pair(k, carry):
        arrived(wg.at[1 - c, 0, z_at(-k)], WPA + k)
        arrived(wg.at[1 - c, 1, y_at(-k)], WPB + k)
        return carry

    lax.fori_loop(0, RING, from_pair, 0)

    def natural(zz, carry):
        at = pl.ds(pl.multiple_of(zz * 128, 128), 128)
        for core in range(2):
            wq[2 * core, at] = wg[core, 0, zz].reshape(128, 256)
            wq[2 * core + 1, at] = wg[core, 1, :, zz].reshape(128, 256)
        return carry

    lax.fori_loop(0, RING, natural, 0)
    arrived(gx.at[pl.ds(slots, 16)], G_NEXT)

    def partial_of(index):
        at = pl.ds(pl.multiple_of(index * 256, 256), 256)
        value = dot_nt(gx[:, 0:256], wq[0, at])
        for q in range(1, 4):
            value = value + dot_nt(gx[:, 256 * q:256 * q + 256], wq[q, at])
        return value.astype(BF16)

    part[0] = partial_of(a_far)
    send(part.at[0, pl.ds(0, half)], cr_up, C_UPR, up)
    send(part.at[0, pl.ds(half, half + 16)], cr_dn, C_DNR, dn)
    part[1] = partial_of(a_up)
    send(part.at[1, pl.ds(half, half + 16)], c_up.at[pl.ds(half, half + 16)], C_UPD, up)
    part[2] = partial_of(a_dn)
    send(part.at[2, pl.ds(0, half)], c_dn.at[pl.ds(0, half)], C_DND, dn)
    part[3] = partial_of(a)

    for step, index in ((0, a), (1, a_dn), (2, a_up), (3, a_far)):
        for part_half in range(2):
            arrived(pf.at[1, index, part_half], PF_PAIR + 2 * step + part_half)
    copy_gc.wait()
    arrived(gc.at[1], G_PAIR)

    def grad_block(i, carry):
        value = None
        for core in range(2):
            for part_half in range(2):
                term = dot_tn(
                    pf[core, i, part_half], gc[core, half * part_half:half * part_half + half, :]
                )
                value = term if value is None else value + term
        value = value.astype(BF16)
        for zz in range(2):
            for yy in range(RING):
                at = (zz * RING + yy) * 16
                sa[yy, 2 * i + zz] = value[at:at + 16, 0:256]
                sb[2 * i + zz, yy] = value[at:at + 16, 256:512]
        return carry

    lax.fori_loop(0, 4, grad_block, 0)

    def reduce_send(k, carry):
        send(sa.at[y_at(k)], ra.at[k - 1], D1A + k - 1, dev_y(k))
        send(sb.at[z_at(k)], rb.at[k - 1], D1B + k - 1, dev_z(k))
        return carry

    lax.fori_loop(1, RING, reduce_send, 0)

    arrived(cr_up, C_UPR)
    cs_up[...] = (cr_up[...].astype(F32) + part[1, 0:half].astype(F32)).astype(BF16)
    send(cs_up, c_up.at[pl.ds(0, half)], C_UPS, up)
    arrived(cr_dn, C_DNR)
    cs_dn[...] = (cr_dn[...].astype(F32) + part[2, half:half + half + 16].astype(F32)).astype(BF16)
    send(cs_dn, c_dn.at[pl.ds(half, half + 16)], C_DNS, dn)

    def latent(q, carry):
        for part_half in range(2):
            value = dot(pf[0, 0, part_half], wq[q, 0:256])
            for index in range(1, 4):
                value = value + dot(
                    pf[0, index, part_half], wq[q, 256 * index:256 * index + 256]
                )
            lat[q, half * part_half:half * part_half + half] = value.astype(BF16)
        return carry

    lax.fori_loop(0, 4, latent, 0)
    copies = []
    for q in range(4):
        copies.append(
            pltpu.make_async_copy(lat.at[q], lat_hbm.at[:, pl.ds(256 * q, 256)], loc.at[3 + q])
        )
        copies[-1].start()

    def reduced(k, carry):
        arrived(ra.at[k - 1], D1A + k - 1)
        arrived(rb.at[k - 1], D1B + k - 1)
        return carry

    lax.fori_loop(1, RING, reduced, 0)
    sum_a, sum_b = sa[y].astype(F32), sb[z].astype(F32)
    for k in range(RING - 1):
        sum_a = sum_a + ra[k].astype(F32)
        sum_b = sum_b + rb[k].astype(F32)
    ta[...] = sum_a.astype(BF16)
    tb[...] = sum_b.astype(BF16)

    def reduce_more(k, carry):
        send(ta.at[z_at(k)], ua.at[k - 1], D2A + k - 1, dev_z(k))
        send(tb.at[y_at(k)], ub.at[k - 1], D2B + k - 1, dev_y(k))
        return carry

    lax.fori_loop(1, RING, reduce_more, 0)

    arrived(c_up.at[pl.ds(half, half + 16)], C_UPD)
    arrived(c_dn.at[pl.ds(0, half)], C_DND)
    arrived(c_up.at[pl.ds(0, half)], C_UPS)
    arrived(c_dn.at[pl.ds(half, half + 16)], C_DNS)
    grad = part[3].astype(F32) + c_up[...].astype(F32) + c_dn[...].astype(F32)
    zv[:, 0:256], zv[:, 256:512] = split(grad[:slots])
    prev_grad = grad[slots:slots + 1]

    def byte_grad(at, extra):
        got = dot(hot_t[at], zv[...])
        grad_rows = got[:, 0:256] + got[:, 256:512]
        if extra is not None:
            grad_rows = grad_rows + extra
        high, low = split(grad_rows * diff_s[at])
        inner = dot(high, head_ones) + dot(low, head_ones)
        gb[at] = (share_s[at] * grad_rows + coef_s[at] * inner).astype(BF16)

    byte_grad(pl.ds(0, 256), lead_rows(lead8 * prev_grad, 256))

    def byte_more(i, carry):
        byte_grad(pl.ds(pl.multiple_of(i * 256, 256), 256), None)
        return carry

    lax.fori_loop(1, rows // 256, byte_more, 0)
    copies.append(pltpu.make_async_copy(gb, gb_hbm, loc.at[7]))
    copies[-1].start()

    def reduced_more(k, carry):
        arrived(ua.at[k - 1], D2A + k - 1)
        arrived(ub.at[k - 1], D2B + k - 1)
        return carry

    lax.fori_loop(1, RING, reduced_more, 0)
    sum_a, sum_b = ta[z].astype(F32), tb[y].astype(F32)
    for k in range(RING - 1):
        sum_a = sum_a + ua[k].astype(F32)
        sum_b = sum_b + ub[k].astype(F32)
    grad_scale = 1.0 / math.sqrt(n_seq * slots)
    both = jnp.concatenate([sum_a, sum_b], axis=1) * grad_scale
    fin_s[...] = jnp.where(first, both[8:16], both[0:8])
    send(fin_s, fin_r, F_PAIR, pair)
    mine = jnp.where(first, both[0:8], both[8:16])
    arrived(fin_r, F_PAIR)
    other = fin_r[...]
    gw_ref[:, 0:512] = jnp.where(first, mine, other)
    gw_ref[:, 512:1024] = jnp.where(first, other, mine)

    sent(w32, W_PAIR)
    sent(hx.at[pl.ds(0, 16)], H_NEXT)
    sent(hx.at[pl.ds(0, 16)], H_PREV)
    sent(st_p, S_NEXT)
    sent(st_n, S_PREV)
    sent(gl_send, G_NEXT)
    sent(gc.at[0], G_PAIR)
    sent(wg.at[c, 0, z], WPA)
    sent(wg.at[c, 1, y], WPB)

    def all_sent(k, carry):
        sent(wg.at[c, 0, z, y], A1A + k - 1)
        sent(wg.at[c, 1, y, z], A1B + k - 1)
        sent(wg.at[c, 0, z], A2A + k - 1)
        sent(wg.at[c, 1, y], A2B + k - 1)
        sent(wg.at[c, 0, z], WPA + k)
        sent(wg.at[c, 1, y], WPB + k)
        sent(sa.at[y], D1A + k - 1)
        sent(sb.at[z], D1B + k - 1)
        sent(ta.at[z], D2A + k - 1)
        sent(tb.at[y], D2B + k - 1)
        return carry

    lax.fori_loop(1, RING, all_sent, 0)
    for slot in range(X_UP0, X_DNF + 1):
        sent(pf.at[0, a, 0], slot)
    for slot in range(PF_PAIR, PF_PAIR + 8):
        sent(pf.at[0, a, 0], slot)
    sent(part.at[0, pl.ds(0, half)], C_UPR)
    sent(part.at[0, pl.ds(half, half + 16)], C_DNR)
    sent(part.at[1, pl.ds(half, half + 16)], C_UPD)
    sent(part.at[2, pl.ds(0, half)], C_DND)
    sent(cs_up, C_UPS)
    sent(cs_dn, C_DNS)
    sent(fin_s, F_PAIR)
    for copy in copies:
        copy.wait()


def shards(byte_hidden, patch_start, pool_query, in_weight, latent_grad):
    rows, feats = byte_hidden.shape
    slots, width = latent_grad.shape
    half = slots // 2
    any_spec = pl.BlockSpec(memory_space=pl.ANY)
    vmem = pl.BlockSpec(memory_space=pltpu.VMEM)

    def buf(*shape, dtype=BF16):
        return pltpu.VMEM(shape, dtype)

    scratch = [
        buf(rows + 128, feats),
        buf(8, rows, dtype=F32), buf(8, 128, dtype=F32), buf(8, 128, dtype=F32),
        buf(8, width, dtype=F32), buf(8, width, dtype=F32),
        buf(2, 2, RING, RING, 16, 256),
        buf(4, 1024, 256),
        buf(slots + 16, width), buf(16, width), buf(2, slots, 512),
        buf(slots + 16, rows + 128), buf(rows, slots),
        buf(rows + 128, 1024), buf(rows + 128, feats, dtype=F32), buf(rows + 128, feats, dtype=F32),
        buf(8, 128, dtype=F32), buf(8, 128, dtype=F32),
        buf(slots, 1024),
        buf(rows, feats, dtype=F32), buf(rows, feats, dtype=F32), buf(rows, feats, dtype=F32),
        buf(2, 4, 2, half, 256),
        buf(4, slots + 16, 256),
        buf(half, 256), buf(half + 16, 256), buf(half, 256), buf(half + 16, 256),
        buf(slots + 16, 256), buf(slots + 16, 256),
        buf(slots, 512),
        buf(4, slots, 256), buf(rows, feats),
        buf(RING, RING, 16, 256), buf(RING, RING, 16, 256),
        buf(RING - 1, RING, 16, 256), buf(RING - 1, RING, 16, 256),
        buf(RING, 16, 256), buf(RING, 16, 256),
        buf(RING - 1, 16, 256), buf(RING - 1, 16, 256),
        buf(8, 512, dtype=F32), buf(8, 512, dtype=F32),
        pltpu.SemaphoreType.DMA((8,)),
        pltpu.SemaphoreType.DMA((SLOTS_SEM,)),
        pltpu.SemaphoreType.DMA((SLOTS_SEM,)),
    ]
    return pl.pallas_call(
        kernel,
        out_shape=(
            jax.ShapeDtypeStruct((slots, width), BF16),
            jax.ShapeDtypeStruct((8, width), F32),
            jax.ShapeDtypeStruct((rows, feats), BF16),
        ),
        in_specs=[any_spec, vmem, vmem, vmem, any_spec],
        out_specs=(any_spec, vmem, any_spec),
        scratch_shapes=scratch,
        compiler_params=pltpu.CompilerParams(
            collective_id=0, has_side_effects=True, vmem_limit_bytes=48 * 1024 * 1024
        ),
        name="patch_pool",
    )(
        byte_hidden, patch_start.reshape(1, rows), pool_query.reshape(1, feats),
        in_weight, latent_grad,
    )


def solution(mesh):
    in_specs = (P("seq", "mp"), P("seq"), P("mp"), P("seq", "mp"), P("seq", "mp"))
    out_specs = (P("seq", "mp"), P("seq", "mp"), P("seq", "mp"))
    return jax.shard_map(shards, mesh=mesh, in_specs=in_specs, out_specs=out_specs, check_vma=False)
```

```python
import math

import jax
import jax.numpy as jnp
from jax import lax
from jax.experimental import pallas as pl
from jax.experimental.pallas import tpu as pltpu
from jax.sharding import PartitionSpec as P

HEAD_DIM = 64
SOFT_CAP = 20.0
RING = 8
F32 = jnp.float32
BF16 = jnp.bfloat16
MESH = pl.DeviceIdType.MESH
VMEM_LIMIT = 60 * 1024 * 1024

W_PAIR, H_NEXT, H_PREV, S_NEXT, S_PREV, G_NEXT, G_PAIR, F_PAIR = range(8)
X_UP0, X_UP1, X_UPF, X_DN1, X_DN0, X_DNF = range(8, 14)
C_UPR, C_UPD, C_UPS, C_DNR, C_DND, C_DNS = range(14, 20)
PF_PAIR = 20
A1A, A1B, A2A, A2B = 28, 36, 44, 52
WPA, WPB = 60, 68
D1A = 76
D1B, D2A, D2B = 108, 116, 124
SLOTS_SEM = 132


def dot(a, b):
    return jnp.dot(a, b, preferred_element_type=F32)


def dot_nt(a, b):
    return lax.dot_general(a, b, (((1,), (1,)), ((), ())), preferred_element_type=F32)


def dot_tn(a, b):
    return lax.dot_general(a, b, (((0,), (0,)), ((), ())), preferred_element_type=F32)


def split(value):
    high = value.astype(BF16)
    return high, (value - high.astype(F32)).astype(BF16)


def iota(shape, dim):
    return lax.broadcasted_iota(jnp.int32, shape, dim)


def kernel(
    h_hbm, st_hbm, q_hbm, w_hbm, g_hbm,
    lat_hbm, gw_hbm, gb_hbm,
    lat_ref, gw_ref, gb_ref, hx, st_own, q_own, st8, st_n, st_p, w_own, w32, w32r, wg, wq, gx, gl_send, gc,
    hot, hot_t, xs, ws, ts, yv, share_s, diff_s, coef_s,
    pf, part, cr_up, cr_dn, cs_up, cs_dn, c_up, c_dn, zv,
    sa, sb, ra, rb, ta, tb, ua, ub, fin_s, fin_r,
    loc, ss, rs,
):
    s = lax.axis_index("seq")
    a = lax.axis_index("mp")
    n_seq, n_mp = lax.axis_size("seq"), lax.axis_size("mp")
    slots = g_hbm.shape[0]
    rows, feats = h_hbm.shape
    half = slots // 2
    c = lax.rem(s, 2)
    y = lax.rem(lax.div(s, 2), RING)
    z = lax.div(s, 2 * RING)
    first = c == 0

    def wrap(value, size):
        return lax.rem(value + size, size)

    pair = (s + 1 - 2 * c, a)
    nxt = (wrap(s + 1, n_seq), a)
    prv = (wrap(s - 1, n_seq), a)
    a_up, a_dn, a_far = wrap(a + 1, n_mp), wrap(a - 1, n_mp), wrap(a + 2, n_mp)
    up, dn = (s, a_up), (s, a_dn)

    def y_at(k):
        return wrap(y + k, RING)

    def z_at(k):
        return wrap(z + k, RING)

    def dev_y(k):
        return ((z * RING + y_at(k)) * 2 + c, a)

    def dev_z(k):
        return ((z_at(k) * RING + y) * 2 + c, a)

    def remote(src, dst, slot, device):
        return pltpu.make_async_remote_copy(
            src_ref=src, dst_ref=dst, send_sem=ss.at[slot], recv_sem=rs.at[slot],
            device_id=device, device_id_type=MESH,
        )

    flying, landing = {}, {}

    def note(slot, ref):
        flying[slot] = ref
        landing[slot] = ref

    def send(src, dst, slot, device):
        remote(src, dst, slot, device).start()
        if isinstance(slot, int):
            note(slot, src)

    def arrived(dst, slot):
        remote(dst, dst, slot, pair).wait_recv()
        if isinstance(slot, int):
            landing.pop(slot)

    def ring(body, low=1, high=RING):
        def step(k, carry):
            body(k)
            return carry

        lax.fori_loop(low, high, step, 0)

    def noted(base, ref, low=1, high=RING):
        for k in range(low, high):
            note(base + k, ref)

    def landed(base, low=1, high=RING):
        for k in range(low, high):
            landing.pop(base + k)

    copies = []

    def fetch(src, dst):
        copy = pltpu.make_async_copy(src, dst, loc.at[len(copies)])
        copy.start()
        copies.append(copy)
        return len(copies) - 1

    def fetched(index):
        copies[index].wait()
        copies[index] = None

    def drain():
        for copy in copies:
            if copy is not None:
                copy.wait()
        for slot, ref in landing.items():
            remote(ref, ref, slot, pair).wait_recv()
        for slot, ref in flying.items():
            remote(ref, ref, slot, pair).wait_send()

    barrier = pltpu.get_barrier_semaphore()

    def greet(device):
        pl.semaphore_signal(barrier, inc=1, device_id=device, device_id_type=MESH)

    for device in (pair, nxt, prv, up, dn):
        greet(device)

    def greet_ring(k):
        greet(dev_y(k))
        greet(dev_z(k))

    ring(greet_ring)

    own_cols = pl.ds(pl.multiple_of(c * 512, 512), 512)
    pair_cols = pl.ds(pl.multiple_of((1 - c) * 512, 512), 512)
    copy_w = fetch(w_hbm, w_own)
    copy_st = fetch(st_hbm, st_own)
    copy_q = fetch(q_hbm, q_own)
    copy_h = fetch(h_hbm, hx.at[pl.ds(0, rows)])
    copy_g = fetch(g_hbm, gx.at[pl.ds(0, slots)])
    copy_gc = fetch(g_hbm.at[:, own_cols], gc.at[0])
    hx[rows + 16:rows + 112, :] = jnp.zeros((96, feats), BF16)
    same = lax.div(iota((feats, feats), 0), HEAD_DIM) == lax.div(iota((feats, feats), 1), HEAD_DIM)
    fetched(copy_q)
    query = q_own[...].astype(F32)
    query = jnp.concatenate([query[0:1], query[1:2]], axis=1)
    q_mat = jnp.where(same, jnp.broadcast_to(query, (feats, feats)), 0.0).astype(BF16)
    head_ones = jnp.where(same, 1.0, 0.0).astype(BF16)
    inv_root = 1.0 / math.sqrt(HEAD_DIM)
    fetched(copy_w)
    w32[...] = w_own[...].astype(F32)
    fetched(copy_st)
    st8[...] = jnp.broadcast_to(st_own[...].astype(F32), st8.shape)

    pl.semaphore_wait(barrier, 5 + 2 * (RING - 1))

    send(w32, w32r, W_PAIR, pair)
    send(h_hbm.at[pl.ds(rows - 16, 16)], hx.at[pl.ds(rows + 112, 16)], H_NEXT, nxt)
    send(h_hbm.at[pl.ds(0, 16)], hx.at[pl.ds(rows, 16)], H_PREV, prv)
    send(st8.at[:, pl.ds(rows - 128, 128)], st_p, S_NEXT, nxt)
    send(st8.at[:, pl.ds(0, 128)], st_n, S_PREV, prv)

    arrived(w32r, W_PAIR)
    w_mine, w_other = w32[...], w32r[...]
    w16 = jnp.concatenate(
        [jnp.where(first, w_mine, w_other), jnp.where(first, w_other, w_mine)], axis=0
    )
    w_half = jnp.where(first, w16[:, :512], w16[:, 512:]).astype(BF16)
    wg[c, 0, z, y] = w_half[:, :256]
    wg[c, 1, y, z] = w_half[:, 256:]

    def lines(k):
        send(wg.at[c, 0, z, y], wg.at[c, 0, z, y], A1A + k, dev_y(k))
        send(wg.at[c, 1, y, z], wg.at[c, 1, y, z], A1B + k, dev_z(k))

    ring(lines)
    noted(A1A, wg.at[c, 0, z, y])
    noted(A1B, wg.at[c, 1, y, z])
    send(g_hbm.at[:, pair_cols], gc.at[1], G_PAIR, pair)

    def score(start, size):
        at = pl.ds(start, size)
        h = hx[at]
        t = jnp.tanh(dot_nt(h, q_mat) * (inv_root / SOFT_CAP))
        w = jnp.exp(SOFT_CAP * t)
        ws[at] = w
        ts[at] = t
        xs[at, 0:256], xs[at, 256:512] = split(w * h.astype(F32))
        xs[at, 512:768], xs[at, 768:1024] = split(w)

    fetched(copy_h)

    def score_own(i):
        score(pl.multiple_of(i * 256, 256), 256)

    ring(score_own, 0, rows // 256)

    r128, c128 = iota((128, 128), 0), iota((128, 128), 1)
    upper = jnp.where(r128 <= c128, 1.0, 0.0).astype(BF16)
    lower = jnp.where(c128 <= r128, 1.0, 0.0).astype(BF16)
    ones = jnp.ones((128, 128), BF16)
    hot_rows = hot.shape[0]
    slot_col = iota((hot_rows, 128), 0).astype(F32)
    lane = iota((128, 128), 1).astype(F32)
    total = jnp.zeros((8, 128), F32)
    lead8 = None
    for k in range(rows // 128):
        st_k = st8[:, 128 * k:128 * k + 128].astype(BF16)
        row_id = total + dot(st_k, upper) - 1.0
        row_id = jnp.where(row_id < 0.0, F32(slots), row_id)
        hot[:, 128 * k:128 * k + 128] = jnp.where(slot_col == row_id[0:1], 1.0, 0.0).astype(BF16)
        st_t = jnp.broadcast_to(st8[0:1, 128 * k:128 * k + 128], (128, 128)).astype(BF16)
        col_id = dot_nt(lower, st_t) + total[0:1] - 1.0
        if k == 0:
            lead8 = jnp.where(col_id[0:8] < 0.0, 1.0, 0.0).astype(F32)
        for j in range(slots // 128):
            hot_t[128 * k:128 * k + 128, 128 * j:128 * j + 128] = jnp.where(
                col_id == lane + 128.0 * j, 1.0, 0.0
            ).astype(BF16)
        total = total + dot(st_k, ones)
    lead8 = jnp.concatenate([lead8, lead8], axis=1)

    def planes(k):
        arrived(wg.at[c, 0, z, y], A1A + k)
        arrived(wg.at[c, 1, y, z], A1B + k)

    ring(planes)
    landed(A1A)
    landed(A1B)
    mine_a, mine_b = wg.at[c, 0, z], wg.at[c, 1, y]
    for k in (2, 6, 1, 7):
        send(mine_a, mine_a, A2A + k, dev_z(k))
        send(mine_b, mine_b, A2B + k, dev_y(k))
    send(mine_a, mine_a, WPA, pair)
    send(mine_b, mine_b, WPB, pair)

    arrived(hx.at[pl.ds(rows + 112, 16)], H_NEXT)
    arrived(hx.at[pl.ds(rows, 16)], H_PREV)
    arrived(st_p, S_NEXT)
    arrived(st_n, S_PREV)
    score(rows, 128)
    after = jnp.where((r128 <= c128) & (c128 < 64), 1.0, 0.0).astype(BF16)
    before = jnp.where((r128 > c128) & (c128 >= 64), 1.0, 0.0).astype(BF16)
    starts_n = jnp.where(s == n_seq - 1, 1.0, st_n[...]).astype(BF16)
    starts_p = jnp.where(s == 0, 1.0, st_p[...]).astype(BF16)
    count = dot(starts_n, after) + dot(starts_p, before)
    halo_slot = jnp.where(iota((8, 128), 1) < 64, total - 1.0, F32(slots))
    halo_slot = jnp.where(count == 0.0, halo_slot, -9.0)
    hot[:, rows:rows + 128] = jnp.where(slot_col == halo_slot[0:1], 1.0, 0.0).astype(BF16)

    onehot = hot[...]
    denom = dot(onehot, xs[:, 512:768]) + dot(onehot, xs[:, 768:1024])
    numer = dot(onehot, xs[:, 0:256]) + dot(onehot, xs[:, 256:512])
    live = denom > 0.0
    denom = jnp.where(live, denom, 1.0)
    pooled = jnp.where(live, numer / denom, 0.0)
    pf[0, a, 0] = pooled[:half].astype(BF16)
    pf[0, a, 1] = pooled[half:slots].astype(BF16)
    send(pf.at[0, a, 0], pf.at[0, a, 0], X_UP0, up)
    send(pf.at[0, a, 1], pf.at[0, a, 1], X_DN1, dn)
    send(pf.at[0, a, 1], pf.at[0, a, 1], X_UP1, up)
    send(pf.at[0, a, 0], pf.at[0, a, 0], X_DN0, dn)

    def to_pair(step, index, part_half):
        send(pf.at[0, index, part_half], pf.at[1, index, part_half],
             PF_PAIR + 2 * step + part_half, pair)

    to_pair(0, a, 0)
    to_pair(0, a, 1)

    fetched(copy_g)
    pick = iota((16, slots), 1).astype(F32) == (total[0:1, 0:1] - 1.0)
    pick = jnp.where(pick & (iota((16, slots), 0) == 0), 1.0, 0.0).astype(BF16)
    gl_send[...] = dot(pick, gx[0:slots, :]).astype(BF16)
    send(gl_send, gx.at[pl.ds(slots, 16)], G_NEXT, nxt)

    yv[:, 0:256], yv[:, 256:512] = split(pooled[:slots])
    yv[:, 512:768], yv[:, 768:1024] = split(denom[:slots])
    prev_pool, prev_den = pooled[slots:slots + 1], denom[slots:slots + 1]

    def lead_rows(value8, size):
        return jnp.concatenate([value8, jnp.zeros((size - 8, feats), F32)], axis=0)

    def weigh(at, extra):
        got = dot(hot_t[at], yv[...])
        pool_rows = got[:, 0:256] + got[:, 256:512]
        den_rows = got[:, 512:768] + got[:, 768:1024]
        if extra is not None:
            pool_rows = pool_rows + extra[0]
            den_rows = den_rows + extra[1]
        t = ts[at]
        share = ws[at] / den_rows
        share_s[at] = share
        diff_s[at] = hx[at].astype(F32) - pool_rows
        coef_s[at] = share * (1.0 - t * t) * (query * inv_root)

    weigh(pl.ds(0, 256), (lead_rows(lead8 * prev_pool, 256), lead_rows(lead8 * prev_den, 256)))

    def weigh_more(i):
        weigh(pl.ds(pl.multiple_of(i * 256, 256), 256), None)

    ring(weigh_more, 1, rows // 256)

    def whole(kind, k):
        return wg.at[c, kind, z_at(-k) if kind == 0 else y_at(-k)]

    def piece(kind, k, lower_half):
        return wg.at[c, kind, z_at(-k) if kind == 0 else y_at(-k), pl.ds(0 if lower_half else 4, 4)]

    kinds = ((0, A2A, dev_z, WPA), (1, A2B, dev_y, WPB))
    for kind, base, dev, _ in kinds:
        arrived(whole(kind, 2), base + 2)
        send(whole(kind, 2), whole(kind, 2), base + 3, dev(1))
        send(piece(kind, 2, True), piece(kind, 2, True), base + 4, dev(2))
        arrived(whole(kind, 6), base + 6)
        send(whole(kind, 6), whole(kind, 6), base + 5, dev(-1))
        send(piece(kind, 6, False), piece(kind, 6, False), base, dev(-2))

    arrived(pf.at[0, a_dn, 0], X_UP0)
    send(pf.at[0, a_dn, 0], pf.at[0, a_dn, 0], X_UPF, up)
    arrived(pf.at[0, a_up, 1], X_DN1)
    send(pf.at[0, a_up, 1], pf.at[0, a_up, 1], X_DNF, dn)
    to_pair(1, a_dn, 0)
    to_pair(2, a_up, 1)
    for kind, base, dev, pair_base in kinds:
        for k in (2, 6, 1, 7):
            if k in (1, 7):
                arrived(whole(kind, k), base + k)
            send(whole(kind, k), whole(kind, k), pair_base + k, pair)
    arrived(pf.at[0, a_dn, 1], X_UP1)
    to_pair(1, a_dn, 1)
    arrived(pf.at[0, a_up, 0], X_DN0)
    to_pair(2, a_up, 0)
    for kind, base, dev, pair_base in kinds:
        for k in (3, 5, 4):
            if k == 4:
                arrived(piece(kind, k, True), base + 4)
                arrived(piece(kind, k, False), base)
            else:
                arrived(whole(kind, k), base + k)
            send(whole(kind, k), whole(kind, k), pair_base + k, pair)
    arrived(pf.at[0, a_far, 0], X_UPF)
    to_pair(3, a_far, 0)
    arrived(pf.at[0, a_far, 1], X_DNF)
    to_pair(3, a_far, 1)

    for step, index in ((0, a), (1, a_dn), (2, a_up), (3, a_far)):
        for part_half in range(2):
            arrived(pf.at[1, index, part_half], PF_PAIR + 2 * step + part_half)
    fetched(copy_gc)
    arrived(gc.at[1], G_PAIR)

    def block_at(i):
        turn = jnp.where(i == 0, 2, jnp.where(i == 1, 1, jnp.where(i == 2, 3, 0)))
        return lax.rem(lax.div(z, 2) + turn, 4)

    def grad_block(i):
        index = block_at(i)
        value = None
        for core in range(2):
            for part_half in range(2):
                term = dot_tn(
                    pf[core, index, part_half], gc[core, half * part_half:half * part_half + half, :]
                )
                value = term if value is None else value + term
        value = value.astype(BF16)
        for zz in range(2):
            for yy in range(RING):
                at = (zz * RING + yy) * 16
                sa[yy, 2 * index + zz] = value[at:at + 16, 0:256]
                sb[2 * index + zz, yy] = value[at:at + 16, 256:512]
        two = pl.ds(2 * index, 2)

        def spread(k):
            send(sa.at[y_at(k), two], ra.at[k - 1, two], D1A + 8 * i + k, dev_y(k))

        ring(spread)
        for zz in range(2):
            k = wrap(2 * index + zz - z, RING)

            @pl.when(k > 0)
            def _():
                send(sb.at[2 * index + zz], rb.at[k - 1], D1B + k, dev_z(k))

    ring(grad_block, 0, 4)
    for i in range(4):
        noted(D1A + 8 * i, sa.at[0, pl.ds(0, 2)])
    noted(D1B, sb.at[0])

    def from_pair(k):
        arrived(wg.at[1 - c, 0, z_at(-k)], WPA + k)
        arrived(wg.at[1 - c, 1, y_at(-k)], WPB + k)

    ring(from_pair, 0)
    landed(WPA, 0)
    landed(WPB, 0)

    def natural(zz):
        at = pl.ds(pl.multiple_of(zz * 128, 128), 128)
        for core in range(2):
            wq[2 * core, at] = wg[core, 0, zz].reshape(128, 256)
            wq[2 * core + 1, at] = wg[core, 1, :, zz].reshape(128, 256)

    ring(natural, 0)
    arrived(gx.at[pl.ds(slots, 16)], G_NEXT)

    def partial_of(index):
        at = pl.ds(pl.multiple_of(index * 256, 256), 256)
        value = dot_nt(gx[:, 0:256], wq[0, at])
        for q in range(1, 4):
            value = value + dot_nt(gx[:, 256 * q:256 * q + 256], wq[q, at])
        return value.astype(BF16)

    upper_rows = pl.ds(half, half + 16)
    lower_rows = pl.ds(0, half)
    part[0] = partial_of(a_far)
    send(part.at[0, lower_rows], cr_up, C_UPR, up)
    send(part.at[0, upper_rows], cr_dn, C_DNR, dn)
    part[1] = partial_of(a_up)
    send(part.at[1, upper_rows], c_up.at[upper_rows], C_UPD, up)
    part[2] = partial_of(a_dn)
    send(part.at[2, lower_rows], c_dn.at[lower_rows], C_DND, dn)

    arrived(cr_up, C_UPR)
    cs_up[...] = (cr_up[...].astype(F32) + part[1, 0:half].astype(F32)).astype(BF16)
    send(cs_up, c_up.at[lower_rows], C_UPS, up)
    arrived(cr_dn, C_DNR)
    cs_dn[...] = (cr_dn[...].astype(F32) + part[2, half:half + half + 16].astype(F32)).astype(BF16)
    send(cs_dn, c_dn.at[upper_rows], C_DNS, dn)
    part[3] = partial_of(a)

    def latent(part_half):
        at = pl.ds(pl.multiple_of(part_half * half, half), half)
        for q in range(4):
            value = dot(pf[0, 0, part_half], wq[q, 0:256])
            for index in range(1, 4):
                value = value + dot(
                    pf[0, index, part_half], wq[q, 256 * index:256 * index + 256]
                )
            lat_ref[at, 256 * q:256 * q + 256] = value.astype(BF16)

    ring(latent, 0, 2)
    fetch(lat_ref, lat_hbm)

    def reduced(k):
        def blocks(i):
            two = pl.ds(2 * block_at(i), 2)
            arrived(ra.at[k - 1, two], D1A + 8 * i + k)

        ring(blocks, 0, 4)
        arrived(rb.at[k - 1], D1B + k)

    ring(reduced)
    for i in range(4):
        landed(D1A + 8 * i)
    landed(D1B)
    sum_a, sum_b = sa[y].astype(F32), sb[z].astype(F32)
    for k in range(RING - 1):
        sum_a = sum_a + ra[k].astype(F32)
        sum_b = sum_b + rb[k].astype(F32)
    ta[...] = sum_a.astype(BF16)
    tb[...] = sum_b.astype(BF16)

    def reduce_more(k):
        send(ta.at[z_at(k)], ua.at[k - 1], D2A + k, dev_z(k))
        send(tb.at[y_at(k)], ub.at[k - 1], D2B + k, dev_y(k))

    ring(reduce_more)
    noted(D2A, ta.at[0])
    noted(D2B, tb.at[0])

    arrived(c_up.at[upper_rows], C_UPD)
    arrived(c_dn.at[lower_rows], C_DND)
    arrived(c_up.at[lower_rows], C_UPS)
    arrived(c_dn.at[upper_rows], C_DNS)
    grad = part[3].astype(F32) + c_up[...].astype(F32) + c_dn[...].astype(F32)
    zv[:, 0:256], zv[:, 256:512] = split(grad[:slots])
    prev_grad = grad[slots:slots + 1]

    def byte_grad(at, extra):
        got = dot(hot_t[at], zv[...])
        grad_rows = got[:, 0:256] + got[:, 256:512]
        if extra is not None:
            grad_rows = grad_rows + extra
        high, low = split(grad_rows * diff_s[at])
        inner = dot(high, head_ones) + dot(low, head_ones)
        gb_ref[at] = (share_s[at] * grad_rows + coef_s[at] * inner).astype(BF16)

    byte_grad(pl.ds(0, 256), lead_rows(lead8 * prev_grad, 256))

    def byte_more(i):
        byte_grad(pl.ds(pl.multiple_of(i * 256, 256), 256), None)

    ring(byte_more, 1, rows // 256)
    fetch(gb_ref, gb_hbm)

    def reduced_more(k):
        arrived(ua.at[k - 1], D2A + k)
        arrived(ub.at[k - 1], D2B + k)

    ring(reduced_more)
    landed(D2A)
    landed(D2B)
    sum_a, sum_b = ta[z].astype(F32), tb[y].astype(F32)
    for k in range(RING - 1):
        sum_a = sum_a + ua[k].astype(F32)
        sum_b = sum_b + ub[k].astype(F32)
    grad_scale = 1.0 / math.sqrt(n_seq * slots)
    both = jnp.concatenate([sum_a, sum_b], axis=1) * grad_scale
    fin_s[...] = jnp.where(first, both[8:16], both[0:8])
    send(fin_s, fin_r, F_PAIR, pair)
    mine = jnp.where(first, both[0:8], both[8:16])
    arrived(fin_r, F_PAIR)
    other = fin_r[...]
    gw_ref[:, 0:512] = jnp.where(first, mine, other)
    gw_ref[:, 512:1024] = jnp.where(first, other, mine)
    fetch(gw_ref, gw_hbm)

    drain()


def place(lat_in, gw_in, gb_in, lat_out, gw_out, gb_out, lat, gw, gb, sem_in, sem_out):
    parts = [(lat_in, lat, lat_out, 256 * i, 256) for i in range(lat.shape[0] // 256)]
    parts += [(gb_in, gb, gb_out, 512 * i, 512) for i in range(gb.shape[0] // 512)]
    parts.append((gw_in, gw, gw_out, 0, 8))
    reads, writes = [], []
    for i, (src, mid, dst, start, size) in enumerate(parts):
        at = pl.ds(start, size)
        reads.append(pltpu.make_async_copy(src.at[at], mid.at[at], sem_in.at[i]))
        writes.append(pltpu.make_async_copy(mid.at[at], dst.at[at], sem_out.at[i]))
    for copy in reads:
        copy.start()
    for read, write in zip(reads, writes):
        read.wait()
        write.start()
    for copy in writes:
        copy.wait()


def shards(byte_hidden, patch_start, pool_query, in_weight, latent_grad):
    rows, feats = byte_hidden.shape
    slots, width = latent_grad.shape
    half = slots // 2
    hbm = pl.BlockSpec(memory_space=pltpu.HBM)

    def buf(*shape, dtype=BF16):
        return pltpu.VMEM(shape, dtype)

    scratch = [
        buf(slots, width), buf(8, width, dtype=F32), buf(rows, feats),
        buf(rows + 128, feats), buf(1, rows, dtype=jnp.int32), buf(2, 128),
        buf(8, rows, dtype=F32), buf(8, 128, dtype=F32), buf(8, 128, dtype=F32),
        buf(8, width), buf(8, width, dtype=F32), buf(8, width, dtype=F32),
        buf(2, 2, RING, RING, 16, 256), buf(4, 1024, 256),
        buf(slots + 16, width), buf(16, width), buf(2, slots, 512),
        buf(slots + 16, rows + 128), buf(rows, slots),
        buf(rows + 128, 1024), buf(rows + 128, feats, dtype=F32), buf(rows + 128, feats, dtype=F32),
        buf(slots, 1024),
        buf(rows, feats, dtype=F32), buf(rows, feats, dtype=F32), buf(rows, feats, dtype=F32),
        buf(2, 4, 2, half, 256), buf(4, slots + 16, 256),
        buf(half, 256), buf(half + 16, 256), buf(half, 256), buf(half + 16, 256),
        buf(slots + 16, 256), buf(slots + 16, 256), buf(slots, 512),
        buf(RING, RING, 16, 256), buf(RING, RING, 16, 256),
        buf(RING - 1, RING, 16, 256), buf(RING - 1, RING, 16, 256),
        buf(RING, 16, 256), buf(RING, 16, 256),
        buf(RING - 1, 16, 256), buf(RING - 1, 16, 256),
        buf(8, 512, dtype=F32), buf(8, 512, dtype=F32),
        pltpu.SemaphoreType.DMA((9,)),
        pltpu.SemaphoreType.DMA((SLOTS_SEM,)),
        pltpu.SemaphoreType.DMA((SLOTS_SEM,)),
    ]
    shapes = (
        jax.ShapeDtypeStruct((slots, width), BF16),
        jax.ShapeDtypeStruct((8, width), F32),
        jax.ShapeDtypeStruct((rows, feats), BF16),
    )
    outs = pl.pallas_call(
        kernel,
        out_shape=shapes,
        in_specs=[hbm] * 5,
        out_specs=(hbm, hbm, hbm),
        scratch_shapes=scratch,
        compiler_params=pltpu.CompilerParams(
            collective_id=0, has_side_effects=True, vmem_limit_bytes=VMEM_LIMIT
        ),
        name="patch_pool",
    )(
        byte_hidden, patch_start.reshape(1, rows), pool_query.reshape(2, feats // 2),
        in_weight, latent_grad,
    )
    return pl.pallas_call(
        place,
        out_shape=shapes,
        in_specs=[hbm] * 3,
        out_specs=(hbm, hbm, hbm),
        scratch_shapes=[
            buf(slots, width), buf(8, width, dtype=F32), buf(rows, feats),
            pltpu.SemaphoreType.DMA((5,)), pltpu.SemaphoreType.DMA((5,)),
        ],
        compiler_params=pltpu.CompilerParams(vmem_limit_bytes=VMEM_LIMIT),
        name="place",
    )(*outs)


def solution(mesh):
    in_specs = (P("seq", "mp"), P("seq"), P("mp"), P("seq", "mp"), P("seq", "mp"))
    out_specs = (P("seq", "mp"), P("seq", "mp"), P("seq", "mp"))
    return jax.shard_map(shards, mesh=mesh, in_specs=in_specs, out_specs=out_specs, check_vma=False)
```

```python
import math

import jax
import jax.numpy as jnp
from jax import lax
from jax.experimental import pallas as pl
from jax.experimental.pallas import tpu as pltpu
from jax.sharding import PartitionSpec as P

HEAD_DIM = 64
SOFT_CAP = 20.0
RING = 8
F32 = jnp.float32
BF16 = jnp.bfloat16
MESH = pl.DeviceIdType.MESH
VMEM_LIMIT = 60 * 1024 * 1024

W_PAIR, H_NEXT, H_PREV, S_NEXT, S_PREV, G_NEXT, G_PAIR, F_PAIR = range(8)
X_UP0, X_UP1, X_UPF, X_DN1, X_DN0, X_DNF = range(8, 14)
C_UPR, C_UPD, C_UPS, C_DNR, C_DND, C_DNS = range(14, 20)
PF_PAIR = 20
A1A, A1B, A2A, A2B = 28, 36, 44, 52
WPA, WPB = 60, 68
D1A = 76
D1B, D2A, D2B = 108, 116, 124
SLOTS_SEM = 132


def dot(a, b):
    return jnp.dot(a, b, preferred_element_type=F32)


def dot_nt(a, b):
    return lax.dot_general(a, b, (((1,), (1,)), ((), ())), preferred_element_type=F32)


def split(value):
    high = value.astype(BF16)
    return high, (value - high.astype(F32)).astype(BF16)


def iota(shape, dim):
    return lax.broadcasted_iota(jnp.int32, shape, dim)


def kernel(
    h_hbm, st_hbm, q_hbm, w_hbm, g_hbm,
    lat_hbm, gw_hbm, gb_hbm,
    lat_ref, gw_ref, gb_ref, hx, st_own, q_own, st8, st_n, st_p, w_own, w32, w32r, wg, wq, gx, gl_send, gc,
    hot, hot_t, xs, ws, ts, yv, share_s, diff_s, coef_s,
    pf, part, cr_up, cr_dn, cs_up, cs_dn, c_up, c_dn, zv,
    sa, sb, ra, rb, ta, tb, ua, ub, fin_s, fin_r,
    loc, ss, rs,
):
    s = lax.axis_index("seq")
    a = lax.axis_index("mp")
    n_seq, n_mp = lax.axis_size("seq"), lax.axis_size("mp")
    slots = g_hbm.shape[0]
    rows, feats = h_hbm.shape
    half = slots // 2
    c = lax.rem(s, 2)
    y = lax.rem(lax.div(s, 2), RING)
    z = lax.div(s, 2 * RING)
    first = c == 0

    def wrap(value, size):
        return lax.rem(value + size, size)

    pair = (s + 1 - 2 * c, a)
    nxt = (wrap(s + 1, n_seq), a)
    prv = (wrap(s - 1, n_seq), a)
    a_up, a_dn, a_far = wrap(a + 1, n_mp), wrap(a - 1, n_mp), wrap(a + 2, n_mp)
    up, dn = (s, a_up), (s, a_dn)

    def y_at(k):
        return wrap(y + k, RING)

    def z_at(k):
        return wrap(z + k, RING)

    def dev_y(k):
        return ((z * RING + y_at(k)) * 2 + c, a)

    def dev_z(k):
        return ((z_at(k) * RING + y) * 2 + c, a)

    def remote(src, dst, slot, device):
        return pltpu.make_async_remote_copy(
            src_ref=src, dst_ref=dst, send_sem=ss.at[slot], recv_sem=rs.at[slot],
            device_id=device, device_id_type=MESH,
        )

    flying, landing = {}, {}

    def note(slot, ref):
        flying[slot] = ref
        landing[slot] = ref

    def send(src, dst, slot, device):
        remote(src, dst, slot, device).start()
        if isinstance(slot, int):
            note(slot, src)

    def arrived(dst, slot):
        remote(dst, dst, slot, pair).wait_recv()
        if isinstance(slot, int):
            landing.pop(slot)

    def ring(body, low=1, high=RING):
        def step(k, carry):
            body(k)
            return carry

        lax.fori_loop(low, high, step, 0)

    def noted(base, ref, low=1, high=RING):
        for k in range(low, high):
            note(base + k, ref)

    def landed(base, low=1, high=RING):
        for k in range(low, high):
            landing.pop(base + k)

    copies = []

    def fetch(src, dst):
        copy = pltpu.make_async_copy(src, dst, loc.at[len(copies)])
        copy.start()
        copies.append(copy)
        return len(copies) - 1

    def fetched(index):
        copies[index].wait()
        copies[index] = None

    def drain():
        for copy in copies:
            if copy is not None:
                copy.wait()
        for slot, ref in landing.items():
            remote(ref, ref, slot, pair).wait_recv()
        for slot, ref in flying.items():
            remote(ref, ref, slot, pair).wait_send()

    barrier = pltpu.get_barrier_semaphore()

    def greet(device):
        pl.semaphore_signal(barrier, inc=1, device_id=device, device_id_type=MESH)

    for device in (pair, nxt, prv, up, dn):
        greet(device)

    def greet_ring(k):
        greet(dev_y(k))
        greet(dev_z(k))

    ring(greet_ring)

    own_cols = pl.ds(pl.multiple_of(c * 512, 512), 512)
    pair_cols = pl.ds(pl.multiple_of((1 - c) * 512, 512), 512)
    copy_w = fetch(w_hbm, w_own)
    copy_st = fetch(st_hbm, st_own)
    copy_q = fetch(q_hbm, q_own)
    copy_h = fetch(h_hbm, hx.at[pl.ds(0, rows)])
    copy_g = fetch(g_hbm, gx.at[pl.ds(0, slots)])
    copy_gc = fetch(g_hbm.at[:, own_cols], gc.at[0])
    hx[rows + 16:rows + 112, :] = jnp.zeros((96, feats), BF16)
    same = lax.div(iota((feats, feats), 0), HEAD_DIM) == lax.div(iota((feats, feats), 1), HEAD_DIM)
    fetched(copy_q)
    query = q_own[...].astype(F32)
    query = jnp.concatenate([query[0:1], query[1:2]], axis=1)
    q_mat = jnp.where(same, jnp.broadcast_to(query, (feats, feats)), 0.0).astype(BF16)
    head_ones = jnp.where(same, 1.0, 0.0).astype(BF16)
    inv_root = 1.0 / math.sqrt(HEAD_DIM)
    fetched(copy_w)
    w32[...] = w_own[...].astype(F32)
    fetched(copy_st)
    st8[...] = st_own[...].astype(F32)

    pl.semaphore_wait(barrier, 5 + 2 * (RING - 1))

    send(w32, w32r, W_PAIR, pair)
    send(h_hbm.at[pl.ds(rows - 16, 16)], hx.at[pl.ds(rows + 112, 16)], H_NEXT, nxt)
    send(h_hbm.at[pl.ds(0, 16)], hx.at[pl.ds(rows, 16)], H_PREV, prv)
    send(st8, st_p, S_NEXT, nxt)
    send(st8, st_n, S_PREV, prv)

    def score(start, size):
        at = pl.ds(start, size)
        h = hx[at]
        t = jnp.tanh(dot_nt(h, q_mat) * (inv_root / SOFT_CAP))
        w = jnp.exp(SOFT_CAP * t)
        ws[at] = w
        ts[at] = t
        xs[at, 0:256], xs[at, 256:512] = split(w * h.astype(F32))
        xs[at, 512:768], xs[at, 768:1024] = split(w)

    def score_own(i):
        score(pl.multiple_of(i * 256, 256), 256)

    fetched(copy_h)
    ring(score_own, 0, rows // 256)

    arrived(w32r, W_PAIR)
    w_mine, w_other = w32[...], w32r[...]
    w16 = jnp.concatenate(
        [jnp.where(first, w_mine, w_other), jnp.where(first, w_other, w_mine)], axis=0
    )
    w_half = jnp.where(first, w16[:, :512], w16[:, 512:]).astype(BF16)
    wg[c, 0, z, y] = w_half[:, :256]
    wg[c, 1, y, z] = w_half[:, 256:]

    def lines(k):
        send(wg.at[c, 0, z, y], wg.at[c, 0, z, y], A1A + k, dev_y(k))
        send(wg.at[c, 1, y, z], wg.at[c, 1, y, z], A1B + k, dev_z(k))

    ring(lines)
    noted(A1A, wg.at[c, 0, z, y])
    noted(A1B, wg.at[c, 1, y, z])
    send(g_hbm.at[:, pair_cols], gc.at[1], G_PAIR, pair)

    r128, c128 = iota((128, 128), 0), iota((128, 128), 1)
    upper = jnp.where(r128 <= c128, 1.0, 0.0).astype(BF16)
    starts = st8[...].astype(BF16)
    within = dot(starts, upper)
    counts = dot(starts, jnp.ones((128, 128), BF16))
    blocks = rows // 128
    spread = jnp.where(iota((blocks, rows), 0) == lax.div(iota((blocks, rows), 1), 128), 1.0, 0.0)
    within_t = lax.dot_general(
        within.astype(BF16), spread.astype(BF16), (((0,), (0,)), ((), ())),
        preferred_element_type=F32,
    )
    hot_rows = hot.shape[0]
    slot_col = iota((hot_rows, 128), 0).astype(F32)
    lane = iota((128, 128), 1).astype(F32)
    total = jnp.zeros((1, 128), F32)
    lead8 = None
    for k in range(blocks):
        row_id = within[k:k + 1] + total - 1.0
        row_id = jnp.where(row_id < 0.0, F32(slots), row_id)
        hot[:, 128 * k:128 * k + 128] = jnp.where(slot_col == row_id, 1.0, 0.0).astype(BF16)
        col_id = within_t[:, 128 * k:128 * k + 128] + total - 1.0
        if k == 0:
            lead8 = jnp.where(col_id[0:8] < 0.0, 1.0, 0.0).astype(F32)
        for j in range(slots // 128):
            hot_t[128 * k:128 * k + 128, 128 * j:128 * j + 128] = jnp.where(
                col_id == lane + 128.0 * j, 1.0, 0.0
            ).astype(BF16)
        total = total + counts[k:k + 1]
    lead8 = jnp.concatenate([lead8, lead8], axis=1)

    onehot = hot[:, 0:rows]
    sums = [dot(onehot, xs[0:rows, 256 * k:256 * k + 256]) for k in range(4)]
    numer, denom = sums[0] + sums[1], sums[2] + sums[3]

    arrived(hx.at[pl.ds(rows + 112, 16)], H_NEXT)
    arrived(hx.at[pl.ds(rows, 16)], H_PREV)
    arrived(st_p, S_NEXT)
    arrived(st_n, S_PREV)
    score(rows, 128)
    after = jnp.where((r128 <= c128) & (c128 < 64), 1.0, 0.0).astype(BF16)
    before = jnp.where((r128 > c128) & (c128 >= 64), 1.0, 0.0).astype(BF16)
    starts_n = jnp.where(s == n_seq - 1, 1.0, jnp.broadcast_to(st_n[0:1], (8, 128))).astype(BF16)
    starts_p = jnp.where(s == 0, 1.0, jnp.broadcast_to(st_p[7:8], (8, 128))).astype(BF16)
    count = dot(starts_n, after) + dot(starts_p, before)
    halo_slot = jnp.where(iota((8, 128), 1) < 64, total - 1.0, F32(slots))
    halo_slot = jnp.where(count == 0.0, halo_slot, -9.0)
    hot[:, rows:rows + 128] = jnp.where(slot_col == halo_slot[0:1], 1.0, 0.0).astype(BF16)

    onehot = hot[:, rows:rows + 128]
    sums = [dot(onehot, xs[rows:rows + 128, 256 * k:256 * k + 256]) for k in range(4)]
    numer, denom = numer + sums[0] + sums[1], denom + sums[2] + sums[3]
    live = denom > 0.0
    denom = jnp.where(live, denom, 1.0)
    pooled = jnp.where(live, numer / denom, 0.0)
    pf[0, a, 0] = pooled[:half].T.astype(BF16)
    pf[0, a, 1] = pooled[half:slots].T.astype(BF16)
    send(pf.at[0, a, 0], pf.at[0, a, 0], X_UP0, up)
    send(pf.at[0, a, 1], pf.at[0, a, 1], X_DN1, dn)
    send(pf.at[0, a, 1], pf.at[0, a, 1], X_UP1, up)
    send(pf.at[0, a, 0], pf.at[0, a, 0], X_DN0, dn)

    def to_pair(step, index, part_half):
        send(pf.at[0, index, part_half], pf.at[1, index, part_half],
             PF_PAIR + 2 * step + part_half, pair)

    to_pair(0, a, 0)
    to_pair(0, a, 1)

    fetched(copy_g)
    pick = iota((16, slots), 1).astype(F32) == (total[0:1, 0:1] - 1.0)
    pick = jnp.where(pick & (iota((16, slots), 0) == 0), 1.0, 0.0).astype(BF16)
    gl_send[...] = dot(pick, gx[0:slots, :]).astype(BF16)
    send(gl_send, gx.at[pl.ds(slots, 16)], G_NEXT, nxt)

    def grad_block(index, column):
        value = None
        for core in range(2):
            for part_half in range(2):
                term = dot(
                    pf[core, index, part_half],
                    gc[core, half * part_half:half * part_half + half, column:column + 256],
                )
                value = term if value is None else value + term
        return value.astype(BF16)

    def pair_features(step, index):
        for part_half in range(2):
            arrived(pf.at[1, index, part_half], PF_PAIR + 2 * step + part_half)

    def grad_y(step, index):
        if step < 3:
            pair_features(step, index)
        value = grad_block(index, 0)
        for zz in range(2):
            for yy in range(RING):
                at = (zz * RING + yy) * 16
                sa[yy, 2 * index + zz] = value[at:at + 16]
        two = pl.ds(2 * index, 2)
        base = D1A + 8 * step

        def spread(k):
            send(sa.at[y_at(k), two], ra.at[k - 1, two], base + k, dev_y(k))

        ring(spread)
        noted(base, sa.at[0, two])

    def finish_y(step, index):
        two = pl.ds(2 * index, 2)
        base = D1A + 8 * step

        def wait(k):
            arrived(ra.at[k - 1, two], base + k)

        ring(wait)
        landed(base)
        value = sa[y, two].astype(F32)
        for k in range(RING - 1):
            value = value + ra[k, two].astype(F32)
        ta[two] = value.astype(BF16)
        for zz in range(2):
            k = wrap(2 * index + zz - z, RING)

            @pl.when(k > 0)
            def _():
                send(ta.at[2 * index + zz], ua.at[k - 1], D2A + k, dev_z(k))

    def grad_z(turn):
        index = lax.rem(lax.div(z, 2) + turn, 4)
        value = grad_block(index, 256)
        for zz in range(2):
            for yy in range(RING):
                at = (zz * RING + yy) * 16
                sb[2 * index + zz, yy] = value[at:at + 16]
        for zz in range(2):
            k = wrap(2 * index + zz - z, RING)

            @pl.when(k > 0)
            def _():
                send(sb.at[2 * index + zz], rb.at[k - 1], D1B + k, dev_z(k))

    yv[:, 0:256], yv[:, 256:512] = split(pooled[:slots])
    yv[:, 512:768], yv[:, 768:1024] = split(denom[:slots])
    prev_pool, prev_den = pooled[slots:slots + 1], denom[slots:slots + 1]

    def lead_rows(value8, size):
        return jnp.concatenate([value8, jnp.zeros((size - 8, feats), F32)], axis=0)

    def weigh(at, extra):
        got = dot(hot_t[at], yv[...])
        pool_rows = got[:, 0:256] + got[:, 256:512]
        den_rows = got[:, 512:768] + got[:, 768:1024]
        if extra is not None:
            pool_rows = pool_rows + extra[0]
            den_rows = den_rows + extra[1]
        t = ts[at]
        share = ws[at] / den_rows
        share_s[at] = share
        diff_s[at] = hx[at].astype(F32) - pool_rows
        coef_s[at] = share * (1.0 - t * t) * (query * inv_root)

    weigh(pl.ds(0, 256), (lead_rows(lead8 * prev_pool, 256), lead_rows(lead8 * prev_den, 256)))

    def weigh_more(i):
        weigh(pl.ds(pl.multiple_of(i * 256, 256), 256), None)

    ring(weigh_more, 1, rows // 512)

    def planes(k):
        arrived(wg.at[c, 0, z, y], A1A + k)
        arrived(wg.at[c, 1, y, z], A1B + k)

    ring(planes)
    landed(A1A)
    landed(A1B)
    mine_a, mine_b = wg.at[c, 0, z], wg.at[c, 1, y]
    for k in (2, 6, 1, 7):
        send(mine_a, mine_a, A2A + k, dev_z(k))
        send(mine_b, mine_b, A2B + k, dev_y(k))
    send(mine_a, mine_a, WPA, pair)
    send(mine_b, mine_b, WPB, pair)

    fetched(copy_gc)
    arrived(gc.at[1], G_PAIR)
    grad_y(0, a)

    def whole(kind, k):
        return wg.at[c, kind, z_at(-k) if kind == 0 else y_at(-k)]

    def piece(kind, k, lower_half):
        return wg.at[c, kind, z_at(-k) if kind == 0 else y_at(-k), pl.ds(0 if lower_half else 4, 4)]

    kinds = ((0, A2A, dev_z, WPA), (1, A2B, dev_y, WPB))

    arrived(pf.at[0, a_dn, 0], X_UP0)
    send(pf.at[0, a_dn, 0], pf.at[0, a_dn, 0], X_UPF, up)
    arrived(pf.at[0, a_up, 1], X_DN1)
    send(pf.at[0, a_up, 1], pf.at[0, a_up, 1], X_DNF, dn)
    to_pair(1, a_dn, 0)
    to_pair(2, a_up, 1)
    ring(weigh_more, rows // 512, rows // 256)
    for kind, base, dev, _ in kinds:
        arrived(whole(kind, 2), base + 2)
        send(whole(kind, 2), whole(kind, 2), base + 3, dev(1))
        send(piece(kind, 2, True), piece(kind, 2, True), base + 4, dev(2))
        arrived(whole(kind, 6), base + 6)
        send(whole(kind, 6), whole(kind, 6), base + 5, dev(-1))
        send(piece(kind, 6, False), piece(kind, 6, False), base, dev(-2))
    arrived(pf.at[0, a_dn, 1], X_UP1)
    to_pair(1, a_dn, 1)
    arrived(pf.at[0, a_up, 0], X_DN0)
    to_pair(2, a_up, 0)
    grad_y(1, a_dn)
    grad_y(2, a_up)
    arrived(pf.at[0, a_far, 0], X_UPF)
    to_pair(3, a_far, 0)
    arrived(pf.at[0, a_far, 1], X_DNF)
    to_pair(3, a_far, 1)
    for kind, base, dev, pair_base in kinds:
        for k in (2, 6, 1, 7):
            if k in (1, 7):
                arrived(whole(kind, k), base + k)
            send(whole(kind, k), whole(kind, k), pair_base + k, pair)
    pair_features(3, a_far)
    for turn in (2, 1, 3, 0):
        grad_z(turn)
    noted(D1B, sb.at[0])
    grad_y(3, a_far)
    for kind, base, dev, pair_base in kinds:
        for k in (3, 5, 4):
            if k == 4:
                arrived(piece(kind, k, True), base + 4)
                arrived(piece(kind, k, False), base)
            else:
                arrived(whole(kind, k), base + k)
            send(whole(kind, k), whole(kind, k), pair_base + k, pair)
    finish_y(0, a)

    def from_pair(k):
        arrived(wg.at[1 - c, 0, z_at(-k)], WPA + k)
        arrived(wg.at[1 - c, 1, y_at(-k)], WPB + k)

    ring(from_pair, 0)
    landed(WPA, 0)
    landed(WPB, 0)

    def natural(zz):
        at = pl.ds(pl.multiple_of(zz * 128, 128), 128)
        for core in range(2):
            wq[2 * core, at] = wg[core, 0, zz].reshape(128, 256)
            wq[2 * core + 1, at] = wg[core, 1, :, zz].reshape(128, 256)

    ring(natural, 0)
    arrived(gx.at[pl.ds(slots, 16)], G_NEXT)

    def partial_of(index):
        at = pl.ds(pl.multiple_of(index * 256, 256), 256)
        value = dot_nt(gx[:, 0:256], wq[0, at])
        for q in range(1, 4):
            value = value + dot_nt(gx[:, 256 * q:256 * q + 256], wq[q, at])
        return value.astype(BF16)

    upper_rows = pl.ds(half, half + 16)
    lower_rows = pl.ds(0, half)
    part[0] = partial_of(a_far)
    send(part.at[0, lower_rows], cr_up, C_UPR, up)
    send(part.at[0, upper_rows], cr_dn, C_DNR, dn)
    part[1] = partial_of(a_up)
    send(part.at[1, upper_rows], c_up.at[upper_rows], C_UPD, up)
    part[2] = partial_of(a_dn)
    send(part.at[2, lower_rows], c_dn.at[lower_rows], C_DND, dn)

    arrived(cr_up, C_UPR)
    cs_up[...] = (cr_up[...].astype(F32) + part[1, 0:half].astype(F32)).astype(BF16)
    send(cs_up, c_up.at[lower_rows], C_UPS, up)
    arrived(cr_dn, C_DNR)
    cs_dn[...] = (cr_dn[...].astype(F32) + part[2, half:half + half + 16].astype(F32)).astype(BF16)
    send(cs_dn, c_dn.at[upper_rows], C_DNS, dn)
    part[3] = partial_of(a)
    finish_y(1, a_dn)
    finish_y(2, a_up)

    def latent(part_half):
        at = pl.ds(pl.multiple_of(part_half * half, half), half)
        values = [None] * 4
        for index in range(4):
            left = pf[0, index, part_half].astype(F32).T.astype(BF16)
            for q in range(4):
                term = dot(left, wq[q, 256 * index:256 * index + 256])
                values[q] = term if values[q] is None else values[q] + term
        for q in range(4):
            lat_ref[at, 256 * q:256 * q + 256] = values[q].astype(BF16)

    ring(latent, 0, 2)
    fetch(lat_ref, lat_hbm)

    finish_y(3, a_far)
    noted(D2A, ta.at[0])

    def reduced(k):
        arrived(rb.at[k - 1], D1B + k)

    ring(reduced)
    landed(D1B)
    sum_b = sb[z].astype(F32)
    for k in range(RING - 1):
        sum_b = sum_b + rb[k].astype(F32)
    tb[...] = sum_b.astype(BF16)

    def reduce_more(k):
        send(tb.at[y_at(k)], ub.at[k - 1], D2B + k, dev_y(k))

    ring(reduce_more)
    noted(D2B, tb.at[0])

    arrived(c_up.at[upper_rows], C_UPD)
    arrived(c_dn.at[lower_rows], C_DND)
    arrived(c_up.at[lower_rows], C_UPS)
    arrived(c_dn.at[upper_rows], C_DNS)
    grad = part[3].astype(F32) + c_up[...].astype(F32) + c_dn[...].astype(F32)
    zv[:, 0:256], zv[:, 256:512] = split(grad[:slots])
    prev_grad = grad[slots:slots + 1]

    def byte_grad(at, extra):
        got = dot(hot_t[at], zv[...])
        grad_rows = got[:, 0:256] + got[:, 256:512]
        if extra is not None:
            grad_rows = grad_rows + extra
        high, low = split(grad_rows * diff_s[at])
        inner = dot(high, head_ones) + dot(low, head_ones)
        gb_ref[at] = (share_s[at] * grad_rows + coef_s[at] * inner).astype(BF16)

    byte_grad(pl.ds(0, 256), lead_rows(lead8 * prev_grad, 256))

    def byte_more(i):
        byte_grad(pl.ds(pl.multiple_of(i * 256, 256), 256), None)

    ring(byte_more, 1, rows // 256)
    fetch(gb_ref, gb_hbm)

    def reduced_more(k):
        arrived(ua.at[k - 1], D2A + k)
        arrived(ub.at[k - 1], D2B + k)

    ring(reduced_more)
    landed(D2A)
    landed(D2B)
    sum_a, sum_b = ta[z].astype(F32), tb[y].astype(F32)
    for k in range(RING - 1):
        sum_a = sum_a + ua[k].astype(F32)
        sum_b = sum_b + ub[k].astype(F32)
    grad_scale = 1.0 / math.sqrt(n_seq * slots)
    both = jnp.concatenate([sum_a, sum_b], axis=1) * grad_scale
    fin_s[...] = jnp.where(first, both[8:16], both[0:8])
    send(fin_s, fin_r, F_PAIR, pair)
    mine = jnp.where(first, both[0:8], both[8:16])
    arrived(fin_r, F_PAIR)
    other = fin_r[...]
    gw_ref[:, 0:512] = jnp.where(first, mine, other)
    gw_ref[:, 512:1024] = jnp.where(first, other, mine)
    fetch(gw_ref, gw_hbm)

    drain()


def place(lat_in, gw_in, gb_in, lat_out, gw_out, gb_out, lat, gw, gb, sem_in, sem_out):
    parts = [(lat_in, lat, lat_out, 64 * i, 64) for i in range(lat.shape[0] // 64)]
    parts += [(gb_in, gb, gb_out, 256 * i, 256) for i in range(gb.shape[0] // 256)]
    parts.append((gw_in, gw, gw_out, 0, 8))
    reads, writes = [], []
    for i, (src, mid, dst, start, size) in enumerate(parts):
        at = pl.ds(start, size)
        reads.append(pltpu.make_async_copy(src.at[at], mid.at[at], sem_in.at[i]))
        writes.append(pltpu.make_async_copy(mid.at[at], dst.at[at], sem_out.at[i]))
    for copy in reads:
        copy.start()
    for read, write in zip(reads, writes):
        read.wait()
        write.start()
    for copy in writes:
        copy.wait()


def shards(byte_hidden, patch_start, pool_query, in_weight, latent_grad):
    rows, feats = byte_hidden.shape
    slots, width = latent_grad.shape
    half = slots // 2
    hbm = pl.BlockSpec(memory_space=pltpu.HBM)

    def buf(*shape, dtype=BF16):
        return pltpu.VMEM(shape, dtype)

    scratch = [
        buf(slots, width), buf(8, width, dtype=F32), buf(rows, feats),
        buf(rows + 128, feats), buf(rows // 128, 128, dtype=jnp.int32), buf(2, 128),
        buf(8, 128, dtype=F32), buf(8, 128, dtype=F32), buf(8, 128, dtype=F32),
        buf(8, width), buf(8, width, dtype=F32), buf(8, width, dtype=F32),
        buf(2, 2, RING, RING, 16, 256), buf(4, 1024, 256),
        buf(slots + 16, width), buf(16, width), buf(2, slots, 512),
        buf(slots + 16, rows + 128), buf(rows, slots),
        buf(rows + 128, 1024), buf(rows + 128, feats, dtype=F32), buf(rows + 128, feats, dtype=F32),
        buf(slots, 1024),
        buf(rows, feats, dtype=F32), buf(rows, feats, dtype=F32), buf(rows, feats, dtype=F32),
        buf(2, 4, 2, half, 256), buf(4, slots + 16, 256),
        buf(half, 256), buf(half + 16, 256), buf(half, 256), buf(half + 16, 256),
        buf(slots + 16, 256), buf(slots + 16, 256), buf(slots, 512),
        buf(RING, RING, 16, 256), buf(RING, RING, 16, 256),
        buf(RING - 1, RING, 16, 256), buf(RING - 1, RING, 16, 256),
        buf(RING, 16, 256), buf(RING, 16, 256),
        buf(RING - 1, 16, 256), buf(RING - 1, 16, 256),
        buf(8, 512, dtype=F32), buf(8, 512, dtype=F32),
        pltpu.SemaphoreType.DMA((9,)),
        pltpu.SemaphoreType.DMA((SLOTS_SEM,)),
        pltpu.SemaphoreType.DMA((SLOTS_SEM,)),
    ]
    shapes = (
        jax.ShapeDtypeStruct((slots, width), BF16),
        jax.ShapeDtypeStruct((8, width), F32),
        jax.ShapeDtypeStruct((rows, feats), BF16),
    )
    outs = pl.pallas_call(
        kernel,
        out_shape=shapes,
        in_specs=[hbm] * 5,
        out_specs=(hbm, hbm, hbm),
        scratch_shapes=scratch,
        compiler_params=pltpu.CompilerParams(
            collective_id=0, has_side_effects=True, vmem_limit_bytes=VMEM_LIMIT
        ),
        name="patch_pool",
    )(
        byte_hidden, patch_start.reshape(rows // 128, 128), pool_query.reshape(2, feats // 2),
        in_weight, latent_grad,
    )
    return pl.pallas_call(
        place,
        out_shape=shapes,
        in_specs=[hbm] * 3,
        out_specs=(hbm, hbm, hbm),
        scratch_shapes=[
            buf(slots, width), buf(8, width, dtype=F32), buf(rows, feats),
            pltpu.SemaphoreType.DMA((13,)), pltpu.SemaphoreType.DMA((13,)),
        ],
        compiler_params=pltpu.CompilerParams(vmem_limit_bytes=VMEM_LIMIT),
        name="place",
    )(*outs)


def solution(mesh):
    in_specs = (P("seq", "mp"), P("seq"), P("mp"), P("seq", "mp"), P("seq", "mp"))
    out_specs = (P("seq", "mp"), P("seq", "mp"), P("seq", "mp"))
    return jax.shard_map(shards, mesh=mesh, in_specs=in_specs, out_specs=out_specs, check_vma=False)
```

```python
import math

import jax
import jax.numpy as jnp
from jax import lax
from jax.experimental import pallas as pl
from jax.experimental.pallas import tpu as pltpu
from jax.sharding import PartitionSpec as P

HEAD_DIM = 64
SOFT_CAP = 20.0
RING = 8
F32 = jnp.float32
BF16 = jnp.bfloat16
MESH = pl.DeviceIdType.MESH
VMEM_LIMIT = 60 * 1024 * 1024

W_PAIR, H_NEXT, H_PREV, S_NEXT, S_PREV, G_NEXT, G_PAIR, F_PAIR = range(8)
X_UP0, X_UP1, X_UPF, X_DN1, X_DN0, X_DNF = range(8, 14)
C_UPR, C_UPD, C_UPS, C_DNR, C_DND, C_DNS = range(14, 20)
PF_PAIR = 20
A1A, A1B, A2A, A2B = 28, 36, 44, 52
WPA, WPB = 60, 68
D1A = 76
D1B, D2A, D2B, D1F, D2F = 108, 116, 124, 132, 140
SLOTS_SEM = 148


def dot(a, b):
    return jnp.dot(a, b, preferred_element_type=F32)


def dot_nt(a, b):
    return lax.dot_general(a, b, (((1,), (1,)), ((), ())), preferred_element_type=F32)


def split(value):
    high = value.astype(BF16)
    return high, (value - high.astype(F32)).astype(BF16)


def iota(shape, dim):
    return lax.broadcasted_iota(jnp.int32, shape, dim)


def kernel(
    h_hbm, st_hbm, q_hbm, w_hbm, g_hbm,
    lat_hbm, gw_hbm, gb_hbm,
    lat_ref, gw_ref, gb_ref, hx, st_own, q_own, st8, st_n, st_p, w_own, w32, w32r, wg, wq, gx, gl_send, gc,
    hot, hot_t, xs, ws, ts, yv, share_s, diff_s, coef_s,
    pf, part, cr_up, cr_dn, cs_up, cs_dn, c_up, c_dn, zv,
    sa, sb, ra, rb, ta, tb, ua, ub, sf, rf, tf, uf, half_b, fin_s, fin_r,
    loc, ss, rs,
):
    s = lax.axis_index("seq")
    a = lax.axis_index("mp")
    n_seq, n_mp = lax.axis_size("seq"), lax.axis_size("mp")
    slots = g_hbm.shape[0]
    rows, feats = h_hbm.shape
    half = slots // 2
    c = lax.rem(s, 2)
    y = lax.rem(lax.div(s, 2), RING)
    z = lax.div(s, 2 * RING)
    first = c == 0

    def wrap(value, size):
        return lax.rem(value + size, size)

    pair = (s + 1 - 2 * c, a)
    nxt = (wrap(s + 1, n_seq), a)
    prv = (wrap(s - 1, n_seq), a)
    a_up, a_dn, a_far = wrap(a + 1, n_mp), wrap(a - 1, n_mp), wrap(a + 2, n_mp)
    up, dn = (s, a_up), (s, a_dn)

    def y_at(k):
        return wrap(y + k, RING)

    def z_at(k):
        return wrap(z + k, RING)

    def dev_y(k):
        return ((z * RING + y_at(k)) * 2 + c, a)

    def dev_z(k):
        return ((z_at(k) * RING + y) * 2 + c, a)

    def remote(src, dst, slot, device):
        return pltpu.make_async_remote_copy(
            src_ref=src, dst_ref=dst, send_sem=ss.at[slot], recv_sem=rs.at[slot],
            device_id=device, device_id_type=MESH,
        )

    flying, landing = {}, {}

    def note(slot, ref):
        flying[slot] = ref
        landing[slot] = ref

    def send(src, dst, slot, device):
        remote(src, dst, slot, device).start()
        if isinstance(slot, int):
            note(slot, src)

    def arrived(dst, slot):
        remote(dst, dst, slot, pair).wait_recv()
        if isinstance(slot, int):
            landing.pop(slot)

    def ring(body, low=1, high=RING):
        def step(k, carry):
            body(k)
            return carry

        lax.fori_loop(low, high, step, 0)

    def noted(base, ref, low=1, high=RING):
        for k in range(low, high):
            note(base + k, ref)

    def landed(base, low=1, high=RING):
        for k in range(low, high):
            landing.pop(base + k)

    copies = []

    def fetch(src, dst):
        copy = pltpu.make_async_copy(src, dst, loc.at[len(copies)])
        copy.start()
        copies.append(copy)
        return len(copies) - 1

    def fetched(index):
        copies[index].wait()
        copies[index] = None

    def drain():
        for copy in copies:
            if copy is not None:
                copy.wait()
        for slot, ref in landing.items():
            remote(ref, ref, slot, pair).wait_recv()
        for slot, ref in flying.items():
            remote(ref, ref, slot, pair).wait_send()

    barrier = pltpu.get_barrier_semaphore()

    def greet(device):
        pl.semaphore_signal(barrier, inc=1, device_id=device, device_id_type=MESH)

    for device in (pair, nxt, prv, up, dn):
        greet(device)

    def greet_ring(k):
        greet(dev_y(k))
        greet(dev_z(k))

    ring(greet_ring)

    own_cols = pl.ds(pl.multiple_of(c * 512, 512), 512)
    pair_cols = pl.ds(pl.multiple_of((1 - c) * 512, 512), 512)
    copy_w = fetch(w_hbm, w_own)
    copy_st = fetch(st_hbm, st_own)
    copy_q = fetch(q_hbm, q_own)
    copy_h = fetch(h_hbm, hx.at[pl.ds(0, rows)])
    copy_g = fetch(g_hbm, gx.at[pl.ds(0, slots)])
    copy_gc = fetch(g_hbm.at[:, own_cols], gc.at[0])
    hx[rows + 16:rows + 112, :] = jnp.zeros((96, feats), BF16)
    same = lax.div(iota((feats, feats), 0), HEAD_DIM) == lax.div(iota((feats, feats), 1), HEAD_DIM)
    fetched(copy_q)
    query = q_own[...].astype(F32)
    query = jnp.concatenate([query[0:1], query[1:2]], axis=1)
    q_mat = jnp.where(same, jnp.broadcast_to(query, (feats, feats)), 0.0).astype(BF16)
    head_ones = jnp.where(same, 1.0, 0.0).astype(BF16)
    inv_root = 1.0 / math.sqrt(HEAD_DIM)
    fetched(copy_w)
    w32[...] = w_own[...].astype(F32)
    fetched(copy_st)
    st8[...] = st_own[...].astype(F32)

    pl.semaphore_wait(barrier, 5 + 2 * (RING - 1))

    send(w32, w32r, W_PAIR, pair)
    send(h_hbm.at[pl.ds(rows - 16, 16)], hx.at[pl.ds(rows + 112, 16)], H_NEXT, nxt)
    send(h_hbm.at[pl.ds(0, 16)], hx.at[pl.ds(rows, 16)], H_PREV, prv)
    send(st8, st_p, S_NEXT, nxt)
    send(st8, st_n, S_PREV, prv)

    def score(start, size):
        at = pl.ds(start, size)
        h = hx[at]
        t = jnp.tanh(dot_nt(h, q_mat) * (inv_root / SOFT_CAP))
        w = jnp.exp(SOFT_CAP * t)
        ws[at] = w
        ts[at] = t
        xs[at, 0:256], xs[at, 256:512] = split(w * h.astype(F32))
        xs[at, 512:768], xs[at, 768:1024] = split(w)

    def score_own(i):
        score(pl.multiple_of(i * 256, 256), 256)

    fetched(copy_h)
    ring(score_own, 0, rows // 256)

    arrived(w32r, W_PAIR)
    w_mine, w_other = w32[...], w32r[...]
    w16 = jnp.concatenate(
        [jnp.where(first, w_mine, w_other), jnp.where(first, w_other, w_mine)], axis=0
    )
    w_half = jnp.where(first, w16[:, :512], w16[:, 512:]).astype(BF16)
    wg[c, 0, z, y] = w_half[:, :256]
    wg[c, 1, y, z] = w_half[:, 256:]

    def lines(k):
        send(wg.at[c, 0, z, y], wg.at[c, 0, z, y], A1A + k, dev_y(k))
        send(wg.at[c, 1, y, z], wg.at[c, 1, y, z], A1B + k, dev_z(k))

    ring(lines)
    noted(A1A, wg.at[c, 0, z, y])
    noted(A1B, wg.at[c, 1, y, z])
    send(g_hbm.at[:, pair_cols], gc.at[1], G_PAIR, pair)

    r128, c128 = iota((128, 128), 0), iota((128, 128), 1)
    upper = jnp.where(r128 <= c128, 1.0, 0.0).astype(BF16)
    starts = st8[...].astype(BF16)
    within = dot(starts, upper)
    counts = dot(starts, jnp.ones((128, 128), BF16))
    blocks = rows // 128
    spread = jnp.where(iota((blocks, rows), 0) == lax.div(iota((blocks, rows), 1), 128), 1.0, 0.0)
    within_t = lax.dot_general(
        within.astype(BF16), spread.astype(BF16), (((0,), (0,)), ((), ())),
        preferred_element_type=F32,
    )
    hot_rows = hot.shape[0]
    slot_col = iota((hot_rows, 128), 0).astype(F32)
    lane = iota((128, 128), 1).astype(F32)
    total = jnp.zeros((1, 128), F32)
    lead8 = None
    for k in range(blocks):
        row_id = within[k:k + 1] + total - 1.0
        row_id = jnp.where(row_id < 0.0, F32(slots), row_id)
        hot[:, 128 * k:128 * k + 128] = jnp.where(slot_col == row_id, 1.0, 0.0).astype(BF16)
        col_id = within_t[:, 128 * k:128 * k + 128] + total - 1.0
        if k == 0:
            lead8 = jnp.where(col_id[0:8] < 0.0, 1.0, 0.0).astype(F32)
        for j in range(slots // 128):
            hot_t[128 * k:128 * k + 128, 128 * j:128 * j + 128] = jnp.where(
                col_id == lane + 128.0 * j, 1.0, 0.0
            ).astype(BF16)
        total = total + counts[k:k + 1]
    lead8 = jnp.concatenate([lead8, lead8], axis=1)

    onehot = hot[:, 0:rows]
    sums = [dot(onehot, xs[0:rows, 256 * k:256 * k + 256]) for k in range(4)]
    numer, denom = sums[0] + sums[1], sums[2] + sums[3]

    arrived(hx.at[pl.ds(rows + 112, 16)], H_NEXT)
    arrived(hx.at[pl.ds(rows, 16)], H_PREV)
    arrived(st_p, S_NEXT)
    arrived(st_n, S_PREV)
    score(rows, 128)
    after = jnp.where((r128 <= c128) & (c128 < 64), 1.0, 0.0).astype(BF16)
    before = jnp.where((r128 > c128) & (c128 >= 64), 1.0, 0.0).astype(BF16)
    starts_n = jnp.where(s == n_seq - 1, 1.0, jnp.broadcast_to(st_n[0:1], (8, 128))).astype(BF16)
    starts_p = jnp.where(s == 0, 1.0, jnp.broadcast_to(st_p[7:8], (8, 128))).astype(BF16)
    count = dot(starts_n, after) + dot(starts_p, before)
    halo_slot = jnp.where(iota((8, 128), 1) < 64, total - 1.0, F32(slots))
    halo_slot = jnp.where(count == 0.0, halo_slot, -9.0)
    hot[:, rows:rows + 128] = jnp.where(slot_col == halo_slot[0:1], 1.0, 0.0).astype(BF16)

    onehot = hot[:, rows:rows + 128]
    sums = [dot(onehot, xs[rows:rows + 128, 256 * k:256 * k + 256]) for k in range(4)]
    numer, denom = numer + sums[0] + sums[1], denom + sums[2] + sums[3]
    live = denom > 0.0
    denom = jnp.where(live, denom, 1.0)
    pooled = jnp.where(live, numer / denom, 0.0)
    pf[0, a, 0] = pooled[:half].T.astype(BF16)
    pf[0, a, 1] = pooled[half:slots].T.astype(BF16)
    send(pf.at[0, a, 0], pf.at[0, a, 0], X_UP0, up)
    send(pf.at[0, a, 1], pf.at[0, a, 1], X_DN1, dn)
    send(pf.at[0, a, 1], pf.at[0, a, 1], X_UP1, up)
    send(pf.at[0, a, 0], pf.at[0, a, 0], X_DN0, dn)

    def to_pair(step, index, part_half):
        send(pf.at[0, index, part_half], pf.at[1, index, part_half],
             PF_PAIR + 2 * step + part_half, pair)

    to_pair(0, a, 0)
    to_pair(0, a, 1)

    fetched(copy_g)
    pick = iota((16, slots), 1).astype(F32) == (total[0:1, 0:1] - 1.0)
    pick = jnp.where(pick & (iota((16, slots), 0) == 0), 1.0, 0.0).astype(BF16)
    gl_send[...] = dot(pick, gx[0:slots, :]).astype(BF16)
    send(gl_send, gx.at[pl.ds(slots, 16)], G_NEXT, nxt)

    def grad_block(index, column):
        value = None
        for core in range(2):
            for part_half in range(2):
                term = dot(
                    pf[core, index, part_half],
                    gc[core, half * part_half:half * part_half + half, column:column + 256],
                )
                value = term if value is None else value + term
        return value.astype(BF16)

    def pair_features(step, index):
        for part_half in range(2):
            arrived(pf.at[1, index, part_half], PF_PAIR + 2 * step + part_half)

    def grad_y(step, index):
        if step < 3:
            pair_features(step, index)
        value = grad_block(index, 0)
        for zz in range(2):
            for yy in range(RING):
                at = (zz * RING + yy) * 16
                sa[yy, 2 * index + zz] = value[at:at + 16]
        two = pl.ds(2 * index, 2)
        base = D1A + 8 * step

        def spread(k):
            send(sa.at[y_at(k), two], ra.at[k - 1, two], base + k, dev_y(k))

        ring(spread)
        noted(base, sa.at[0, two])

    def finish_y(step, index):
        two = pl.ds(2 * index, 2)
        base = D1A + 8 * step

        def wait(k):
            arrived(ra.at[k - 1, two], base + k)

        ring(wait)
        landed(base)
        value = sa[y, two].astype(F32)
        for k in range(RING - 1):
            value = value + ra[k, two].astype(F32)
        ta[two] = value.astype(BF16)
        for zz in range(2):
            k = wrap(2 * index + zz - z, RING)

            @pl.when(k > 0)
            def _():
                send(ta.at[2 * index + zz], ua.at[k - 1], D2A + k, dev_z(k))

    def grad_z(index):
        value = grad_block(index, 256)
        for zz in range(2):
            for yy in range(RING):
                at = (zz * RING + yy) * 16
                sb[2 * index + zz, yy] = value[at:at + 16]
        for zz in range(2):
            k = wrap(2 * index + zz - z, RING)

            @pl.when(k > 0)
            def _():
                send(sb.at[2 * index + zz], rb.at[k - 1], D1B + k, dev_z(k))

    far_here = lax.div(z, 2) == a_far

    def grad_far():
        value = grad_block(a_far, 256)
        for zz in range(2):
            for yy in range(RING):
                at = (zz * RING + yy) * 16
                sf[yy, zz] = value[at:at + 16]

        def spread(k):
            send(sf.at[y_at(k)], rf.at[k - 1], D1F + k, dev_y(k))

        ring(spread)
        noted(D1F, sf.at[0])

    def finish_far():
        def wait(k):
            arrived(rf.at[k - 1], D1F + k)

        ring(wait)
        landed(D1F)
        value = sf[y].astype(F32)
        for k in range(RING - 1):
            value = value + rf[k].astype(F32)
        tf[...] = value.astype(BF16)
        for zz in range(2):
            k = wrap(2 * a_far + zz - z, RING)

            @pl.when(k > 0)
            def _():
                send(tf.at[zz], uf.at[k - 1], D2F + k, dev_z(k))

    yv[:, 0:256], yv[:, 256:512] = split(pooled[:slots])
    yv[:, 512:768], yv[:, 768:1024] = split(denom[:slots])
    prev_pool, prev_den = pooled[slots:slots + 1], denom[slots:slots + 1]

    def lead_rows(value8, size):
        return jnp.concatenate([value8, jnp.zeros((size - 8, feats), F32)], axis=0)

    def weigh(at, extra):
        got = dot(hot_t[at], yv[...])
        pool_rows = got[:, 0:256] + got[:, 256:512]
        den_rows = got[:, 512:768] + got[:, 768:1024]
        if extra is not None:
            pool_rows = pool_rows + extra[0]
            den_rows = den_rows + extra[1]
        t = ts[at]
        share = ws[at] / den_rows
        share_s[at] = share
        diff_s[at] = hx[at].astype(F32) - pool_rows
        coef_s[at] = share * (1.0 - t * t) * (query * inv_root)

    weigh(pl.ds(0, 256), (lead_rows(lead8 * prev_pool, 256), lead_rows(lead8 * prev_den, 256)))

    def weigh_more(i):
        weigh(pl.ds(pl.multiple_of(i * 256, 256), 256), None)

    ring(weigh_more, 1, rows // 512)

    def planes(k):
        arrived(wg.at[c, 0, z, y], A1A + k)
        arrived(wg.at[c, 1, y, z], A1B + k)

    ring(planes)
    landed(A1A)
    landed(A1B)
    mine_a, mine_b = wg.at[c, 0, z], wg.at[c, 1, y]
    for k in (2, 6, 1, 7):
        send(mine_a, mine_a, A2A + k, dev_z(k))
        send(mine_b, mine_b, A2B + k, dev_y(k))
    send(mine_a, mine_a, WPA, pair)
    send(mine_b, mine_b, WPB, pair)

    fetched(copy_gc)
    arrived(gc.at[1], G_PAIR)
    grad_y(0, a)
    grad_z(a)

    def whole(kind, k):
        return wg.at[c, kind, z_at(-k) if kind == 0 else y_at(-k)]

    def piece(kind, k, lower_half):
        return wg.at[c, kind, z_at(-k) if kind == 0 else y_at(-k), pl.ds(0 if lower_half else 4, 4)]

    kinds = ((0, A2A, dev_z, WPA), (1, A2B, dev_y, WPB))

    arrived(pf.at[0, a_dn, 0], X_UP0)
    send(pf.at[0, a_dn, 0], pf.at[0, a_dn, 0], X_UPF, up)
    arrived(pf.at[0, a_up, 1], X_DN1)
    send(pf.at[0, a_up, 1], pf.at[0, a_up, 1], X_DNF, dn)
    to_pair(1, a_dn, 0)
    to_pair(2, a_up, 1)
    ring(weigh_more, rows // 512, rows // 256)
    for kind, base, dev, _ in kinds:
        arrived(whole(kind, 2), base + 2)
        send(whole(kind, 2), whole(kind, 2), base + 3, dev(1))
        send(piece(kind, 2, True), piece(kind, 2, True), base + 4, dev(2))
        arrived(whole(kind, 6), base + 6)
        send(whole(kind, 6), whole(kind, 6), base + 5, dev(-1))
        send(piece(kind, 6, False), piece(kind, 6, False), base, dev(-2))
    arrived(pf.at[0, a_dn, 1], X_UP1)
    to_pair(1, a_dn, 1)
    arrived(pf.at[0, a_up, 0], X_DN0)
    to_pair(2, a_up, 0)
    grad_y(1, a_dn)
    grad_z(a_dn)
    grad_y(2, a_up)
    grad_z(a_up)
    arrived(pf.at[0, a_far, 0], X_UPF)
    to_pair(3, a_far, 0)
    arrived(pf.at[0, a_far, 1], X_DNF)
    to_pair(3, a_far, 1)
    for kind, base, dev, pair_base in kinds:
        for k in (2, 6, 1, 7):
            if k in (1, 7):
                arrived(whole(kind, k), base + k)
            send(whole(kind, k), whole(kind, k), pair_base + k, pair)
    pair_features(3, a_far)
    grad_y(3, a_far)
    grad_far()
    for kind, base, dev, pair_base in kinds:
        for k in (3, 5, 4):
            if k == 4:
                arrived(piece(kind, k, True), base + 4)
                arrived(piece(kind, k, False), base)
            else:
                arrived(whole(kind, k), base + k)
            send(whole(kind, k), whole(kind, k), pair_base + k, pair)
    finish_y(0, a)

    def from_pair(k):
        arrived(wg.at[1 - c, 0, z_at(-k)], WPA + k)
        arrived(wg.at[1 - c, 1, y_at(-k)], WPB + k)

    ring(from_pair, 0)
    landed(WPA, 0)
    landed(WPB, 0)

    def natural(zz):
        at = pl.ds(pl.multiple_of(zz * 128, 128), 128)
        for core in range(2):
            wq[2 * core, at] = wg[core, 0, zz].reshape(128, 256)
            wq[2 * core + 1, at] = wg[core, 1, :, zz].reshape(128, 256)

    ring(natural, 0)
    arrived(gx.at[pl.ds(slots, 16)], G_NEXT)

    def partial_of(index):
        at = pl.ds(pl.multiple_of(index * 256, 256), 256)
        value = dot_nt(gx[:, 0:256], wq[0, at])
        for q in range(1, 4):
            value = value + dot_nt(gx[:, 256 * q:256 * q + 256], wq[q, at])
        return value.astype(BF16)

    upper_rows = pl.ds(half, half + 16)
    lower_rows = pl.ds(0, half)
    part[0] = partial_of(a_far)
    send(part.at[0, lower_rows], cr_up, C_UPR, up)
    send(part.at[0, upper_rows], cr_dn, C_DNR, dn)
    part[1] = partial_of(a_up)
    send(part.at[1, upper_rows], c_up.at[upper_rows], C_UPD, up)
    part[2] = partial_of(a_dn)
    send(part.at[2, lower_rows], c_dn.at[lower_rows], C_DND, dn)

    arrived(cr_up, C_UPR)
    cs_up[...] = (cr_up[...].astype(F32) + part[1, 0:half].astype(F32)).astype(BF16)
    send(cs_up, c_up.at[lower_rows], C_UPS, up)
    arrived(cr_dn, C_DNR)
    cs_dn[...] = (cr_dn[...].astype(F32) + part[2, half:half + half + 16].astype(F32)).astype(BF16)
    send(cs_dn, c_dn.at[upper_rows], C_DNS, dn)
    part[3] = partial_of(a)
    finish_y(1, a_dn)
    finish_y(2, a_up)

    def latent(part_half):
        at = pl.ds(pl.multiple_of(part_half * half, half), half)
        values = [None] * 4
        for index in range(4):
            left = pf[0, index, part_half].astype(F32).T.astype(BF16)
            for q in range(4):
                term = dot(left, wq[q, 256 * index:256 * index + 256])
                values[q] = term if values[q] is None else values[q] + term
        for q in range(4):
            lat_ref[at, 256 * q:256 * q + 256] = values[q].astype(BF16)

    ring(latent, 0, 2)
    fetch(lat_ref, lat_hbm)

    @pl.when(jnp.logical_not(far_here))
    def _():
        def reduced(k):
            arrived(rb.at[k - 1], D1B + k)

        ring(reduced)
        value = sb[z].astype(F32)
        for k in range(RING - 1):
            value = value + rb[k].astype(F32)
        tb[...] = value.astype(BF16)

        def reduce_more(k):
            send(tb.at[y_at(k)], ub.at[k - 1], D2B + k, dev_y(k))

        ring(reduce_more)

    finish_y(3, a_far)
    noted(D2A, ta.at[0])
    finish_far()

    arrived(c_up.at[upper_rows], C_UPD)
    arrived(c_dn.at[lower_rows], C_DND)
    arrived(c_up.at[lower_rows], C_UPS)
    arrived(c_dn.at[upper_rows], C_DNS)
    grad = part[3].astype(F32) + c_up[...].astype(F32) + c_dn[...].astype(F32)
    zv[:, 0:256], zv[:, 256:512] = split(grad[:slots])
    prev_grad = grad[slots:slots + 1]

    def byte_grad(at, extra):
        got = dot(hot_t[at], zv[...])
        grad_rows = got[:, 0:256] + got[:, 256:512]
        if extra is not None:
            grad_rows = grad_rows + extra
        high, low = split(grad_rows * diff_s[at])
        inner = dot(high, head_ones) + dot(low, head_ones)
        gb_ref[at] = (share_s[at] * grad_rows + coef_s[at] * inner).astype(BF16)

    byte_grad(pl.ds(0, 256), lead_rows(lead8 * prev_grad, 256))

    def byte_more(i):
        byte_grad(pl.ds(pl.multiple_of(i * 256, 256), 256), None)

    ring(byte_more, 1, rows // 256)
    fetch(gb_ref, gb_hbm)

    def reduced_more(k):
        arrived(ua.at[k - 1], D2A + k)

    ring(reduced_more)
    landed(D2A)
    sum_a = ta[z].astype(F32)
    for k in range(RING - 1):
        sum_a = sum_a + ua[k].astype(F32)

    @pl.when(far_here)
    def _():
        def wait(k):
            arrived(uf.at[k - 1], D2F + k)

        ring(wait)
        value = tf[lax.rem(z, 2)].astype(F32)
        for k in range(RING - 1):
            value = value + uf[k].astype(F32)
        half_b[...] = value

    @pl.when(jnp.logical_not(far_here))
    def _():
        def wait(k):
            arrived(ub.at[k - 1], D2B + k)

        ring(wait)
        value = tb[y].astype(F32)
        for k in range(RING - 1):
            value = value + ub[k].astype(F32)
        half_b[...] = value

    sum_b = half_b[...]
    grad_scale = 1.0 / math.sqrt(n_seq * slots)
    both = jnp.concatenate([sum_a, sum_b], axis=1) * grad_scale
    fin_s[...] = jnp.where(first, both[8:16], both[0:8])
    send(fin_s, fin_r, F_PAIR, pair)
    mine = jnp.where(first, both[0:8], both[8:16])
    arrived(fin_r, F_PAIR)
    other = fin_r[...]
    gw_ref[:, 0:512] = jnp.where(first, mine, other)
    gw_ref[:, 512:1024] = jnp.where(first, other, mine)
    fetch(gw_ref, gw_hbm)

    def left(k):
        @pl.when(lax.div(z_at(k), 2) != a_far)
        def _():
            remote(sb.at[0], sb.at[0], D1B + k, pair).wait_send()

        @pl.when(lax.div(z_at(k), 2) == a_far)
        def _():
            remote(tf.at[0], tf.at[0], D2F + k, pair).wait_send()

        @pl.when(jnp.logical_not(far_here))
        def _():
            remote(tb.at[0], tb.at[0], D2B + k, pair).wait_send()

    ring(left)
    drain()


def place(lat_in, gw_in, gb_in, lat_out, gw_out, gb_out, lat, gw, gb, sem_in, sem_out):
    parts = [(lat_in, lat, lat_out, 64 * i, 64) for i in range(lat.shape[0] // 64)]
    parts += [(gb_in, gb, gb_out, 256 * i, 256) for i in range(gb.shape[0] // 256)]
    parts.append((gw_in, gw, gw_out, 0, 8))
    reads, writes = [], []
    for i, (src, mid, dst, start, size) in enumerate(parts):
        at = pl.ds(start, size)
        reads.append(pltpu.make_async_copy(src.at[at], mid.at[at], sem_in.at[i]))
        writes.append(pltpu.make_async_copy(mid.at[at], dst.at[at], sem_out.at[i]))
    for copy in reads:
        copy.start()
    for read, write in zip(reads, writes):
        read.wait()
        write.start()
    for copy in writes:
        copy.wait()


def shards(byte_hidden, patch_start, pool_query, in_weight, latent_grad):
    rows, feats = byte_hidden.shape
    slots, width = latent_grad.shape
    half = slots // 2
    hbm = pl.BlockSpec(memory_space=pltpu.HBM)

    def buf(*shape, dtype=BF16):
        return pltpu.VMEM(shape, dtype)

    scratch = [
        buf(slots, width), buf(8, width, dtype=F32), buf(rows, feats),
        buf(rows + 128, feats), buf(rows // 128, 128, dtype=jnp.int32), buf(2, 128),
        buf(8, 128, dtype=F32), buf(8, 128, dtype=F32), buf(8, 128, dtype=F32),
        buf(8, width), buf(8, width, dtype=F32), buf(8, width, dtype=F32),
        buf(2, 2, RING, RING, 16, 256), buf(4, 1024, 256),
        buf(slots + 16, width), buf(16, width), buf(2, slots, 512),
        buf(slots + 16, rows + 128), buf(rows, slots),
        buf(rows + 128, 1024), buf(rows + 128, feats, dtype=F32), buf(rows + 128, feats, dtype=F32),
        buf(slots, 1024),
        buf(rows, feats, dtype=F32), buf(rows, feats, dtype=F32), buf(rows, feats, dtype=F32),
        buf(2, 4, 2, half, 256), buf(4, slots + 16, 256),
        buf(half, 256), buf(half + 16, 256), buf(half, 256), buf(half + 16, 256),
        buf(slots + 16, 256), buf(slots + 16, 256), buf(slots, 512),
        buf(RING, RING, 16, 256), buf(RING, RING, 16, 256),
        buf(RING - 1, RING, 16, 256), buf(RING - 1, RING, 16, 256),
        buf(RING, 16, 256), buf(RING, 16, 256),
        buf(RING - 1, 16, 256), buf(RING - 1, 16, 256),
        buf(RING, 2, 16, 256), buf(RING - 1, 2, 16, 256),
        buf(2, 16, 256), buf(RING - 1, 16, 256), buf(16, 256, dtype=F32),
        buf(8, 512, dtype=F32), buf(8, 512, dtype=F32),
        pltpu.SemaphoreType.DMA((9,)),
        pltpu.SemaphoreType.DMA((SLOTS_SEM,)),
        pltpu.SemaphoreType.DMA((SLOTS_SEM,)),
    ]
    shapes = (
        jax.ShapeDtypeStruct((slots, width), BF16),
        jax.ShapeDtypeStruct((8, width), F32),
        jax.ShapeDtypeStruct((rows, feats), BF16),
    )
    outs = pl.pallas_call(
        kernel,
        out_shape=shapes,
        in_specs=[hbm] * 5,
        out_specs=(hbm, hbm, hbm),
        scratch_shapes=scratch,
        compiler_params=pltpu.CompilerParams(
            collective_id=0, has_side_effects=True, vmem_limit_bytes=VMEM_LIMIT
        ),
        name="patch_pool",
    )(
        byte_hidden, patch_start.reshape(rows // 128, 128), pool_query.reshape(2, feats // 2),
        in_weight, latent_grad,
    )
    return pl.pallas_call(
        place,
        out_shape=shapes,
        in_specs=[hbm] * 3,
        out_specs=(hbm, hbm, hbm),
        scratch_shapes=[
            buf(slots, width), buf(8, width, dtype=F32), buf(rows, feats),
            pltpu.SemaphoreType.DMA((13,)), pltpu.SemaphoreType.DMA((13,)),
        ],
        compiler_params=pltpu.CompilerParams(vmem_limit_bytes=VMEM_LIMIT),
        name="place",
    )(*outs)


def solution(mesh):
    in_specs = (P("seq", "mp"), P("seq"), P("mp"), P("seq", "mp"), P("seq", "mp"))
    out_specs = (P("seq", "mp"), P("seq", "mp"), P("seq", "mp"))
    return jax.shard_map(shards, mesh=mesh, in_specs=in_specs, out_specs=out_specs, check_vma=False)
```

```python
import math

import jax
import jax.numpy as jnp
from jax import lax
from jax.experimental import pallas as pl
from jax.experimental.pallas import tpu as pltpu
from jax.sharding import PartitionSpec as P

HEAD_DIM = 64
SOFT_CAP = 20.0
RING = 8
F32 = jnp.float32
BF16 = jnp.bfloat16
MESH = pl.DeviceIdType.MESH
VMEM_LIMIT = 60 * 1024 * 1024

W_PAIR, H_NEXT, H_PREV, S_NEXT, S_PREV, G_NEXT, G_PAIR, F_PAIR = range(8)
X_UP0, X_UP1, X_UPF, X_DN1, X_DN0, X_DNF = range(8, 14)
C_UPR, C_UPD, C_UPS, C_DNR, C_DND, C_DNS = range(14, 20)
PF_PAIR = 20
A1A, A1B, A2A, A2B = 28, 36, 44, 52
WPA, WPB = 60, 68
D1A = 76
D1B, D2A, D2B = 108, 116, 124
SLOTS_SEM = 132


def dot(a, b):
    return jnp.dot(a, b, preferred_element_type=F32)


def dot_nt(a, b):
    return lax.dot_general(a, b, (((1,), (1,)), ((), ())), preferred_element_type=F32)


def split(value):
    high = value.astype(BF16)
    return high, (value - high.astype(F32)).astype(BF16)


def iota(shape, dim):
    return lax.broadcasted_iota(jnp.int32, shape, dim)


def kernel(
    h_hbm, st_hbm, q_hbm, w_hbm, g_hbm,
    lat_hbm, gw_hbm, gb_hbm,
    lat_ref, gw_ref, gb_ref, hx, st_own, q_own, st8, st_n, st_p, w_own, w32, w32r, wg, wq, gx, gl_send, gc,
    hot, hot_t, xs, ws, ts, yv, share_s, diff_s, coef_s,
    pf, part, cr_up, cr_dn, cs_up, cs_dn, c_up, c_dn, zv,
    sa, sb, ra, rb, up3, up4, dn3, dn4, up_sum, dn_sum, ta, tb, ua, ub, fin_s, fin_r,
    loc, ss, rs,
):
    s = lax.axis_index("seq")
    a = lax.axis_index("mp")
    n_seq, n_mp = lax.axis_size("seq"), lax.axis_size("mp")
    slots = g_hbm.shape[0]
    rows, feats = h_hbm.shape
    half = slots // 2
    c = lax.rem(s, 2)
    y = lax.rem(lax.div(s, 2), RING)
    z = lax.div(s, 2 * RING)
    first = c == 0

    def wrap(value, size):
        return lax.rem(value + size, size)

    pair = (s + 1 - 2 * c, a)
    nxt = (wrap(s + 1, n_seq), a)
    prv = (wrap(s - 1, n_seq), a)
    a_up, a_dn, a_far = wrap(a + 1, n_mp), wrap(a - 1, n_mp), wrap(a + 2, n_mp)
    up, dn = (s, a_up), (s, a_dn)

    def y_at(k):
        return wrap(y + k, RING)

    def z_at(k):
        return wrap(z + k, RING)

    def dev_y(k):
        return ((z * RING + y_at(k)) * 2 + c, a)

    def dev_z(k):
        return ((z_at(k) * RING + y) * 2 + c, a)

    def remote(src, dst, slot, device):
        return pltpu.make_async_remote_copy(
            src_ref=src, dst_ref=dst, send_sem=ss.at[slot], recv_sem=rs.at[slot],
            device_id=device, device_id_type=MESH,
        )

    flying, landing = {}, {}

    def note(slot, ref):
        flying[slot] = ref
        landing[slot] = ref

    def send(src, dst, slot, device):
        remote(src, dst, slot, device).start()
        if isinstance(slot, int):
            note(slot, src)

    def arrived(dst, slot):
        remote(dst, dst, slot, pair).wait_recv()
        if isinstance(slot, int):
            landing.pop(slot)

    def ring(body, low=1, high=RING):
        def step(k, carry):
            body(k)
            return carry

        lax.fori_loop(low, high, step, 0)

    def noted(base, ref, low=1, high=RING):
        for k in range(low, high):
            note(base + k, ref)

    def landed(base, low=1, high=RING):
        for k in range(low, high):
            landing.pop(base + k)

    copies = []

    def fetch(src, dst):
        copy = pltpu.make_async_copy(src, dst, loc.at[len(copies)])
        copy.start()
        copies.append(copy)
        return len(copies) - 1

    def fetched(index):
        copies[index].wait()
        copies[index] = None

    def drain():
        for copy in copies:
            if copy is not None:
                copy.wait()
        for slot, ref in landing.items():
            remote(ref, ref, slot, pair).wait_recv()
        for slot, ref in flying.items():
            remote(ref, ref, slot, pair).wait_send()

    barrier = pltpu.get_barrier_semaphore()

    def greet(device):
        pl.semaphore_signal(barrier, inc=1, device_id=device, device_id_type=MESH)

    for device in (pair, nxt, prv, up, dn):
        greet(device)

    def greet_ring(k):
        greet(dev_y(k))
        greet(dev_z(k))

    ring(greet_ring)

    own_cols = pl.ds(pl.multiple_of(c * 512, 512), 512)
    pair_cols = pl.ds(pl.multiple_of((1 - c) * 512, 512), 512)
    copy_w = fetch(w_hbm, w_own)
    copy_st = fetch(st_hbm, st_own)
    copy_q = fetch(q_hbm, q_own)
    copy_h = fetch(h_hbm, hx.at[pl.ds(0, rows)])
    copy_g = fetch(g_hbm, gx.at[pl.ds(0, slots)])
    copy_gc = fetch(g_hbm.at[:, own_cols], gc.at[0])
    hx[rows + 16:rows + 112, :] = jnp.zeros((96, feats), BF16)
    same = lax.div(iota((feats, feats), 0), HEAD_DIM) == lax.div(iota((feats, feats), 1), HEAD_DIM)
    fetched(copy_q)
    query = q_own[...].astype(F32)
    query = jnp.concatenate([query[0:1], query[1:2]], axis=1)
    q_mat = jnp.where(same, jnp.broadcast_to(query, (feats, feats)), 0.0).astype(BF16)
    head_ones = jnp.where(same, 1.0, 0.0).astype(BF16)
    inv_root = 1.0 / math.sqrt(HEAD_DIM)
    fetched(copy_w)
    w32[...] = w_own[...].astype(F32)
    fetched(copy_st)
    st8[...] = st_own[...].astype(F32)

    pl.semaphore_wait(barrier, 5 + 2 * (RING - 1))

    send(w32, w32r, W_PAIR, pair)
    send(h_hbm.at[pl.ds(rows - 16, 16)], hx.at[pl.ds(rows + 112, 16)], H_NEXT, nxt)
    send(h_hbm.at[pl.ds(0, 16)], hx.at[pl.ds(rows, 16)], H_PREV, prv)
    send(st8, st_p, S_NEXT, nxt)
    send(st8, st_n, S_PREV, prv)

    def score(start, size):
        at = pl.ds(start, size)
        h = hx[at]
        t = jnp.tanh(dot_nt(h, q_mat) * (inv_root / SOFT_CAP))
        w = jnp.exp(SOFT_CAP * t)
        ws[at] = w
        ts[at] = t
        xs[at, 0:256], xs[at, 256:512] = split(w * h.astype(F32))
        xs[at, 512:768], xs[at, 768:1024] = split(w)

    def score_own(i):
        score(pl.multiple_of(i * 256, 256), 256)

    fetched(copy_h)
    ring(score_own, 0, rows // 256)

    arrived(w32r, W_PAIR)
    w_mine, w_other = w32[...], w32r[...]
    w16 = jnp.concatenate(
        [jnp.where(first, w_mine, w_other), jnp.where(first, w_other, w_mine)], axis=0
    )
    w_half = jnp.where(first, w16[:, :512], w16[:, 512:]).astype(BF16)
    wg[c, 0, z, y] = w_half[:, :256]
    wg[c, 1, y, z] = w_half[:, 256:]

    def lines(k):
        send(wg.at[c, 0, z, y], wg.at[c, 0, z, y], A1A + k, dev_y(k))
        send(wg.at[c, 1, y, z], wg.at[c, 1, y, z], A1B + k, dev_z(k))

    ring(lines)
    noted(A1A, wg.at[c, 0, z, y])
    noted(A1B, wg.at[c, 1, y, z])
    send(g_hbm.at[:, pair_cols], gc.at[1], G_PAIR, pair)

    r128, c128 = iota((128, 128), 0), iota((128, 128), 1)
    upper = jnp.where(r128 <= c128, 1.0, 0.0).astype(BF16)
    starts = st8[...].astype(BF16)
    within = dot(starts, upper)
    counts = dot(starts, jnp.ones((128, 128), BF16))
    blocks = rows // 128
    spread = jnp.where(iota((blocks, rows), 0) == lax.div(iota((blocks, rows), 1), 128), 1.0, 0.0)
    within_t = lax.dot_general(
        within.astype(BF16), spread.astype(BF16), (((0,), (0,)), ((), ())),
        preferred_element_type=F32,
    )
    hot_rows = hot.shape[0]
    slot_col = iota((hot_rows, 128), 0).astype(F32)
    lane = iota((128, 128), 1).astype(F32)
    total = jnp.zeros((1, 128), F32)
    lead8 = None
    for k in range(blocks):
        row_id = within[k:k + 1] + total - 1.0
        row_id = jnp.where(row_id < 0.0, F32(slots), row_id)
        hot[:, 128 * k:128 * k + 128] = jnp.where(slot_col == row_id, 1.0, 0.0).astype(BF16)
        col_id = within_t[:, 128 * k:128 * k + 128] + total - 1.0
        if k == 0:
            lead8 = jnp.where(col_id[0:8] < 0.0, 1.0, 0.0).astype(F32)
        for j in range(slots // 128):
            hot_t[128 * k:128 * k + 128, 128 * j:128 * j + 128] = jnp.where(
                col_id == lane + 128.0 * j, 1.0, 0.0
            ).astype(BF16)
        total = total + counts[k:k + 1]
    lead8 = jnp.concatenate([lead8, lead8], axis=1)

    onehot = hot[:, 0:rows]
    sums = [dot(onehot, xs[0:rows, 256 * k:256 * k + 256]) for k in range(4)]
    numer, denom = sums[0] + sums[1], sums[2] + sums[3]

    arrived(hx.at[pl.ds(rows + 112, 16)], H_NEXT)
    arrived(hx.at[pl.ds(rows, 16)], H_PREV)
    arrived(st_p, S_NEXT)
    arrived(st_n, S_PREV)
    score(rows, 128)
    after = jnp.where((r128 <= c128) & (c128 < 64), 1.0, 0.0).astype(BF16)
    before = jnp.where((r128 > c128) & (c128 >= 64), 1.0, 0.0).astype(BF16)
    starts_n = jnp.where(s == n_seq - 1, 1.0, jnp.broadcast_to(st_n[0:1], (8, 128))).astype(BF16)
    starts_p = jnp.where(s == 0, 1.0, jnp.broadcast_to(st_p[7:8], (8, 128))).astype(BF16)
    count = dot(starts_n, after) + dot(starts_p, before)
    halo_slot = jnp.where(iota((8, 128), 1) < 64, total - 1.0, F32(slots))
    halo_slot = jnp.where(count == 0.0, halo_slot, -9.0)
    hot[:, rows:rows + 128] = jnp.where(slot_col == halo_slot[0:1], 1.0, 0.0).astype(BF16)

    onehot = hot[:, rows:rows + 128]
    sums = [dot(onehot, xs[rows:rows + 128, 256 * k:256 * k + 256]) for k in range(4)]
    numer, denom = numer + sums[0] + sums[1], denom + sums[2] + sums[3]
    live = denom > 0.0
    denom = jnp.where(live, denom, 1.0)
    pooled = jnp.where(live, numer / denom, 0.0)
    pf[0, a, 0] = pooled[:half].T.astype(BF16)
    pf[0, a, 1] = pooled[half:slots].T.astype(BF16)
    send(pf.at[0, a, 0], pf.at[0, a, 0], X_UP0, up)
    send(pf.at[0, a, 1], pf.at[0, a, 1], X_DN1, dn)
    send(pf.at[0, a, 1], pf.at[0, a, 1], X_UP1, up)
    send(pf.at[0, a, 0], pf.at[0, a, 0], X_DN0, dn)

    def to_pair(step, index, part_half):
        send(pf.at[0, index, part_half], pf.at[1, index, part_half],
             PF_PAIR + 2 * step + part_half, pair)

    to_pair(0, a, 0)
    to_pair(0, a, 1)

    fetched(copy_g)
    pick = iota((16, slots), 1).astype(F32) == (total[0:1, 0:1] - 1.0)
    pick = jnp.where(pick & (iota((16, slots), 0) == 0), 1.0, 0.0).astype(BF16)
    gl_send[...] = dot(pick, gx[0:slots, :]).astype(BF16)
    send(gl_send, gx.at[pl.ds(slots, 16)], G_NEXT, nxt)

    def grad_block(index, column):
        value = None
        for core in range(2):
            for part_half in range(2):
                term = dot(
                    pf[core, index, part_half],
                    gc[core, half * part_half:half * part_half + half, column:column + 256],
                )
                value = term if value is None else value + term
        return value.astype(BF16)

    def pair_features(step, index):
        for part_half in range(2):
            arrived(pf.at[1, index, part_half], PF_PAIR + 2 * step + part_half)

    def grad_y(step, index):
        if step < 3:
            pair_features(step, index)
        value = grad_block(index, 0)
        for zz in range(2):
            for yy in range(RING):
                at = (zz * RING + yy) * 16
                sa[yy, 2 * index + zz] = value[at:at + 16]
        two = pl.ds(2 * index, 2)
        base = D1A + 8 * step

        def spread(k):
            send(sa.at[y_at(k), two], ra.at[k - 1, two], base + k, dev_y(k))

        ring(spread)
        noted(base, sa.at[0, two])

    def finish_y(step, index):
        two = pl.ds(2 * index, 2)
        base = D1A + 8 * step

        def wait(k):
            arrived(ra.at[k - 1, two], base + k)

        ring(wait)
        landed(base)
        value = sa[y, two].astype(F32)
        for k in range(RING - 1):
            value = value + ra[k, two].astype(F32)
        ta[two] = value.astype(BF16)
        for zz in range(2):
            k = wrap(2 * index + zz - z, RING)

            @pl.when(k > 0)
            def _():
                send(ta.at[2 * index + zz], ua.at[k - 1], D2A + k, dev_z(k))

    def grad_z(turn):
        index = lax.rem(lax.div(z, 2) + turn, 4)
        value = grad_block(index, 256)
        for zz in range(2):
            for yy in range(RING):
                at = (zz * RING + yy) * 16
                sb[2 * index + zz, yy] = value[at:at + 16]

    yv[:, 0:256], yv[:, 256:512] = split(pooled[:slots])
    yv[:, 512:768], yv[:, 768:1024] = split(denom[:slots])
    prev_pool, prev_den = pooled[slots:slots + 1], denom[slots:slots + 1]

    def lead_rows(value8, size):
        return jnp.concatenate([value8, jnp.zeros((size - 8, feats), F32)], axis=0)

    def weigh(at, extra):
        got = dot(hot_t[at], yv[...])
        pool_rows = got[:, 0:256] + got[:, 256:512]
        den_rows = got[:, 512:768] + got[:, 768:1024]
        if extra is not None:
            pool_rows = pool_rows + extra[0]
            den_rows = den_rows + extra[1]
        t = ts[at]
        share = ws[at] / den_rows
        share_s[at] = share
        diff_s[at] = hx[at].astype(F32) - pool_rows
        coef_s[at] = share * (1.0 - t * t) * (query * inv_root)

    weigh(pl.ds(0, 256), (lead_rows(lead8 * prev_pool, 256), lead_rows(lead8 * prev_den, 256)))

    def weigh_more(i):
        weigh(pl.ds(pl.multiple_of(i * 256, 256), 256), None)

    ring(weigh_more, 1, rows // 512)

    def planes(k):
        arrived(wg.at[c, 0, z, y], A1A + k)
        arrived(wg.at[c, 1, y, z], A1B + k)

    ring(planes)
    landed(A1A)
    landed(A1B)
    mine_a, mine_b = wg.at[c, 0, z], wg.at[c, 1, y]
    for k in (2, 6, 1, 7):
        send(mine_a, mine_a, A2A + k, dev_z(k))
        send(mine_b, mine_b, A2B + k, dev_y(k))
    send(mine_a, mine_a, WPA, pair)
    send(mine_b, mine_b, WPB, pair)

    def whole(kind, k):
        return wg.at[c, kind, z_at(-k) if kind == 0 else y_at(-k)]

    def piece(kind, k, lower_half):
        return wg.at[c, kind, z_at(-k) if kind == 0 else y_at(-k), pl.ds(0 if lower_half else 4, 4)]

    kinds = ((0, A2A, dev_z, WPA), (1, A2B, dev_y, WPB))

    arrived(pf.at[0, a_dn, 0], X_UP0)
    send(pf.at[0, a_dn, 0], pf.at[0, a_dn, 0], X_UPF, up)
    arrived(pf.at[0, a_up, 1], X_DN1)
    send(pf.at[0, a_up, 1], pf.at[0, a_up, 1], X_DNF, dn)
    to_pair(1, a_dn, 0)
    to_pair(2, a_up, 1)
    ring(weigh_more, rows // 512, rows // 256)
    for kind, base, dev, _ in kinds:
        arrived(whole(kind, 2), base + 2)
        send(whole(kind, 2), whole(kind, 2), base + 3, dev(1))
        send(piece(kind, 2, True), piece(kind, 2, True), base + 4, dev(2))
        arrived(whole(kind, 6), base + 6)
        send(whole(kind, 6), whole(kind, 6), base + 5, dev(-1))
        send(piece(kind, 6, False), piece(kind, 6, False), base, dev(-2))
    fetched(copy_gc)
    arrived(gc.at[1], G_PAIR)
    grad_y(0, a)

    arrived(pf.at[0, a_dn, 1], X_UP1)
    to_pair(1, a_dn, 1)
    arrived(pf.at[0, a_up, 0], X_DN0)
    to_pair(2, a_up, 0)
    grad_y(1, a_dn)
    grad_y(2, a_up)
    arrived(pf.at[0, a_far, 0], X_UPF)
    to_pair(3, a_far, 0)
    arrived(pf.at[0, a_far, 1], X_DNF)
    to_pair(3, a_far, 1)
    for kind, base, dev, pair_base in kinds:
        for k in (2, 6, 1, 7):
            if k in (1, 7):
                arrived(whole(kind, k), base + k)
            send(whole(kind, k), whole(kind, k), pair_base + k, pair)
    pair_features(3, a_far)
    for turn in range(4):
        grad_z(turn)
    near, last = pl.ds(0, RING // 2), pl.ds(RING // 2, RING // 2)
    send(sb.at[z_at(4), near], up4, D1B + 4, dev_z(2))
    send(sb.at[z_at(4), last], dn4, D1B, dev_z(-2))
    send(sb.at[z_at(3)], up3, D1B + 3, dev_z(1))
    send(sb.at[z_at(5)], dn3, D1B + 5, dev_z(-1))
    send(sb.at[z_at(1)], rb.at[0], D1B + 1, dev_z(1))
    send(sb.at[z_at(7)], rb.at[3], D1B + 7, dev_z(-1))
    grad_y(3, a_far)
    for kind, base, dev, pair_base in kinds:
        for k in (3, 5, 4):
            if k == 4:
                arrived(piece(kind, k, True), base + 4)
                arrived(piece(kind, k, False), base)
            else:
                arrived(whole(kind, k), base + k)
            send(whole(kind, k), whole(kind, k), pair_base + k, pair)

    def from_pair(k):
        arrived(wg.at[1 - c, 0, z_at(-k)], WPA + k)
        arrived(wg.at[1 - c, 1, y_at(-k)], WPB + k)

    ring(from_pair, 0)
    landed(WPA, 0)
    landed(WPB, 0)

    def natural(zz):
        at = pl.ds(pl.multiple_of(zz * 128, 128), 128)
        for core in range(2):
            wq[2 * core, at] = wg[core, 0, zz].reshape(128, 256)
            wq[2 * core + 1, at] = wg[core, 1, :, zz].reshape(128, 256)

    ring(natural, 0)
    arrived(gx.at[pl.ds(slots, 16)], G_NEXT)

    def partial_of(index):
        at = pl.ds(pl.multiple_of(index * 256, 256), 256)
        value = dot_nt(gx[:, 0:256], wq[0, at])
        for q in range(1, 4):
            value = value + dot_nt(gx[:, 256 * q:256 * q + 256], wq[q, at])
        return value.astype(BF16)

    upper_rows = pl.ds(half, half + 16)
    lower_rows = pl.ds(0, half)
    part[0] = partial_of(a_far)
    send(part.at[0, lower_rows], cr_up, C_UPR, up)
    send(part.at[0, upper_rows], cr_dn, C_DNR, dn)
    part[1] = partial_of(a_up)
    send(part.at[1, upper_rows], c_up.at[upper_rows], C_UPD, up)
    part[2] = partial_of(a_dn)
    send(part.at[2, lower_rows], c_dn.at[lower_rows], C_DND, dn)

    arrived(up4, D1B + 4)
    arrived(up3, D1B + 3)
    value = sb[z_at(2)].astype(F32) + up3[...].astype(F32)
    up_sum[near] = (value[:RING // 2] + up4[...].astype(F32)).astype(BF16)
    up_sum[last] = value[RING // 2:].astype(BF16)
    send(up_sum, rb.at[1], D1B + 2, dev_z(2))
    arrived(dn4, D1B)
    arrived(dn3, D1B + 5)
    value = sb[z_at(6)].astype(F32) + dn3[...].astype(F32)
    dn_sum[near] = value[:RING // 2].astype(BF16)
    dn_sum[last] = (value[RING // 2:] + dn4[...].astype(F32)).astype(BF16)
    send(dn_sum, rb.at[2], D1B + 6, dev_z(-2))

    arrived(cr_up, C_UPR)
    cs_up[...] = (cr_up[...].astype(F32) + part[1, 0:half].astype(F32)).astype(BF16)
    send(cs_up, c_up.at[lower_rows], C_UPS, up)
    arrived(cr_dn, C_DNR)
    cs_dn[...] = (cr_dn[...].astype(F32) + part[2, half:half + half + 16].astype(F32)).astype(BF16)
    send(cs_dn, c_dn.at[upper_rows], C_DNS, dn)
    part[3] = partial_of(a)
    finish_y(0, a)
    finish_y(1, a_dn)
    finish_y(2, a_up)

    def latent(part_half):
        at = pl.ds(pl.multiple_of(part_half * half, half), half)
        values = [None] * 4
        for index in range(4):
            left = pf[0, index, part_half].astype(F32).T.astype(BF16)
            for q in range(4):
                term = dot(left, wq[q, 256 * index:256 * index + 256])
                values[q] = term if values[q] is None else values[q] + term
        for q in range(4):
            lat_ref[at, 256 * q:256 * q + 256] = values[q].astype(BF16)

    ring(latent, 0, 2)
    fetch(lat_ref, lat_hbm)

    finish_y(3, a_far)
    noted(D2A, ta.at[0])

    sum_b = sb[z].astype(F32)
    for i, k in enumerate((1, 2, 6, 7)):
        arrived(rb.at[i], D1B + k)
        sum_b = sum_b + rb[i].astype(F32)
    tb[...] = sum_b.astype(BF16)

    def reduce_more(k):
        send(tb.at[y_at(k)], ub.at[k - 1], D2B + k, dev_y(k))

    ring(reduce_more)
    noted(D2B, tb.at[0])

    arrived(c_up.at[upper_rows], C_UPD)
    arrived(c_dn.at[lower_rows], C_DND)
    arrived(c_up.at[lower_rows], C_UPS)
    arrived(c_dn.at[upper_rows], C_DNS)
    grad = part[3].astype(F32) + c_up[...].astype(F32) + c_dn[...].astype(F32)
    zv[:, 0:256], zv[:, 256:512] = split(grad[:slots])
    prev_grad = grad[slots:slots + 1]

    def byte_grad(at, extra):
        got = dot(hot_t[at], zv[...])
        grad_rows = got[:, 0:256] + got[:, 256:512]
        if extra is not None:
            grad_rows = grad_rows + extra
        high, low = split(grad_rows * diff_s[at])
        inner = dot(high, head_ones) + dot(low, head_ones)
        gb_ref[at] = (share_s[at] * grad_rows + coef_s[at] * inner).astype(BF16)

    byte_grad(pl.ds(0, 256), lead_rows(lead8 * prev_grad, 256))

    def byte_more(i):
        byte_grad(pl.ds(pl.multiple_of(i * 256, 256), 256), None)

    ring(byte_more, 1, rows // 256)
    fetch(gb_ref, gb_hbm)

    def reduced_more(k):
        arrived(ua.at[k - 1], D2A + k)
        arrived(ub.at[k - 1], D2B + k)

    ring(reduced_more)
    landed(D2A)
    landed(D2B)
    sum_a, sum_b = ta[z].astype(F32), tb[y].astype(F32)
    for k in range(RING - 1):
        sum_a = sum_a + ua[k].astype(F32)
        sum_b = sum_b + ub[k].astype(F32)
    grad_scale = 1.0 / math.sqrt(n_seq * slots)
    both = jnp.concatenate([sum_a, sum_b], axis=1) * grad_scale
    fin_s[...] = jnp.where(first, both[8:16], both[0:8])
    send(fin_s, fin_r, F_PAIR, pair)
    mine = jnp.where(first, both[0:8], both[8:16])
    arrived(fin_r, F_PAIR)
    other = fin_r[...]
    gw_ref[:, 0:512] = jnp.where(first, mine, other)
    gw_ref[:, 512:1024] = jnp.where(first, other, mine)
    fetch(gw_ref, gw_hbm)

    drain()


def place(lat_in, gw_in, gb_in, lat_out, gw_out, gb_out, lat, gw, gb, sem_in, sem_out):
    parts = [(lat_in, lat, lat_out, 64 * i, 64) for i in range(lat.shape[0] // 64)]
    parts += [(gb_in, gb, gb_out, 256 * i, 256) for i in range(gb.shape[0] // 256)]
    parts.append((gw_in, gw, gw_out, 0, 8))
    reads, writes = [], []
    for i, (src, mid, dst, start, size) in enumerate(parts):
        at = pl.ds(start, size)
        reads.append(pltpu.make_async_copy(src.at[at], mid.at[at], sem_in.at[i]))
        writes.append(pltpu.make_async_copy(mid.at[at], dst.at[at], sem_out.at[i]))
    for copy in reads:
        copy.start()
    for read, write in zip(reads, writes):
        read.wait()
        write.start()
    for copy in writes:
        copy.wait()


def shards(byte_hidden, patch_start, pool_query, in_weight, latent_grad):
    rows, feats = byte_hidden.shape
    slots, width = latent_grad.shape
    half = slots // 2
    hbm = pl.BlockSpec(memory_space=pltpu.HBM)

    def buf(*shape, dtype=BF16):
        return pltpu.VMEM(shape, dtype)

    scratch = [
        buf(slots, width), buf(8, width, dtype=F32), buf(rows, feats),
        buf(rows + 128, feats), buf(rows // 128, 128, dtype=jnp.int32), buf(2, 128),
        buf(8, 128, dtype=F32), buf(8, 128, dtype=F32), buf(8, 128, dtype=F32),
        buf(8, width), buf(8, width, dtype=F32), buf(8, width, dtype=F32),
        buf(2, 2, RING, RING, 16, 256), buf(4, 1024, 256),
        buf(slots + 16, width), buf(16, width), buf(2, slots, 512),
        buf(slots + 16, rows + 128), buf(rows, slots),
        buf(rows + 128, 1024), buf(rows + 128, feats, dtype=F32), buf(rows + 128, feats, dtype=F32),
        buf(slots, 1024),
        buf(rows, feats, dtype=F32), buf(rows, feats, dtype=F32), buf(rows, feats, dtype=F32),
        buf(2, 4, 2, half, 256), buf(4, slots + 16, 256),
        buf(half, 256), buf(half + 16, 256), buf(half, 256), buf(half + 16, 256),
        buf(slots + 16, 256), buf(slots + 16, 256), buf(slots, 512),
        buf(RING, RING, 16, 256), buf(RING, RING, 16, 256),
        buf(RING - 1, RING, 16, 256), buf(4, RING, 16, 256),
        buf(RING, 16, 256), buf(RING // 2, 16, 256), buf(RING, 16, 256), buf(RING // 2, 16, 256),
        buf(RING, 16, 256), buf(RING, 16, 256),
        buf(RING, 16, 256), buf(RING, 16, 256),
        buf(RING - 1, 16, 256), buf(RING - 1, 16, 256),
        buf(8, 512, dtype=F32), buf(8, 512, dtype=F32),
        pltpu.SemaphoreType.DMA((9,)),
        pltpu.SemaphoreType.DMA((SLOTS_SEM,)),
        pltpu.SemaphoreType.DMA((SLOTS_SEM,)),
    ]
    shapes = (
        jax.ShapeDtypeStruct((slots, width), BF16),
        jax.ShapeDtypeStruct((8, width), F32),
        jax.ShapeDtypeStruct((rows, feats), BF16),
    )
    outs = pl.pallas_call(
        kernel,
        out_shape=shapes,
        in_specs=[hbm] * 5,
        out_specs=(hbm, hbm, hbm),
        scratch_shapes=scratch,
        compiler_params=pltpu.CompilerParams(
            collective_id=0, has_side_effects=True, vmem_limit_bytes=VMEM_LIMIT
        ),
        name="patch_pool",
    )(
        byte_hidden, patch_start.reshape(rows // 128, 128), pool_query.reshape(2, feats // 2),
        in_weight, latent_grad,
    )
    return pl.pallas_call(
        place,
        out_shape=shapes,
        in_specs=[hbm] * 3,
        out_specs=(hbm, hbm, hbm),
        scratch_shapes=[
            buf(slots, width), buf(8, width, dtype=F32), buf(rows, feats),
            pltpu.SemaphoreType.DMA((13,)), pltpu.SemaphoreType.DMA((13,)),
        ],
        compiler_params=pltpu.CompilerParams(vmem_limit_bytes=VMEM_LIMIT),
        name="place",
    )(*outs)


def solution(mesh):
    in_specs = (P("seq", "mp"), P("seq"), P("mp"), P("seq", "mp"), P("seq", "mp"))
    out_specs = (P("seq", "mp"), P("seq", "mp"), P("seq", "mp"))
    return jax.shard_map(shards, mesh=mesh, in_specs=in_specs, out_specs=out_specs, check_vma=False)
```

```python
import math

import jax
import jax.numpy as jnp
from jax import lax
from jax.experimental import pallas as pl
from jax.experimental.pallas import tpu as pltpu
from jax.sharding import PartitionSpec as P

HEAD_DIM = 64
SOFT_CAP = 20.0
RING = 8
F32 = jnp.float32
BF16 = jnp.bfloat16
MESH = pl.DeviceIdType.MESH
VMEM_LIMIT = 60 * 1024 * 1024

W_PAIR, H_NEXT, H_PREV, S_NEXT, S_PREV, G_NEXT, G_PAIR, F_PAIR = range(8)
X_UP0, X_UP1, X_UPF, X_DN1, X_DN0, X_DNF = range(8, 14)
C_UPR, C_UPD, C_UPS, C_DNR, C_DND, C_DNS = range(14, 20)
PF_PAIR = 20
A1A, A1B, A2A, A2B = 28, 36, 44, 52
WPA, WPB = 60, 68
D1A = 76
D1B, D2A, D2B = 108, 116, 124
SLOTS_SEM = 132


def dot(a, b):
    return jnp.dot(a, b, preferred_element_type=F32)


def dot_nt(a, b):
    return lax.dot_general(a, b, (((1,), (1,)), ((), ())), preferred_element_type=F32)


def split(value):
    high = value.astype(BF16)
    return high, (value - high.astype(F32)).astype(BF16)


def iota(shape, dim):
    return lax.broadcasted_iota(jnp.int32, shape, dim)


def kernel(
    h_hbm, st_hbm, q_hbm, w_hbm, g_hbm,
    lat_hbm, gw_hbm, gb_hbm,
    lat_ref, gw_ref, gb_ref, hx, st_own, q_own, st8, st_n, st_p, w_own, w32, w32r, wg, wq, gx, gl_send, gc,
    hot, hot_t, xs, ws, ts, yv, share_s, diff_s, coef_s,
    pf, part, cr_up, cr_dn, cs_up, cs_dn, c_up, c_dn, zv,
    sa, sb, ra, rb, up3, up4, dn3, dn4, up_sum, dn_sum, ta, tb, ua, ub, fin_s, fin_r,
    loc, ss, rs,
):
    s = lax.axis_index("seq")
    a = lax.axis_index("mp")
    n_seq, n_mp = lax.axis_size("seq"), lax.axis_size("mp")
    slots = g_hbm.shape[0]
    rows, feats = h_hbm.shape
    half = slots // 2
    c = lax.rem(s, 2)
    y = lax.rem(lax.div(s, 2), RING)
    z = lax.div(s, 2 * RING)
    first = c == 0

    def wrap(value, size):
        return lax.rem(value + size, size)

    pair = (s + 1 - 2 * c, a)
    nxt = (wrap(s + 1, n_seq), a)
    prv = (wrap(s - 1, n_seq), a)
    a_up, a_dn, a_far = wrap(a + 1, n_mp), wrap(a - 1, n_mp), wrap(a + 2, n_mp)
    up, dn = (s, a_up), (s, a_dn)

    def y_at(k):
        return wrap(y + k, RING)

    def z_at(k):
        return wrap(z + k, RING)

    def dev_y(k):
        return ((z * RING + y_at(k)) * 2 + c, a)

    def dev_z(k):
        return ((z_at(k) * RING + y) * 2 + c, a)

    def remote(src, dst, slot, device):
        return pltpu.make_async_remote_copy(
            src_ref=src, dst_ref=dst, send_sem=ss.at[slot], recv_sem=rs.at[slot],
            device_id=device, device_id_type=MESH,
        )

    flying, landing = {}, {}

    def note(slot, ref):
        flying[slot] = ref
        landing[slot] = ref

    def send(src, dst, slot, device):
        remote(src, dst, slot, device).start()
        if isinstance(slot, int):
            note(slot, src)

    def arrived(dst, slot):
        remote(dst, dst, slot, pair).wait_recv()
        if isinstance(slot, int):
            landing.pop(slot)

    def ring(body, low=1, high=RING):
        def step(k, carry):
            body(k)
            return carry

        lax.fori_loop(low, high, step, 0)

    def noted(base, ref, low=1, high=RING):
        for k in range(low, high):
            note(base + k, ref)

    def landed(base, low=1, high=RING):
        for k in range(low, high):
            landing.pop(base + k)

    copies = []

    def fetch(src, dst):
        copy = pltpu.make_async_copy(src, dst, loc.at[len(copies)])
        copy.start()
        copies.append(copy)
        return len(copies) - 1

    def fetched(index):
        copies[index].wait()
        copies[index] = None

    def drain():
        for copy in copies:
            if copy is not None:
                copy.wait()
        for slot, ref in landing.items():
            remote(ref, ref, slot, pair).wait_recv()
        for slot, ref in flying.items():
            remote(ref, ref, slot, pair).wait_send()

    barrier = pltpu.get_barrier_semaphore()

    def greet(device):
        pl.semaphore_signal(barrier, inc=1, device_id=device, device_id_type=MESH)

    for device in (pair, nxt, prv, up, dn):
        greet(device)

    def greet_ring(k):
        greet(dev_y(k))
        greet(dev_z(k))

    ring(greet_ring)

    own_cols = pl.ds(pl.multiple_of(c * 512, 512), 512)
    pair_cols = pl.ds(pl.multiple_of((1 - c) * 512, 512), 512)
    copy_w = fetch(w_hbm, w_own)
    copy_st = fetch(st_hbm, st_own)
    copy_q = fetch(q_hbm, q_own)
    copy_h = fetch(h_hbm, hx.at[pl.ds(0, rows)])
    copy_g = fetch(g_hbm, gx.at[pl.ds(0, slots)])
    copy_gc = fetch(g_hbm.at[:, own_cols], gc.at[0])
    hx[rows + 16:rows + 112, :] = jnp.zeros((96, feats), BF16)
    same = lax.div(iota((feats, feats), 0), HEAD_DIM) == lax.div(iota((feats, feats), 1), HEAD_DIM)
    fetched(copy_q)
    query = q_own[...].astype(F32)
    query = jnp.concatenate([query[0:1], query[1:2]], axis=1)
    q_mat = jnp.where(same, jnp.broadcast_to(query, (feats, feats)), 0.0).astype(BF16)
    head_ones = jnp.where(same, 1.0, 0.0).astype(BF16)
    inv_root = 1.0 / math.sqrt(HEAD_DIM)
    fetched(copy_w)
    w32[...] = w_own[...].astype(F32)
    fetched(copy_st)
    st8[...] = st_own[...].astype(F32)

    pl.semaphore_wait(barrier, 5 + 2 * (RING - 1))

    send(w32, w32r, W_PAIR, pair)
    send(h_hbm.at[pl.ds(rows - 16, 16)], hx.at[pl.ds(rows + 112, 16)], H_NEXT, nxt)
    send(h_hbm.at[pl.ds(0, 16)], hx.at[pl.ds(rows, 16)], H_PREV, prv)
    send(st8, st_p, S_NEXT, nxt)
    send(st8, st_n, S_PREV, prv)

    def score(start, size):
        at = pl.ds(start, size)
        h = hx[at]
        t = jnp.tanh(dot_nt(h, q_mat) * (inv_root / SOFT_CAP))
        w = jnp.exp(SOFT_CAP * t)
        ws[at] = w
        ts[at] = t
        xs[at, 0:256], xs[at, 256:512] = split(w * h.astype(F32))
        xs[at, 512:768], xs[at, 768:1024] = split(w)

    def score_own(i):
        score(pl.multiple_of(i * 256, 256), 256)

    fetched(copy_h)
    ring(score_own, 0, rows // 256)

    arrived(w32r, W_PAIR)
    w_mine, w_other = w32[...], w32r[...]
    w16 = jnp.concatenate(
        [jnp.where(first, w_mine, w_other), jnp.where(first, w_other, w_mine)], axis=0
    )
    w_half = jnp.where(first, w16[:, :512], w16[:, 512:]).astype(BF16)
    wg[c, 0, z, y] = w_half[:, :256]
    wg[c, 1, y, z] = w_half[:, 256:]

    def lines(k):
        send(wg.at[c, 0, z, y], wg.at[c, 0, z, y], A1A + k, dev_y(k))
        send(wg.at[c, 1, y, z], wg.at[c, 1, y, z], A1B + k, dev_z(k))

    ring(lines)
    noted(A1A, wg.at[c, 0, z, y])
    noted(A1B, wg.at[c, 1, y, z])
    send(g_hbm.at[:, pair_cols], gc.at[1], G_PAIR, pair)

    r128, c128 = iota((128, 128), 0), iota((128, 128), 1)
    upper = jnp.where(r128 <= c128, 1.0, 0.0).astype(BF16)
    starts = st8[...].astype(BF16)
    within = dot(starts, upper)
    counts = dot(starts, jnp.ones((128, 128), BF16))
    blocks = rows // 128
    spread = jnp.where(iota((blocks, rows), 0) == lax.div(iota((blocks, rows), 1), 128), 1.0, 0.0)
    within_t = lax.dot_general(
        within.astype(BF16), spread.astype(BF16), (((0,), (0,)), ((), ())),
        preferred_element_type=F32,
    )
    hot_rows = hot.shape[0]
    slot_col = iota((hot_rows, 128), 0).astype(F32)
    lane = iota((128, 128), 1).astype(F32)
    total = jnp.zeros((1, 128), F32)
    lead8 = None
    for k in range(blocks):
        row_id = within[k:k + 1] + total - 1.0
        row_id = jnp.where(row_id < 0.0, F32(slots), row_id)
        hot[:, 128 * k:128 * k + 128] = jnp.where(slot_col == row_id, 1.0, 0.0).astype(BF16)
        col_id = within_t[:, 128 * k:128 * k + 128] + total - 1.0
        if k == 0:
            lead8 = jnp.where(col_id[0:8] < 0.0, 1.0, 0.0).astype(F32)
        for j in range(slots // 128):
            hot_t[128 * k:128 * k + 128, 128 * j:128 * j + 128] = jnp.where(
                col_id == lane + 128.0 * j, 1.0, 0.0
            ).astype(BF16)
        total = total + counts[k:k + 1]
    lead8 = jnp.concatenate([lead8, lead8], axis=1)

    onehot = hot[:, 0:rows]
    sums = [dot(onehot, xs[0:rows, 256 * k:256 * k + 256]) for k in range(4)]
    numer, denom = sums[0] + sums[1], sums[2] + sums[3]

    arrived(hx.at[pl.ds(rows + 112, 16)], H_NEXT)
    arrived(hx.at[pl.ds(rows, 16)], H_PREV)
    arrived(st_p, S_NEXT)
    arrived(st_n, S_PREV)
    score(rows, 128)
    after = jnp.where((r128 <= c128) & (c128 < 64), 1.0, 0.0).astype(BF16)
    before = jnp.where((r128 > c128) & (c128 >= 64), 1.0, 0.0).astype(BF16)
    starts_n = jnp.where(s == n_seq - 1, 1.0, jnp.broadcast_to(st_n[0:1], (8, 128))).astype(BF16)
    starts_p = jnp.where(s == 0, 1.0, jnp.broadcast_to(st_p[7:8], (8, 128))).astype(BF16)
    count = dot(starts_n, after) + dot(starts_p, before)
    halo_slot = jnp.where(iota((8, 128), 1) < 64, total - 1.0, F32(slots))
    halo_slot = jnp.where(count == 0.0, halo_slot, -9.0)
    hot[:, rows:rows + 128] = jnp.where(slot_col == halo_slot[0:1], 1.0, 0.0).astype(BF16)

    onehot = hot[:, rows:rows + 128]
    sums = [dot(onehot, xs[rows:rows + 128, 256 * k:256 * k + 256]) for k in range(4)]
    numer, denom = numer + sums[0] + sums[1], denom + sums[2] + sums[3]
    live = denom > 0.0
    denom = jnp.where(live, denom, 1.0)
    pooled = jnp.where(live, numer / denom, 0.0)
    pf[0, a, 0] = pooled[:half].T.astype(BF16)
    pf[0, a, 1] = pooled[half:slots].T.astype(BF16)
    send(pf.at[0, a, 0], pf.at[0, a, 0], X_UP0, up)
    send(pf.at[0, a, 1], pf.at[0, a, 1], X_DN1, dn)

    def to_pair(step, index, part_half):
        send(pf.at[0, index, part_half], pf.at[1, index, part_half],
             PF_PAIR + 2 * step + part_half, pair)

    to_pair(0, a, 0)
    to_pair(0, a, 1)

    fetched(copy_g)
    pick = iota((16, slots), 1).astype(F32) == (total[0:1, 0:1] - 1.0)
    pick = jnp.where(pick & (iota((16, slots), 0) == 0), 1.0, 0.0).astype(BF16)
    gl_send[...] = dot(pick, gx[0:slots, :]).astype(BF16)
    send(gl_send, gx.at[pl.ds(slots, 16)], G_NEXT, nxt)

    def grad_block(index, column):
        value = None
        for core in range(2):
            for part_half in range(2):
                term = dot(
                    pf[core, index, part_half],
                    gc[core, half * part_half:half * part_half + half, column:column + 256],
                )
                value = term if value is None else value + term
        return value.astype(BF16)

    def pair_features(step, index):
        for part_half in range(2):
            arrived(pf.at[1, index, part_half], PF_PAIR + 2 * step + part_half)

    def grad_y(step, index):
        if step < 3:
            pair_features(step, index)
        value = grad_block(index, 0)
        for zz in range(2):
            for yy in range(RING):
                at = (zz * RING + yy) * 16
                sa[yy, 2 * index + zz] = value[at:at + 16]
        two = pl.ds(2 * index, 2)
        base = D1A + 8 * step

        def spread(k):
            send(sa.at[y_at(k), two], ra.at[k - 1, two], base + k, dev_y(k))

        ring(spread)
        noted(base, sa.at[0, two])

    def finish_y(step, index):
        two = pl.ds(2 * index, 2)
        base = D1A + 8 * step

        def wait(k):
            arrived(ra.at[k - 1, two], base + k)

        ring(wait)
        landed(base)
        value = sa[y, two].astype(F32)
        for k in range(RING - 1):
            value = value + ra[k, two].astype(F32)
        ta[two] = value.astype(BF16)
        for zz in range(2):
            k = wrap(2 * index + zz - z, RING)

            @pl.when(k > 0)
            def _():
                send(ta.at[2 * index + zz], ua.at[k - 1], D2A + k, dev_z(k))

    def grad_z(turn):
        index = lax.rem(lax.div(z, 2) + turn, 4)
        value = grad_block(index, 256)
        for zz in range(2):
            for yy in range(RING):
                at = (zz * RING + yy) * 16
                sb[2 * index + zz, yy] = value[at:at + 16]

    yv[:, 0:256], yv[:, 256:512] = split(pooled[:slots])
    yv[:, 512:768], yv[:, 768:1024] = split(denom[:slots])
    prev_pool, prev_den = pooled[slots:slots + 1], denom[slots:slots + 1]

    def lead_rows(value8, size):
        return jnp.concatenate([value8, jnp.zeros((size - 8, feats), F32)], axis=0)

    def weigh(at, extra):
        got = dot(hot_t[at], yv[...])
        pool_rows = got[:, 0:256] + got[:, 256:512]
        den_rows = got[:, 512:768] + got[:, 768:1024]
        if extra is not None:
            pool_rows = pool_rows + extra[0]
            den_rows = den_rows + extra[1]
        t = ts[at]
        share = ws[at] / den_rows
        share_s[at] = share
        diff_s[at] = hx[at].astype(F32) - pool_rows
        coef_s[at] = share * (1.0 - t * t) * (query * inv_root)

    weigh(pl.ds(0, 256), (lead_rows(lead8 * prev_pool, 256), lead_rows(lead8 * prev_den, 256)))

    def weigh_more(i):
        weigh(pl.ds(pl.multiple_of(i * 256, 256), 256), None)

    ring(weigh_more, 1, rows // 512)

    def planes(k):
        arrived(wg.at[c, 0, z, y], A1A + k)
        arrived(wg.at[c, 1, y, z], A1B + k)

    ring(planes)
    landed(A1A)
    landed(A1B)
    mine_a, mine_b = wg.at[c, 0, z], wg.at[c, 1, y]
    for k in (2, 6):
        send(mine_a, mine_a, A2A + k, dev_z(k))
        send(mine_b, mine_b, A2B + k, dev_y(k))
    send(mine_a, mine_a, WPA, pair)
    send(mine_b, mine_b, WPB, pair)

    def whole(kind, k):
        return wg.at[c, kind, z_at(-k) if kind == 0 else y_at(-k)]

    def piece(kind, k, lower_half):
        return wg.at[c, kind, z_at(-k) if kind == 0 else y_at(-k), pl.ds(0 if lower_half else 4, 4)]

    send(pf.at[0, a, 1], pf.at[0, a, 1], X_UP1, up)
    send(pf.at[0, a, 0], pf.at[0, a, 0], X_DN0, dn)

    kinds = ((0, A2A, dev_z, WPA), (1, A2B, dev_y, WPB))

    arrived(pf.at[0, a_dn, 0], X_UP0)
    send(pf.at[0, a_dn, 0], pf.at[0, a_dn, 0], X_UPF, up)
    arrived(pf.at[0, a_up, 1], X_DN1)
    send(pf.at[0, a_up, 1], pf.at[0, a_up, 1], X_DNF, dn)
    to_pair(1, a_dn, 0)
    to_pair(2, a_up, 1)
    for k in (1, 7):
        send(mine_a, mine_a, A2A + k, dev_z(k))
        send(mine_b, mine_b, A2B + k, dev_y(k))
    ring(weigh_more, rows // 512, rows // 256)
    for kind, base, dev, _ in kinds:
        arrived(whole(kind, 2), base + 2)
        send(whole(kind, 2), whole(kind, 2), base + 3, dev(1))
        send(piece(kind, 2, True), piece(kind, 2, True), base + 4, dev(2))
        arrived(whole(kind, 6), base + 6)
        send(whole(kind, 6), whole(kind, 6), base + 5, dev(-1))
        send(piece(kind, 6, False), piece(kind, 6, False), base, dev(-2))
    fetched(copy_gc)
    arrived(gc.at[1], G_PAIR)
    grad_y(0, a)

    arrived(pf.at[0, a_dn, 1], X_UP1)
    to_pair(1, a_dn, 1)
    arrived(pf.at[0, a_up, 0], X_DN0)
    to_pair(2, a_up, 0)
    grad_y(1, a_dn)
    grad_y(2, a_up)
    arrived(pf.at[0, a_far, 0], X_UPF)
    to_pair(3, a_far, 0)
    arrived(pf.at[0, a_far, 1], X_DNF)
    to_pair(3, a_far, 1)
    for kind, base, dev, pair_base in kinds:
        for k in (2, 6, 1, 7):
            if k in (1, 7):
                arrived(whole(kind, k), base + k)
            send(whole(kind, k), whole(kind, k), pair_base + k, pair)
    pair_features(3, a_far)
    for turn in range(4):
        grad_z(turn)
    near, last = pl.ds(0, RING // 2), pl.ds(RING // 2, RING // 2)
    send(sb.at[z_at(4), near], up4, D1B + 4, dev_z(2))
    send(sb.at[z_at(4), last], dn4, D1B, dev_z(-2))
    send(sb.at[z_at(3)], up3, D1B + 3, dev_z(1))
    send(sb.at[z_at(5)], dn3, D1B + 5, dev_z(-1))
    grad_y(3, a_far)
    for kind, base, dev, pair_base in kinds:
        for k in (3, 5, 4):
            if k == 4:
                arrived(piece(kind, k, True), base + 4)
                arrived(piece(kind, k, False), base)
            else:
                arrived(whole(kind, k), base + k)
            send(whole(kind, k), whole(kind, k), pair_base + k, pair)

    send(sb.at[z_at(1)], rb.at[0], D1B + 1, dev_z(1))
    send(sb.at[z_at(7)], rb.at[3], D1B + 7, dev_z(-1))

    def from_pair(k):
        arrived(wg.at[1 - c, 0, z_at(-k)], WPA + k)
        arrived(wg.at[1 - c, 1, y_at(-k)], WPB + k)

    ring(from_pair, 0)
    landed(WPA, 0)
    landed(WPB, 0)

    def natural(zz):
        at = pl.ds(pl.multiple_of(zz * 128, 128), 128)
        for core in range(2):
            wq[2 * core, at] = wg[core, 0, zz].reshape(128, 256)
            wq[2 * core + 1, at] = wg[core, 1, :, zz].reshape(128, 256)

    ring(natural, 0)
    arrived(gx.at[pl.ds(slots, 16)], G_NEXT)

    def partial_of(index):
        at = pl.ds(pl.multiple_of(index * 256, 256), 256)
        value = dot_nt(gx[:, 0:256], wq[0, at])
        for q in range(1, 4):
            value = value + dot_nt(gx[:, 256 * q:256 * q + 256], wq[q, at])
        return value.astype(BF16)

    upper_rows = pl.ds(half, half + 16)
    lower_rows = pl.ds(0, half)
    part[0] = partial_of(a_far)
    send(part.at[0, lower_rows], cr_up, C_UPR, up)
    send(part.at[0, upper_rows], cr_dn, C_DNR, dn)
    part[1] = partial_of(a_up)
    send(part.at[1, upper_rows], c_up.at[upper_rows], C_UPD, up)
    part[2] = partial_of(a_dn)
    send(part.at[2, lower_rows], c_dn.at[lower_rows], C_DND, dn)

    arrived(up4, D1B + 4)
    arrived(up3, D1B + 3)
    value = sb[z_at(2)].astype(F32) + up3[...].astype(F32)
    up_sum[near] = (value[:RING // 2] + up4[...].astype(F32)).astype(BF16)
    up_sum[last] = value[RING // 2:].astype(BF16)
    send(up_sum, rb.at[1], D1B + 2, dev_z(2))
    arrived(dn4, D1B)
    arrived(dn3, D1B + 5)
    value = sb[z_at(6)].astype(F32) + dn3[...].astype(F32)
    dn_sum[near] = value[:RING // 2].astype(BF16)
    dn_sum[last] = (value[RING // 2:] + dn4[...].astype(F32)).astype(BF16)
    send(dn_sum, rb.at[2], D1B + 6, dev_z(-2))

    arrived(cr_up, C_UPR)
    cs_up[...] = (cr_up[...].astype(F32) + part[1, 0:half].astype(F32)).astype(BF16)
    send(cs_up, c_up.at[lower_rows], C_UPS, up)
    arrived(cr_dn, C_DNR)
    cs_dn[...] = (cr_dn[...].astype(F32) + part[2, half:half + half + 16].astype(F32)).astype(BF16)
    send(cs_dn, c_dn.at[upper_rows], C_DNS, dn)
    part[3] = partial_of(a)
    finish_y(0, a)
    finish_y(1, a_dn)
    finish_y(2, a_up)

    def latent(part_half):
        at = pl.ds(pl.multiple_of(part_half * half, half), half)
        values = [None] * 4
        for index in range(4):
            left = pf[0, index, part_half].astype(F32).T.astype(BF16)
            for q in range(4):
                term = dot(left, wq[q, 256 * index:256 * index + 256])
                values[q] = term if values[q] is None else values[q] + term
        for q in range(4):
            lat_ref[at, 256 * q:256 * q + 256] = values[q].astype(BF16)


    finish_y(3, a_far)
    noted(D2A, ta.at[0])

    sum_b = sb[z].astype(F32)
    for i, k in enumerate((1, 2, 6, 7)):
        arrived(rb.at[i], D1B + k)
        sum_b = sum_b + rb[i].astype(F32)
    tb[...] = sum_b.astype(BF16)

    def reduce_more(k):
        send(tb.at[y_at(k)], ub.at[k - 1], D2B + k, dev_y(k))

    ring(reduce_more)
    noted(D2B, tb.at[0])

    ring(latent, 0, 2)
    fetch(lat_ref, lat_hbm)

    arrived(c_up.at[upper_rows], C_UPD)
    arrived(c_dn.at[lower_rows], C_DND)
    arrived(c_up.at[lower_rows], C_UPS)
    arrived(c_dn.at[upper_rows], C_DNS)
    grad = part[3].astype(F32) + c_up[...].astype(F32) + c_dn[...].astype(F32)
    zv[:, 0:256], zv[:, 256:512] = split(grad[:slots])
    prev_grad = grad[slots:slots + 1]

    def byte_grad(at, extra):
        got = dot(hot_t[at], zv[...])
        grad_rows = got[:, 0:256] + got[:, 256:512]
        if extra is not None:
            grad_rows = grad_rows + extra
        high, low = split(grad_rows * diff_s[at])
        inner = dot(high, head_ones) + dot(low, head_ones)
        gb_ref[at] = (share_s[at] * grad_rows + coef_s[at] * inner).astype(BF16)

    byte_grad(pl.ds(0, 256), lead_rows(lead8 * prev_grad, 256))

    def byte_more(i):
        byte_grad(pl.ds(pl.multiple_of(i * 256, 256), 256), None)

    ring(byte_more, 1, rows // 256)
    fetch(gb_ref, gb_hbm)

    def reduced_more(k):
        arrived(ua.at[k - 1], D2A + k)
        arrived(ub.at[k - 1], D2B + k)

    ring(reduced_more)
    landed(D2A)
    landed(D2B)
    sum_a, sum_b = ta[z].astype(F32), tb[y].astype(F32)
    for k in range(RING - 1):
        sum_a = sum_a + ua[k].astype(F32)
        sum_b = sum_b + ub[k].astype(F32)
    grad_scale = 1.0 / math.sqrt(n_seq * slots)
    both = jnp.concatenate([sum_a, sum_b], axis=1) * grad_scale
    fin_s[...] = jnp.where(first, both[8:16], both[0:8])
    send(fin_s, fin_r, F_PAIR, pair)
    mine = jnp.where(first, both[0:8], both[8:16])
    arrived(fin_r, F_PAIR)
    other = fin_r[...]
    gw_ref[:, 0:512] = jnp.where(first, mine, other)
    gw_ref[:, 512:1024] = jnp.where(first, other, mine)
    fetch(gw_ref, gw_hbm)

    drain()


def place(lat_in, gw_in, gb_in, lat_out, gw_out, gb_out, lat, gw, gb, sem_in, sem_out):
    parts = [(lat_in, lat, lat_out, 64 * i, 64) for i in range(lat.shape[0] // 64)]
    parts += [(gb_in, gb, gb_out, 256 * i, 256) for i in range(gb.shape[0] // 256)]
    parts.append((gw_in, gw, gw_out, 0, 8))
    reads, writes = [], []
    for i, (src, mid, dst, start, size) in enumerate(parts):
        at = pl.ds(start, size)
        reads.append(pltpu.make_async_copy(src.at[at], mid.at[at], sem_in.at[i]))
        writes.append(pltpu.make_async_copy(mid.at[at], dst.at[at], sem_out.at[i]))
    for copy in reads:
        copy.start()
    for read, write in zip(reads, writes):
        read.wait()
        write.start()
    for copy in writes:
        copy.wait()


def shards(byte_hidden, patch_start, pool_query, in_weight, latent_grad):
    rows, feats = byte_hidden.shape
    slots, width = latent_grad.shape
    half = slots // 2
    hbm = pl.BlockSpec(memory_space=pltpu.HBM)

    def buf(*shape, dtype=BF16):
        return pltpu.VMEM(shape, dtype)

    scratch = [
        buf(slots, width), buf(8, width, dtype=F32), buf(rows, feats),
        buf(rows + 128, feats), buf(rows // 128, 128, dtype=jnp.int32), buf(2, 128),
        buf(8, 128, dtype=F32), buf(8, 128, dtype=F32), buf(8, 128, dtype=F32),
        buf(8, width), buf(8, width, dtype=F32), buf(8, width, dtype=F32),
        buf(2, 2, RING, RING, 16, 256), buf(4, 1024, 256),
        buf(slots + 16, width), buf(16, width), buf(2, slots, 512),
        buf(slots + 16, rows + 128), buf(rows, slots),
        buf(rows + 128, 1024), buf(rows + 128, feats, dtype=F32), buf(rows + 128, feats, dtype=F32),
        buf(slots, 1024),
        buf(rows, feats, dtype=F32), buf(rows, feats, dtype=F32), buf(rows, feats, dtype=F32),
        buf(2, 4, 2, half, 256), buf(4, slots + 16, 256),
        buf(half, 256), buf(half + 16, 256), buf(half, 256), buf(half + 16, 256),
        buf(slots + 16, 256), buf(slots + 16, 256), buf(slots, 512),
        buf(RING, RING, 16, 256), buf(RING, RING, 16, 256),
        buf(RING - 1, RING, 16, 256), buf(4, RING, 16, 256),
        buf(RING, 16, 256), buf(RING // 2, 16, 256), buf(RING, 16, 256), buf(RING // 2, 16, 256),
        buf(RING, 16, 256), buf(RING, 16, 256),
        buf(RING, 16, 256), buf(RING, 16, 256),
        buf(RING - 1, 16, 256), buf(RING - 1, 16, 256),
        buf(8, 512, dtype=F32), buf(8, 512, dtype=F32),
        pltpu.SemaphoreType.DMA((9,)),
        pltpu.SemaphoreType.DMA((SLOTS_SEM,)),
        pltpu.SemaphoreType.DMA((SLOTS_SEM,)),
    ]
    shapes = (
        jax.ShapeDtypeStruct((slots, width), BF16),
        jax.ShapeDtypeStruct((8, width), F32),
        jax.ShapeDtypeStruct((rows, feats), BF16),
    )
    outs = pl.pallas_call(
        kernel,
        out_shape=shapes,
        in_specs=[hbm] * 5,
        out_specs=(hbm, hbm, hbm),
        scratch_shapes=scratch,
        compiler_params=pltpu.CompilerParams(
            collective_id=0, has_side_effects=True, vmem_limit_bytes=VMEM_LIMIT
        ),
        name="patch_pool",
    )(
        byte_hidden, patch_start.reshape(rows // 128, 128), pool_query.reshape(2, feats // 2),
        in_weight, latent_grad,
    )
    return pl.pallas_call(
        place,
        out_shape=shapes,
        in_specs=[hbm] * 3,
        out_specs=(hbm, hbm, hbm),
        scratch_shapes=[
            buf(slots, width), buf(8, width, dtype=F32), buf(rows, feats),
            pltpu.SemaphoreType.DMA((13,)), pltpu.SemaphoreType.DMA((13,)),
        ],
        compiler_params=pltpu.CompilerParams(vmem_limit_bytes=VMEM_LIMIT),
        name="place",
    )(*outs)


def solution(mesh):
    in_specs = (P("seq", "mp"), P("seq"), P("mp"), P("seq", "mp"), P("seq", "mp"))
    out_specs = (P("seq", "mp"), P("seq", "mp"), P("seq", "mp"))
    return jax.shard_map(shards, mesh=mesh, in_specs=in_specs, out_specs=out_specs, check_vma=False)
```

```python
import math

import jax
import jax.numpy as jnp
from jax import lax
from jax.experimental import pallas as pl
from jax.experimental.pallas import tpu as pltpu
from jax.sharding import PartitionSpec as P

HEAD_DIM = 64
SOFT_CAP = 20.0
RING = 8
F32 = jnp.float32
BF16 = jnp.bfloat16
MESH = pl.DeviceIdType.MESH
VMEM_LIMIT = 60 * 1024 * 1024

W_PAIR, H_NEXT, H_PREV, S_NEXT, S_PREV, G_NEXT, G_PAIR, F_PAIR = range(8)
X_UP0, X_UP1, X_UPF, X_DN1, X_DN0, X_DNF = range(8, 14)
C_UPR, C_UPD, C_UPS, C_DNR, C_DND, C_DNS = range(14, 20)
PF_PAIR = 20
A1A, A1B, A2A, A2B = 28, 36, 44, 52
WPA, WPB = 60, 68
D1A = 76
D1B, D2A, D2B = 108, 116, 124
SLOTS_SEM = 132


def dot(a, b):
    return jnp.dot(a, b, preferred_element_type=F32)


def dot_nt(a, b):
    return lax.dot_general(a, b, (((1,), (1,)), ((), ())), preferred_element_type=F32)


def split(value):
    high = value.astype(BF16)
    return high, (value - high.astype(F32)).astype(BF16)


def iota(shape, dim):
    return lax.broadcasted_iota(jnp.int32, shape, dim)


def kernel(
    h_hbm, st_hbm, q_hbm, w_hbm, g_hbm,
    lat_hbm, gw_hbm, gb_hbm,
    lat_ref, gw_ref, gb_ref, hx, st_own, q_own, st8, st_n, st_p, w_own, w32, w32r, wg, wq, gx, gl_send, gc,
    hot, hot_t, xs, ws, ts, yv, share_s, diff_s, coef_s,
    pf, part, cr_up, cr_dn, cs_up, cs_dn, c_up, c_dn, zv,
    sa, sb, ra, rb, up3, up4, dn3, dn4, up_sum, dn_sum, ta, tb, ua, ub, fin_s, fin_r,
    loc, ss, rs,
):
    s = lax.axis_index("seq")
    a = lax.axis_index("mp")
    n_seq, n_mp = lax.axis_size("seq"), lax.axis_size("mp")
    slots = g_hbm.shape[0]
    rows, feats = h_hbm.shape
    half = slots // 2
    c = lax.rem(s, 2)
    y = lax.rem(lax.div(s, 2), RING)
    z = lax.div(s, 2 * RING)
    first = c == 0

    def wrap(value, size):
        return lax.rem(value + size, size)

    pair = (s + 1 - 2 * c, a)
    nxt = (wrap(s + 1, n_seq), a)
    prv = (wrap(s - 1, n_seq), a)
    a_up, a_dn, a_far = wrap(a + 1, n_mp), wrap(a - 1, n_mp), wrap(a + 2, n_mp)
    up, dn = (s, a_up), (s, a_dn)

    def y_at(k):
        return wrap(y + k, RING)

    def z_at(k):
        return wrap(z + k, RING)

    def dev_y(k):
        return ((z * RING + y_at(k)) * 2 + c, a)

    def dev_z(k):
        return ((z_at(k) * RING + y) * 2 + c, a)

    def remote(src, dst, slot, device):
        return pltpu.make_async_remote_copy(
            src_ref=src, dst_ref=dst, send_sem=ss.at[slot], recv_sem=rs.at[slot],
            device_id=device, device_id_type=MESH,
        )

    flying, landing = {}, {}

    def note(slot, ref):
        flying[slot] = ref
        landing[slot] = ref

    def send(src, dst, slot, device):
        remote(src, dst, slot, device).start()
        if isinstance(slot, int):
            note(slot, src)

    def arrived(dst, slot):
        remote(dst, dst, slot, pair).wait_recv()
        if isinstance(slot, int):
            landing.pop(slot)

    def ring(body, low=1, high=RING):
        def step(k, carry):
            body(k)
            return carry

        lax.fori_loop(low, high, step, 0)

    def farthest_first(body):
        def step(i):
            turn = lax.div(i, 2)
            body(RING // 2 + jnp.where(lax.rem(i, 2) == 0, turn, -turn))

        ring(step)

    def noted(base, ref, low=1, high=RING):
        for k in range(low, high):
            note(base + k, ref)

    def landed(base, low=1, high=RING):
        for k in range(low, high):
            landing.pop(base + k)

    copies = []

    def fetch(src, dst):
        copy = pltpu.make_async_copy(src, dst, loc.at[len(copies)])
        copy.start()
        copies.append(copy)
        return len(copies) - 1

    def fetched(index):
        copies[index].wait()
        copies[index] = None

    def drain():
        for copy in copies:
            if copy is not None:
                copy.wait()
        for slot, ref in landing.items():
            remote(ref, ref, slot, pair).wait_recv()
        for slot, ref in flying.items():
            remote(ref, ref, slot, pair).wait_send()

    barrier = pltpu.get_barrier_semaphore()

    def greet(device):
        pl.semaphore_signal(barrier, inc=1, device_id=device, device_id_type=MESH)

    for device in (pair, nxt, prv, up, dn):
        greet(device)

    def greet_ring(k):
        greet(dev_y(k))
        greet(dev_z(k))

    farthest_first(greet_ring)

    own_cols = pl.ds(pl.multiple_of(c * 512, 512), 512)
    pair_cols = pl.ds(pl.multiple_of((1 - c) * 512, 512), 512)
    copy_w = fetch(w_hbm, w_own)
    copy_st = fetch(st_hbm, st_own)
    copy_q = fetch(q_hbm, q_own)
    copy_h = fetch(h_hbm, hx.at[pl.ds(0, rows)])
    copy_g = fetch(g_hbm, gx.at[pl.ds(0, slots)])
    copy_gc = fetch(g_hbm.at[:, own_cols], gc.at[0])
    hx[rows + 16:rows + 112, :] = jnp.zeros((96, feats), BF16)
    same = lax.div(iota((feats, feats), 0), HEAD_DIM) == lax.div(iota((feats, feats), 1), HEAD_DIM)
    fetched(copy_q)
    query = q_own[...].astype(F32)
    query = jnp.concatenate([query[0:1], query[1:2]], axis=1)
    q_mat = jnp.where(same, jnp.broadcast_to(query, (feats, feats)), 0.0).astype(BF16)
    head_ones = jnp.where(same, 1.0, 0.0).astype(BF16)
    inv_root = 1.0 / math.sqrt(HEAD_DIM)
    fetched(copy_w)
    w32[...] = w_own[...].astype(F32)
    fetched(copy_st)
    st8[...] = st_own[...].astype(F32)

    pl.semaphore_wait(barrier, 5 + 2 * (RING - 1))

    send(w32, w32r, W_PAIR, pair)
    send(h_hbm.at[pl.ds(rows - 16, 16)], hx.at[pl.ds(rows + 112, 16)], H_NEXT, nxt)
    send(h_hbm.at[pl.ds(0, 16)], hx.at[pl.ds(rows, 16)], H_PREV, prv)
    send(st8, st_p, S_NEXT, nxt)
    send(st8, st_n, S_PREV, prv)

    def score(start, size):
        at = pl.ds(start, size)
        h = hx[at]
        t = jnp.tanh(dot_nt(h, q_mat) * (inv_root / SOFT_CAP))
        w = jnp.exp(SOFT_CAP * t)
        ws[at] = w
        ts[at] = t
        xs[at, 0:256], xs[at, 256:512] = split(w * h.astype(F32))
        xs[at, 512:768], xs[at, 768:1024] = split(w)

    def score_own(i):
        score(pl.multiple_of(i * 256, 256), 256)

    fetched(copy_h)
    ring(score_own, 0, rows // 256)

    arrived(w32r, W_PAIR)
    w_mine, w_other = w32[...], w32r[...]
    w16 = jnp.concatenate(
        [jnp.where(first, w_mine, w_other), jnp.where(first, w_other, w_mine)], axis=0
    )
    w_half = jnp.where(first, w16[:, :512], w16[:, 512:]).astype(BF16)
    wg[c, 0, z, y] = w_half[:, :256]
    wg[c, 1, y, z] = w_half[:, 256:]

    def lines(k):
        send(wg.at[c, 0, z, y], wg.at[c, 0, z, y], A1A + k, dev_y(k))
        send(wg.at[c, 1, y, z], wg.at[c, 1, y, z], A1B + k, dev_z(k))

    farthest_first(lines)
    noted(A1A, wg.at[c, 0, z, y])
    noted(A1B, wg.at[c, 1, y, z])
    send(g_hbm.at[:, pair_cols], gc.at[1], G_PAIR, pair)

    r128, c128 = iota((128, 128), 0), iota((128, 128), 1)
    upper = jnp.where(r128 <= c128, 1.0, 0.0).astype(BF16)
    starts = st8[...].astype(BF16)
    within = dot(starts, upper)
    counts = dot(starts, jnp.ones((128, 128), BF16))
    blocks = rows // 128
    spread = jnp.where(iota((blocks, rows), 0) == lax.div(iota((blocks, rows), 1), 128), 1.0, 0.0)
    within_t = lax.dot_general(
        within.astype(BF16), spread.astype(BF16), (((0,), (0,)), ((), ())),
        preferred_element_type=F32,
    )
    hot_rows = hot.shape[0]
    slot_col = iota((hot_rows, 128), 0).astype(F32)
    lane = iota((128, 128), 1).astype(F32)
    total = jnp.zeros((1, 128), F32)
    lead8 = None
    for k in range(blocks):
        row_id = within[k:k + 1] + total - 1.0
        row_id = jnp.where(row_id < 0.0, F32(slots), row_id)
        hot[:, 128 * k:128 * k + 128] = jnp.where(slot_col == row_id, 1.0, 0.0).astype(BF16)
        col_id = within_t[:, 128 * k:128 * k + 128] + total - 1.0
        if k == 0:
            lead8 = jnp.where(col_id[0:8] < 0.0, 1.0, 0.0).astype(F32)
        for j in range(slots // 128):
            hot_t[128 * k:128 * k + 128, 128 * j:128 * j + 128] = jnp.where(
                col_id == lane + 128.0 * j, 1.0, 0.0
            ).astype(BF16)
        total = total + counts[k:k + 1]
    lead8 = jnp.concatenate([lead8, lead8], axis=1)

    onehot = hot[:, 0:rows]
    sums = [dot(onehot, xs[0:rows, 256 * k:256 * k + 256]) for k in range(4)]
    numer, denom = sums[0] + sums[1], sums[2] + sums[3]

    arrived(hx.at[pl.ds(rows + 112, 16)], H_NEXT)
    arrived(hx.at[pl.ds(rows, 16)], H_PREV)
    arrived(st_p, S_NEXT)
    arrived(st_n, S_PREV)
    score(rows, 128)
    after = jnp.where((r128 <= c128) & (c128 < 64), 1.0, 0.0).astype(BF16)
    before = jnp.where((r128 > c128) & (c128 >= 64), 1.0, 0.0).astype(BF16)
    starts_n = jnp.where(s == n_seq - 1, 1.0, jnp.broadcast_to(st_n[0:1], (8, 128))).astype(BF16)
    starts_p = jnp.where(s == 0, 1.0, jnp.broadcast_to(st_p[7:8], (8, 128))).astype(BF16)
    count = dot(starts_n, after) + dot(starts_p, before)
    halo_slot = jnp.where(iota((8, 128), 1) < 64, total - 1.0, F32(slots))
    halo_slot = jnp.where(count == 0.0, halo_slot, -9.0)
    hot[:, rows:rows + 128] = jnp.where(slot_col == halo_slot[0:1], 1.0, 0.0).astype(BF16)

    onehot = hot[:, rows:rows + 128]
    sums = [dot(onehot, xs[rows:rows + 128, 256 * k:256 * k + 256]) for k in range(4)]
    numer, denom = numer + sums[0] + sums[1], denom + sums[2] + sums[3]
    live = denom > 0.0
    denom = jnp.where(live, denom, 1.0)
    pooled = jnp.where(live, numer / denom, 0.0)
    pf[0, a, 0] = pooled[:half].T.astype(BF16)
    pf[0, a, 1] = pooled[half:slots].T.astype(BF16)
    send(pf.at[0, a, 0], pf.at[0, a, 0], X_UP0, up)
    send(pf.at[0, a, 1], pf.at[0, a, 1], X_DN1, dn)

    def to_pair(step, index, part_half):
        send(pf.at[0, index, part_half], pf.at[1, index, part_half],
             PF_PAIR + 2 * step + part_half, pair)

    to_pair(0, a, 0)
    to_pair(0, a, 1)

    fetched(copy_g)
    pick = iota((16, slots), 1).astype(F32) == (total[0:1, 0:1] - 1.0)
    pick = jnp.where(pick & (iota((16, slots), 0) == 0), 1.0, 0.0).astype(BF16)
    gl_send[...] = dot(pick, gx[0:slots, :]).astype(BF16)
    send(gl_send, gx.at[pl.ds(slots, 16)], G_NEXT, nxt)

    def grad_block(index, column):
        value = None
        for core in range(2):
            for part_half in range(2):
                term = dot(
                    pf[core, index, part_half],
                    gc[core, half * part_half:half * part_half + half, column:column + 256],
                )
                value = term if value is None else value + term
        return value.astype(BF16)

    def pair_features(step, index):
        for part_half in range(2):
            arrived(pf.at[1, index, part_half], PF_PAIR + 2 * step + part_half)

    def grad_y(step, index):
        if step < 3:
            pair_features(step, index)
        value = grad_block(index, 0)
        for zz in range(2):
            for yy in range(RING):
                at = (zz * RING + yy) * 16
                sa[yy, 2 * index + zz] = value[at:at + 16]
        two = pl.ds(2 * index, 2)
        base = D1A + 8 * step

        def spread(k):
            send(sa.at[y_at(k), two], ra.at[k - 1, two], base + k, dev_y(k))

        farthest_first(spread)
        noted(base, sa.at[0, two])

    def finish_y(step, index):
        two = pl.ds(2 * index, 2)
        base = D1A + 8 * step

        def wait(k):
            arrived(ra.at[k - 1, two], base + k)

        ring(wait)
        landed(base)
        value = sa[y, two].astype(F32)
        for k in range(RING - 1):
            value = value + ra[k, two].astype(F32)
        ta[two] = value.astype(BF16)
        for zz in range(2):
            k = wrap(2 * index + zz - z, RING)

            @pl.when(k > 0)
            def _():
                send(ta.at[2 * index + zz], ua.at[k - 1], D2A + k, dev_z(k))

    def grad_z(turn):
        index = lax.rem(lax.div(z, 2) + turn, 4)
        value = grad_block(index, 256)
        for zz in range(2):
            for yy in range(RING):
                at = (zz * RING + yy) * 16
                sb[2 * index + zz, yy] = value[at:at + 16]

    yv[:, 0:256], yv[:, 256:512] = split(pooled[:slots])
    yv[:, 512:768], yv[:, 768:1024] = split(denom[:slots])
    prev_pool, prev_den = pooled[slots:slots + 1], denom[slots:slots + 1]

    def lead_rows(value8, size):
        return jnp.concatenate([value8, jnp.zeros((size - 8, feats), F32)], axis=0)

    def weigh(at, extra):
        got = dot(hot_t[at], yv[...])
        pool_rows = got[:, 0:256] + got[:, 256:512]
        den_rows = got[:, 512:768] + got[:, 768:1024]
        if extra is not None:
            pool_rows = pool_rows + extra[0]
            den_rows = den_rows + extra[1]
        t = ts[at]
        share = ws[at] / den_rows
        share_s[at] = share
        diff_s[at] = hx[at].astype(F32) - pool_rows
        coef_s[at] = share * (1.0 - t * t) * (query * inv_root)

    weigh(pl.ds(0, 256), (lead_rows(lead8 * prev_pool, 256), lead_rows(lead8 * prev_den, 256)))

    def weigh_more(i):
        weigh(pl.ds(pl.multiple_of(i * 256, 256), 256), None)

    ring(weigh_more, 1, rows // 512)

    def planes(k):
        arrived(wg.at[c, 0, z, y], A1A + k)
        arrived(wg.at[c, 1, y, z], A1B + k)

    ring(planes)
    landed(A1A)
    landed(A1B)
    mine_a, mine_b = wg.at[c, 0, z], wg.at[c, 1, y]
    for k in (2, 6):
        send(mine_a, mine_a, A2A + k, dev_z(k))
        send(mine_b, mine_b, A2B + k, dev_y(k))
    send(mine_a, mine_a, WPA, pair)
    send(mine_b, mine_b, WPB, pair)

    def whole(kind, k):
        return wg.at[c, kind, z_at(-k) if kind == 0 else y_at(-k)]

    def piece(kind, k, lower_half):
        return wg.at[c, kind, z_at(-k) if kind == 0 else y_at(-k), pl.ds(0 if lower_half else 4, 4)]

    send(pf.at[0, a, 1], pf.at[0, a, 1], X_UP1, up)
    send(pf.at[0, a, 0], pf.at[0, a, 0], X_DN0, dn)

    kinds = ((0, A2A, dev_z, WPA), (1, A2B, dev_y, WPB))

    arrived(pf.at[0, a_dn, 0], X_UP0)
    send(pf.at[0, a_dn, 0], pf.at[0, a_dn, 0], X_UPF, up)
    arrived(pf.at[0, a_up, 1], X_DN1)
    send(pf.at[0, a_up, 1], pf.at[0, a_up, 1], X_DNF, dn)
    to_pair(1, a_dn, 0)
    to_pair(2, a_up, 1)
    for k in (1, 7):
        send(mine_a, mine_a, A2A + k, dev_z(k))
        send(mine_b, mine_b, A2B + k, dev_y(k))
    ring(weigh_more, rows // 512, rows // 256)
    for kind, base, dev, _ in kinds:
        arrived(whole(kind, 2), base + 2)
        send(whole(kind, 2), whole(kind, 2), base + 3, dev(1))
        send(piece(kind, 2, True), piece(kind, 2, True), base + 4, dev(2))
        arrived(whole(kind, 6), base + 6)
        send(whole(kind, 6), whole(kind, 6), base + 5, dev(-1))
        send(piece(kind, 6, False), piece(kind, 6, False), base, dev(-2))
    fetched(copy_gc)
    arrived(gc.at[1], G_PAIR)
    grad_y(0, a)

    arrived(pf.at[0, a_dn, 1], X_UP1)
    to_pair(1, a_dn, 1)
    arrived(pf.at[0, a_up, 0], X_DN0)
    to_pair(2, a_up, 0)
    grad_y(1, a_dn)
    grad_y(2, a_up)
    arrived(pf.at[0, a_far, 0], X_UPF)
    to_pair(3, a_far, 0)
    arrived(pf.at[0, a_far, 1], X_DNF)
    to_pair(3, a_far, 1)
    for kind, base, dev, pair_base in kinds:
        for k in (2, 6, 1, 7):
            if k in (1, 7):
                arrived(whole(kind, k), base + k)
            send(whole(kind, k), whole(kind, k), pair_base + k, pair)
    pair_features(3, a_far)
    for turn in range(4):
        grad_z(turn)
    near, last = pl.ds(0, RING // 2), pl.ds(RING // 2, RING // 2)
    send(sb.at[z_at(4), near], up4, D1B + 4, dev_z(2))
    send(sb.at[z_at(4), last], dn4, D1B, dev_z(-2))
    send(sb.at[z_at(3)], up3, D1B + 3, dev_z(1))
    send(sb.at[z_at(5)], dn3, D1B + 5, dev_z(-1))
    grad_y(3, a_far)
    for kind, base, dev, pair_base in kinds:
        for k in (3, 5, 4):
            if k == 4:
                arrived(piece(kind, k, True), base + 4)
                arrived(piece(kind, k, False), base)
            else:
                arrived(whole(kind, k), base + k)
            send(whole(kind, k), whole(kind, k), pair_base + k, pair)

    send(sb.at[z_at(1)], rb.at[0], D1B + 1, dev_z(1))
    send(sb.at[z_at(7)], rb.at[3], D1B + 7, dev_z(-1))

    def from_pair(k):
        arrived(wg.at[1 - c, 0, z_at(-k)], WPA + k)
        arrived(wg.at[1 - c, 1, y_at(-k)], WPB + k)

    ring(from_pair, 0)
    landed(WPA, 0)
    landed(WPB, 0)

    def natural(zz):
        at = pl.ds(pl.multiple_of(zz * 128, 128), 128)
        for core in range(2):
            wq[2 * core, at] = wg[core, 0, zz].reshape(128, 256)
            wq[2 * core + 1, at] = wg[core, 1, :, zz].reshape(128, 256)

    ring(natural, 0)
    arrived(gx.at[pl.ds(slots, 16)], G_NEXT)

    def partial_of(index):
        at = pl.ds(pl.multiple_of(index * 256, 256), 256)
        value = dot_nt(gx[:, 0:256], wq[0, at])
        for q in range(1, 4):
            value = value + dot_nt(gx[:, 256 * q:256 * q + 256], wq[q, at])
        return value.astype(BF16)

    upper_rows = pl.ds(half, half + 16)
    lower_rows = pl.ds(0, half)
    part[0] = partial_of(a_far)
    send(part.at[0, lower_rows], cr_up, C_UPR, up)
    send(part.at[0, upper_rows], cr_dn, C_DNR, dn)
    part[1] = partial_of(a_up)
    send(part.at[1, upper_rows], c_up.at[upper_rows], C_UPD, up)
    part[2] = partial_of(a_dn)
    send(part.at[2, lower_rows], c_dn.at[lower_rows], C_DND, dn)

    arrived(up4, D1B + 4)
    arrived(up3, D1B + 3)
    value = sb[z_at(2)].astype(F32) + up3[...].astype(F32)
    up_sum[near] = (value[:RING // 2] + up4[...].astype(F32)).astype(BF16)
    up_sum[last] = value[RING // 2:].astype(BF16)
    send(up_sum, rb.at[1], D1B + 2, dev_z(2))
    arrived(dn4, D1B)
    arrived(dn3, D1B + 5)
    value = sb[z_at(6)].astype(F32) + dn3[...].astype(F32)
    dn_sum[near] = value[:RING // 2].astype(BF16)
    dn_sum[last] = (value[RING // 2:] + dn4[...].astype(F32)).astype(BF16)
    send(dn_sum, rb.at[2], D1B + 6, dev_z(-2))

    arrived(cr_up, C_UPR)
    cs_up[...] = (cr_up[...].astype(F32) + part[1, 0:half].astype(F32)).astype(BF16)
    send(cs_up, c_up.at[lower_rows], C_UPS, up)
    arrived(cr_dn, C_DNR)
    cs_dn[...] = (cr_dn[...].astype(F32) + part[2, half:half + half + 16].astype(F32)).astype(BF16)
    send(cs_dn, c_dn.at[upper_rows], C_DNS, dn)
    part[3] = partial_of(a)
    finish_y(0, a)
    finish_y(1, a_dn)
    finish_y(2, a_up)

    def latent(part_half):
        at = pl.ds(pl.multiple_of(part_half * half, half), half)
        values = [None] * 4
        for index in range(4):
            left = pf[0, index, part_half].astype(F32).T.astype(BF16)
            for q in range(4):
                term = dot(left, wq[q, 256 * index:256 * index + 256])
                values[q] = term if values[q] is None else values[q] + term
        for q in range(4):
            lat_ref[at, 256 * q:256 * q + 256] = values[q].astype(BF16)


    finish_y(3, a_far)
    noted(D2A, ta.at[0])

    sum_b = sb[z].astype(F32)
    for i, k in enumerate((1, 2, 6, 7)):
        arrived(rb.at[i], D1B + k)
        sum_b = sum_b + rb[i].astype(F32)
    tb[...] = sum_b.astype(BF16)

    def reduce_more(k):
        send(tb.at[y_at(k)], ub.at[k - 1], D2B + k, dev_y(k))

    farthest_first(reduce_more)
    noted(D2B, tb.at[0])

    ring(latent, 0, 2)
    fetch(lat_ref, lat_hbm)

    arrived(c_up.at[upper_rows], C_UPD)
    arrived(c_dn.at[lower_rows], C_DND)
    arrived(c_up.at[lower_rows], C_UPS)
    arrived(c_dn.at[upper_rows], C_DNS)
    grad = part[3].astype(F32) + c_up[...].astype(F32) + c_dn[...].astype(F32)
    zv[:, 0:256], zv[:, 256:512] = split(grad[:slots])
    prev_grad = grad[slots:slots + 1]

    def byte_grad(at, extra):
        got = dot(hot_t[at], zv[...])
        grad_rows = got[:, 0:256] + got[:, 256:512]
        if extra is not None:
            grad_rows = grad_rows + extra
        high, low = split(grad_rows * diff_s[at])
        inner = dot(high, head_ones) + dot(low, head_ones)
        gb_ref[at] = (share_s[at] * grad_rows + coef_s[at] * inner).astype(BF16)

    byte_grad(pl.ds(0, 256), lead_rows(lead8 * prev_grad, 256))

    def byte_more(i):
        byte_grad(pl.ds(pl.multiple_of(i * 256, 256), 256), None)

    ring(byte_more, 1, rows // 256)
    fetch(gb_ref, gb_hbm)

    def reduced_more(k):
        arrived(ua.at[k - 1], D2A + k)
        arrived(ub.at[k - 1], D2B + k)

    ring(reduced_more)
    landed(D2A)
    landed(D2B)
    sum_a, sum_b = ta[z].astype(F32), tb[y].astype(F32)
    for k in range(RING - 1):
        sum_a = sum_a + ua[k].astype(F32)
        sum_b = sum_b + ub[k].astype(F32)
    grad_scale = 1.0 / math.sqrt(n_seq * slots)
    both = jnp.concatenate([sum_a, sum_b], axis=1) * grad_scale
    fin_s[...] = jnp.where(first, both[8:16], both[0:8])
    send(fin_s, fin_r, F_PAIR, pair)
    mine = jnp.where(first, both[0:8], both[8:16])
    arrived(fin_r, F_PAIR)
    other = fin_r[...]
    gw_ref[:, 0:512] = jnp.where(first, mine, other)
    gw_ref[:, 512:1024] = jnp.where(first, other, mine)
    fetch(gw_ref, gw_hbm)

    drain()


def place(lat_in, gw_in, gb_in, lat_out, gw_out, gb_out, lat, gw, gb, sem_in, sem_out):
    parts = [(lat_in, lat, lat_out, 64 * i, 64) for i in range(lat.shape[0] // 64)]
    parts += [(gb_in, gb, gb_out, 256 * i, 256) for i in range(gb.shape[0] // 256)]
    parts.append((gw_in, gw, gw_out, 0, 8))
    reads, writes = [], []
    for i, (src, mid, dst, start, size) in enumerate(parts):
        at = pl.ds(start, size)
        reads.append(pltpu.make_async_copy(src.at[at], mid.at[at], sem_in.at[i]))
        writes.append(pltpu.make_async_copy(mid.at[at], dst.at[at], sem_out.at[i]))
    for copy in reads:
        copy.start()
    for read, write in zip(reads, writes):
        read.wait()
        write.start()
    for copy in writes:
        copy.wait()


def shards(byte_hidden, patch_start, pool_query, in_weight, latent_grad):
    rows, feats = byte_hidden.shape
    slots, width = latent_grad.shape
    half = slots // 2
    hbm = pl.BlockSpec(memory_space=pltpu.HBM)

    def buf(*shape, dtype=BF16):
        return pltpu.VMEM(shape, dtype)

    scratch = [
        buf(slots, width), buf(8, width, dtype=F32), buf(rows, feats),
        buf(rows + 128, feats), buf(rows // 128, 128, dtype=jnp.int32), buf(2, 128),
        buf(8, 128, dtype=F32), buf(8, 128, dtype=F32), buf(8, 128, dtype=F32),
        buf(8, width), buf(8, width, dtype=F32), buf(8, width, dtype=F32),
        buf(2, 2, RING, RING, 16, 256), buf(4, 1024, 256),
        buf(slots + 16, width), buf(16, width), buf(2, slots, 512),
        buf(slots + 16, rows + 128), buf(rows, slots),
        buf(rows + 128, 1024), buf(rows + 128, feats, dtype=F32), buf(rows + 128, feats, dtype=F32),
        buf(slots, 1024),
        buf(rows, feats, dtype=F32), buf(rows, feats, dtype=F32), buf(rows, feats, dtype=F32),
        buf(2, 4, 2, half, 256), buf(4, slots + 16, 256),
        buf(half, 256), buf(half + 16, 256), buf(half, 256), buf(half + 16, 256),
        buf(slots + 16, 256), buf(slots + 16, 256), buf(slots, 512),
        buf(RING, RING, 16, 256), buf(RING, RING, 16, 256),
        buf(RING - 1, RING, 16, 256), buf(4, RING, 16, 256),
        buf(RING, 16, 256), buf(RING // 2, 16, 256), buf(RING, 16, 256), buf(RING // 2, 16, 256),
        buf(RING, 16, 256), buf(RING, 16, 256),
        buf(RING, 16, 256), buf(RING, 16, 256),
        buf(RING - 1, 16, 256), buf(RING - 1, 16, 256),
        buf(8, 512, dtype=F32), buf(8, 512, dtype=F32),
        pltpu.SemaphoreType.DMA((9,)),
        pltpu.SemaphoreType.DMA((SLOTS_SEM,)),
        pltpu.SemaphoreType.DMA((SLOTS_SEM,)),
    ]
    shapes = (
        jax.ShapeDtypeStruct((slots, width), BF16),
        jax.ShapeDtypeStruct((8, width), F32),
        jax.ShapeDtypeStruct((rows, feats), BF16),
    )
    outs = pl.pallas_call(
        kernel,
        out_shape=shapes,
        in_specs=[hbm] * 5,
        out_specs=(hbm, hbm, hbm),
        scratch_shapes=scratch,
        compiler_params=pltpu.CompilerParams(
            collective_id=0, has_side_effects=True, vmem_limit_bytes=VMEM_LIMIT
        ),
        name="patch_pool",
    )(
        byte_hidden, patch_start.reshape(rows // 128, 128), pool_query.reshape(2, feats // 2),
        in_weight, latent_grad,
    )
    return pl.pallas_call(
        place,
        out_shape=shapes,
        in_specs=[hbm] * 3,
        out_specs=(hbm, hbm, hbm),
        scratch_shapes=[
            buf(slots, width), buf(8, width, dtype=F32), buf(rows, feats),
            pltpu.SemaphoreType.DMA((13,)), pltpu.SemaphoreType.DMA((13,)),
        ],
        compiler_params=pltpu.CompilerParams(vmem_limit_bytes=VMEM_LIMIT),
        name="place",
    )(*outs)


def solution(mesh):
    in_specs = (P("seq", "mp"), P("seq"), P("mp"), P("seq", "mp"), P("seq", "mp"))
    out_specs = (P("seq", "mp"), P("seq", "mp"), P("seq", "mp"))
    return jax.shard_map(shards, mesh=mesh, in_specs=in_specs, out_specs=out_specs, check_vma=False)
```
